128 devices in a mesh: dap: 32 (over y_lo, x, z), grp: 4 (over y_hi, core).
Axes of the slice: x: 4, y: 4 (y_hi: 2, y_lo: 2; y = y_hi * 2 + y_lo), z: 4, core: 2. Of those that a mesh axis runs over, the one named last changes fastest.
Arguments:
- homolog_stack: float32 [128, 512, 256], P('dap'), may hold values from -6 to 6
- couple_score_offset: float32 [8, 512, 512], P('grp', 'dap'), may hold values from -250 to 250
- strand_identity: int32 [512], replicated, may hold values from 0 to 3, never falling along the last dimension, each value on 1 to 256 neighbouring positions
- strand_score_offset: float32 [8], P('grp'), may hold values from -2 to 2
- homolog_presence: int32 [128], replicated, may hold values from 0 to 1, as said below
- horizontal_matrix: float32 [4, 256, 256], P(None, None, 'grp'), may hold values from -0.375 to 0.375
- horizontal_final_matrix: float32 [256, 256], P('grp'), may hold values from -0.375 to 0.375
- vertical_matrix: float32 [4, 256, 256], replicated, may hold values from -4 to 4
- vertical_final_matrix: float32 [256, 256], replicated, may hold values from -0.375 to 0.375
- expand_matrix: float32 [256, 1024], replicated, may hold values from -0.375 to 0.375
- shrink_matrix: float32 [1024, 256], replicated, may hold values from -0.1875 to 0.1875
- tensor_matrix: float32 [2, 256, 32], replicated, may hold values from -0.375 to 0.375
- couple_matrix: float32 [1024, 128], replicated, may hold values from -1 to 1
Outputs:
- revised_homolog_stack: float32 [128, 512, 256], P(None, ('dap', 'grp'))
- pair_outer_update: float32 [512, 512, 128], P('dap', 'grp')
The draws below stay inside these ranges and needn't reach their ends.
Inputs may be any that keep to these rules, and one draw needn't show every extreme that they name: `homolog_presence`: row 0 is always live.
All inputs are finite; a program needn't handle non-finite values.
Results may differ from the reference program's by a relative error of at most 0.0003.
Values sent between devices are 32-bit elements; how exact they have to be, the bound alone decides.
A program may use at most 192 MiB of HBM per device.

```python
import math
import jax
import jax.numpy as jnp
import numpy as np
from jax import lax

LINEUP_BREADTH = 256
FOCUS_GROUPS = 8
GROUP_BREADTH = 32
TENSOR_BREADTH = 32
PAIR_DIM = 128
INNER_BREADTH = 1024
SHARD_AMINOS = 16
HOMOLOG_TOTAL = 128
ASSEMBLY_AMINOS = 512
N_DAP = 32


def draw_couple_score_offset(key, part):
    key = jax.random.fold_in(key, 11)
    tensor_extent = (FOCUS_GROUPS, ASSEMBLY_AMINOS, ASSEMBLY_AMINOS)
    return jax.random.truncated_normal(jax.random.fold_in(key, 1), -6.0, 6.0, tensor_extent, jnp.float32)


def draw_homolog_presence(key, part):
    key = jax.random.fold_in(key, 12)
    value_rows = (jax.random.randint(key, (HOMOLOG_TOTAL,), 0, 4) > 0).astype(jnp.int32)
    return value_rows.at[0].set(1)


def draw_vertical_matrix(key, part):
    key = jax.random.fold_in(key, 13)
    tensor_extent = (4, LINEUP_BREADTH, FOCUS_GROUPS * GROUP_BREADTH)
    starting_point = jax.random.truncated_normal(jax.random.fold_in(key, 1), -6.0, 6.0, tensor_extent, jnp.float32) / jnp.sqrt(jnp.float32(LINEUP_BREADTH))
    return starting_point


def level_of(own_key, shape, cuts, low, high):
    def one(position, parts):
        draws = jax.random.uniform(jax.random.fold_in(jax.random.fold_in(own_key, 6), position), (parts,), jnp.float32, low / len(cuts), high / len(cuts))
        return jnp.repeat(jnp.exp(draws), shape[position] // parts).reshape((-1,) + (1,) * (len(shape) - position - 1))

    loudness = one(*cuts[0])
    for cut in cuts[1:]:
        loudness = loudness * one(*cut)
    return loudness


def split_up(number_of, total, limit, lean):
    portions = [(1 << 20) // math.isqrt(grade ** lean) + 1 for grade in range(2, number_of + 1)]
    rest, holding = total - limit - (number_of - 1), [1] * (number_of - 1)
    while rest > 0:
        free = [i for i in range(number_of - 1) if holding[i] < limit]
        mass, remaining = sum([portions[i] for i in free]), rest
        for i in free:
            extra = min(limit - holding[i], max(1, remaining * portions[i] // mass), rest)
            holding[i] = holding[i] + extra
            rest = rest - extra
    return np.array([limit] + holding)


def uneven(own_key, number_of, total, limit, lean):
    if number_of == 2:
        one = jax.random.randint(own_key, (), max(1, total - limit), min(limit, total - 1) + 1)
        return jnp.stack([one, total - one])
    tallies = jnp.asarray(split_up(number_of, total, limit, lean), jnp.int32)
    pairs = (number_of - 1) // 2
    donor, receiver = tallies[1:1 + 2 * pairs:2], tallies[2:2 + 2 * pairs:2]
    margin = jnp.minimum(donor - 1, limit - receiver)
    shifted = jax.random.randint(jax.random.fold_in(own_key, 1), (pairs,), 0, 1 << 20) % (margin + 1)
    tallies = tallies.at[1:1 + 2 * pairs:2].set(donor - shifted).at[2:2 + 2 * pairs:2].set(receiver + shifted)
    return tallies[jax.random.permutation(jax.random.fold_in(own_key, 2), number_of)]


def scatter_about(own_key, shape, scale, limit, split=(), dtype=jnp.bfloat16):
    result = scale * jax.random.normal(own_key, shape, jnp.float32)
    if split:
        result = result * level_of(own_key, shape, split, -0.22, 0.18)
    return jnp.clip(result, -limit, limit).astype(dtype)


def setup_inputs(seed: int = 0) -> dict:
    splits = jax.random.split(jax.random.key(seed), 14)
    homolog_stack = scatter_about(splits[0], (HOMOLOG_TOTAL, ASSEMBLY_AMINOS, LINEUP_BREADTH), 1.0, 6.0, ((0, 32),), jnp.float32)
    couple_score_offset = draw_couple_score_offset(jax.random.fold_in(splits[13], 71), 0)
    strand_identity = jnp.searchsorted(jnp.cumsum(uneven(splits[2], 4, ASSEMBLY_AMINOS, ASSEMBLY_AMINOS // 2, 0)), jnp.arange(ASSEMBLY_AMINOS), side="right").astype(jnp.int32)
    strand_score_offset = jnp.clip(jax.random.uniform(splits[3], (FOCUS_GROUPS,), jnp.float32, -2.0, 2.0) * level_of(splits[3], (FOCUS_GROUPS,), ((0, 4),), -0.4, 0.0), -2.0, 2.0)
    homolog_presence = draw_homolog_presence(jax.random.fold_in(splits[13], 71), 0)
    horizontal_matrix = scatter_about(splits[5], (4, LINEUP_BREADTH, FOCUS_GROUPS * GROUP_BREADTH), LINEUP_BREADTH ** -0.5, 0.375, ((2, 4),), jnp.float32)
    horizontal_final_matrix = scatter_about(splits[6], (FOCUS_GROUPS * GROUP_BREADTH, LINEUP_BREADTH), (FOCUS_GROUPS * GROUP_BREADTH) ** -0.5, 0.375, ((0, 4),), jnp.float32)
    vertical_matrix = draw_vertical_matrix(jax.random.fold_in(splits[13], 71), 0)
    vertical_final_matrix = scatter_about(splits[8], (FOCUS_GROUPS * GROUP_BREADTH, LINEUP_BREADTH), (FOCUS_GROUPS * GROUP_BREADTH) ** -0.5, 0.375, (), jnp.float32)
    expand_matrix = scatter_about(splits[9], (LINEUP_BREADTH, INNER_BREADTH), LINEUP_BREADTH ** -0.5, 0.375, (), jnp.float32)
    shrink_matrix = scatter_about(splits[10], (INNER_BREADTH, LINEUP_BREADTH), INNER_BREADTH ** -0.5, 0.1875, (), jnp.float32)
    tensor_matrix = scatter_about(splits[11], (2, LINEUP_BREADTH, TENSOR_BREADTH), LINEUP_BREADTH ** -0.5, 0.375, (), jnp.float32)
    couple_matrix = scatter_about(splits[12], (TENSOR_BREADTH * TENSOR_BREADTH, PAIR_DIM), TENSOR_BREADTH ** -0.5, 1.0, (), jnp.float32)
    return {"homolog_stack": homolog_stack, "couple_score_offset": couple_score_offset, "strand_identity": strand_identity, "strand_score_offset": strand_score_offset, "homolog_presence": homolog_presence, "horizontal_matrix": horizontal_matrix, "horizontal_final_matrix": horizontal_final_matrix, "vertical_matrix": vertical_matrix, "vertical_final_matrix": vertical_final_matrix, "expand_matrix": expand_matrix, "shrink_matrix": shrink_matrix, "tensor_matrix": tensor_matrix, "couple_matrix": couple_matrix}


HIGH_PRECISION = lax.Precision.HIGHEST

def standardize_entries(value_rows):
    center = value_rows - lax.optimization_barrier(jnp.mean(value_rows, axis=-1, keepdims=True))
    spread = lax.optimization_barrier(jnp.mean(center * center, axis=-1, keepdims=True))
    return center * lax.rsqrt(spread + 1e-05)

def column_section(current_block, mask_bias, live_rows, vertical_matrix, vertical_final_matrix, expand_matrix, shrink_matrix, tensor_matrix):
    rows, count, embedding_breadth = current_block.shape
    standardized_source = standardize_entries(current_block)
    projected = jnp.einsum('snc,kce->ksne', standardized_source, vertical_matrix, precision=HIGH_PRECISION)
    projected = projected.reshape(4, rows, count, FOCUS_GROUPS, GROUP_BREADTH)
    logits = jnp.einsum('snhd,tnhd->nhst', projected[0], projected[1], precision=HIGH_PRECISION) / jnp.sqrt(jnp.float32(GROUP_BREADTH))
    logits = logits + mask_bias[None, None, None, :]
    weights = jax.nn.softmax(logits, axis=-1)
    attended_rows = jnp.einsum('nhst,tnhd->snhd', weights, projected[2], precision=HIGH_PRECISION)
    attended_rows = attended_rows.reshape(rows, count, FOCUS_GROUPS * GROUP_BREADTH) * jax.nn.sigmoid(projected[3].reshape(rows, count, FOCUS_GROUPS * GROUP_BREADTH))
    first_factor = current_block + jnp.einsum('owq,qg->owg', attended_rows, vertical_final_matrix, precision=HIGH_PRECISION)
    hidden_units = jax.nn.relu(jnp.einsum('dgz,zb->dgb', standardize_entries(first_factor), expand_matrix, precision=HIGH_PRECISION))
    right_operand = first_factor + jnp.einsum('owq,qg->owg', hidden_units, shrink_matrix, precision=HIGH_PRECISION)
    outer_in = jnp.einsum('snc,kce->ksne', standardize_entries(right_operand), tensor_matrix, precision=HIGH_PRECISION)
    outer_in = outer_in * live_rows[None, :, None, None]
    return (right_operand, jnp.concatenate([outer_in[0], outer_in[1]], axis=-1))

def outer_project(left_factor, right, couple_matrix):
    outer = jnp.einsum('sic,sje->ijce', left_factor, right, precision=HIGH_PRECISION)
    count_left, count_right = (outer.shape[0], outer.shape[1])
    flat = outer.reshape(count_left * count_right, TENSOR_BREADTH * TENSOR_BREADTH)
    return jnp.dot(flat, couple_matrix, precision=HIGH_PRECISION).reshape(count_left, count_right, PAIR_DIM)

def reference(homolog_stack, couple_score_offset, strand_identity, strand_score_offset, homolog_presence, horizontal_matrix, horizontal_final_matrix, vertical_matrix, vertical_final_matrix, expand_matrix, shrink_matrix, tensor_matrix, couple_matrix):
    same = (strand_identity[:, None] == strand_identity[None, :]).astype(jnp.float32)
    scale = 1.0 / jnp.sqrt(jnp.float32(GROUP_BREADTH))

    def lone_homolog(row):
        standardized_source = standardize_entries(row)
        projected = jnp.einsum('rc,kce->kre', standardized_source, horizontal_matrix, precision=HIGH_PRECISION).reshape(4, ASSEMBLY_AMINOS, FOCUS_GROUPS, GROUP_BREADTH)
        logits = jnp.einsum('ihd,jhd->hij', projected[0], projected[1], precision=HIGH_PRECISION) * scale
        logits = logits + couple_score_offset + strand_score_offset[:, None, None] * same[None]
        weights = jax.nn.softmax(logits, axis=-1)
        attended_rows = jnp.einsum('hij,jhd->ihd', weights, projected[2], precision=HIGH_PRECISION).reshape(ASSEMBLY_AMINOS, FOCUS_GROUPS * GROUP_BREADTH)
        attended_rows = attended_rows * jax.nn.sigmoid(projected[3].reshape(ASSEMBLY_AMINOS, FOCUS_GROUPS * GROUP_BREADTH))
        return jnp.dot(attended_rows, horizontal_final_matrix, precision=HIGH_PRECISION)
    revised_tensor = homolog_stack + lax.map(lone_homolog, homolog_stack)
    live_rows = homolog_presence.astype(jnp.float32)
    mask_bias = (live_rows - 1.0) * 1000000000.0
    tile_collection = revised_tensor.reshape(HOMOLOG_TOTAL, N_DAP, SHARD_AMINOS, LINEUP_BREADTH).transpose(1, 0, 2, 3)

    def one_block(current_block):
        return column_section(current_block, mask_bias, live_rows, vertical_matrix, vertical_final_matrix, expand_matrix, shrink_matrix, tensor_matrix)
    right_operand, joined_parts = lax.map(one_block, tile_collection)
    revised_homolog_stack = right_operand.transpose(1, 0, 2, 3).reshape(HOMOLOG_TOTAL, ASSEMBLY_AMINOS, LINEUP_BREADTH)
    joined_parts = joined_parts.transpose(1, 0, 2, 3).reshape(HOMOLOG_TOTAL, ASSEMBLY_AMINOS, 2 * TENSOR_BREADTH)
    left_factor = joined_parts[:, :, :TENSOR_BREADTH]
    right = joined_parts[:, :, TENSOR_BREADTH:]
    live = jnp.sum(live_rows)
    left_factor_blocks = left_factor.reshape(HOMOLOG_TOTAL, N_DAP, SHARD_AMINOS, TENSOR_BREADTH).transpose(1, 0, 2, 3)
    pair_blocks = lax.map(lambda piece: outer_project(piece, right, couple_matrix), left_factor_blocks)
    pair_outer_update = pair_blocks.reshape(ASSEMBLY_AMINOS, ASSEMBLY_AMINOS, PAIR_DIM) / live
    return (revised_homolog_stack, pair_outer_update)
```

```python
import functools
import math

import jax
import jax.numpy as jnp
from jax import lax
from jax.experimental import pallas as pl
from jax.experimental.pallas import tpu as pltpu
from jax.sharding import PartitionSpec as P

F32 = jnp.float32
BF16 = jnp.bfloat16
MESH = pl.DeviceIdType.MESH
HEAD = 32
LOG2E = math.log2(math.e)
NN = (((1,), (0,)), ((), ()))
NT = (((1,), (1,)), ((), ()))


def split(a):
    high = a.astype(BF16)
    return high, (a - high.astype(F32)).astype(BF16)


def dot(a, b, dims=NN):
    return lax.dot_general(a, b, dims, preferred_element_type=F32)


def dot3(a, b, dims=NN):
    return dot(a[0], b[0], dims) + (dot(a[0], b[1], dims) + dot(a[1], b[0], dims))


def normed(rows):
    center = rows - jnp.mean(rows, axis=-1, keepdims=True)
    spread = jnp.mean(center * center, axis=-1, keepdims=True)
    return center * lax.rsqrt(spread + 1e-05)


def merge_halves(a, b):
    upper = lax.broadcasted_iota(jnp.int32, a.shape, a.ndim - 2) < 4
    first = jnp.where(upper, a, pltpu.roll(b, 4, axis=b.ndim - 2))
    second = jnp.where(upper, pltpu.roll(a, 4, axis=a.ndim - 2), b)
    return first, second


def lane_iota(shape):
    return lax.broadcasted_iota(jnp.int32, shape, len(shape) - 1)


def drain(ref, sem):
    pltpu.make_async_copy(ref, ref, sem).wait()


def row_kernel(
    x_ref, bias_ref, ids_ref, offset_ref, weight_ref, final_ref,
    xr_ref, or_ref, finals_ref,
    bias_all, xs, xr, os, orr, finals, wide_h, wide_l, qs, ks, vs, gates, chunk_bias,
    bias_send, bias_recv, x_send, x_recv, o_send, o_recv, final_send, final_recv,
):
    dap = lax.axis_index("dap")
    grp = lax.axis_index("grp")

    own = pl.ds(pl.multiple_of(dap * 16, 16), 16)
    pltpu.make_async_copy(bias_ref, bias_all.at[:, own, :], bias_recv.at[dap // 8]).start()

    def send_bias(k, carry):
        to = lax.rem(dap + k, 32)
        pltpu.make_async_remote_copy(
            src_ref=bias_ref, dst_ref=bias_all.at[:, own, :],
            send_sem=bias_send, recv_sem=bias_recv.at[dap // 8],
            device_id=(to, grp), device_id_type=MESH,
        ).start()
        return carry

    lax.fori_loop(1, 32, send_bias, 0)

    half = lax.rem(grp, 2)
    for s2 in range(2):
        a = x_ref[2 * s2, :, grp // 2]
        b = x_ref[2 * s2 + 1, :, grp // 2]
        first, second = merge_halves(a, b)
        xs[:, s2] = jnp.where(half == 0, first, second)
    pltpu.make_async_copy(xs.at[dap], xr.at[:, dap], x_recv).start()

    def send_x(k, carry):
        to = lax.rem(dap + k, 32)
        pltpu.make_async_remote_copy(
            src_ref=xs.at[to], dst_ref=xr.at[:, dap],
            send_sem=x_send, recv_sem=x_recv,
            device_id=(to, grp), device_id_type=MESH,
        ).start()
        return carry

    lax.fori_loop(1, 32, send_x, 0)

    final_to = finals.at[pl.ds(pl.multiple_of(grp * 64, 64), 64)]
    pltpu.make_async_copy(final_ref, final_to, final_recv).start()
    for k in range(1, 4):
        pltpu.make_async_remote_copy(
            src_ref=final_ref, dst_ref=final_to, send_sem=final_send, recv_sem=final_recv,
            device_id=(dap, lax.rem(grp + k, 4)), device_id_type=MESH,
        ).start()

    zero = jnp.zeros((256, 64), F32)
    q_w = weight_ref[0] * (LOG2E / math.sqrt(HEAD))
    k_w, v_w, g_w = weight_ref[1], weight_ref[2], weight_ref[3]
    wide = jnp.concatenate([q_w, q_w, q_w, zero, k_w, k_w, k_w, zero, v_w, v_w, g_w, g_w], axis=-1)
    high, low = split(wide)
    wide_h[...] = high
    wide_l[...] = low

    def project(s, carry):
        rows = split(normed(x_ref[s].reshape(512, 256)))
        out = dot3(rows, (wide_h[...], wide_l[...]))
        lane = lane_iota((512, 256))
        head = lax.rem(lane, 64) // HEAD
        q_hi, q_lo = split(out[:, 0:256])
        q = jnp.where((lane >= 64) & (lane < 128), q_lo.astype(F32), q_hi.astype(F32))
        k_hi, k_lo = split(out[:, 256:512])
        k = jnp.where((lane >= 128) & (lane < 192), k_lo.astype(F32), k_hi.astype(F32))
        ks[s] = k.astype(BF16)
        lane_v = lane_iota((512, 128))
        head_v = lax.rem(lane_v, 64) // HEAD
        v_hi, v_lo = split(out[:, 512:640])
        v = jnp.where(lane_v >= 64, v_lo.astype(F32), v_hi.astype(F32))
        for h in range(2):
            qs[s, h] = jnp.where(head == h, q, 0.0).astype(BF16)
            vs[s, pl.ds(512 * h, 512), 0:128] = jnp.where(head_v == h, v, 0.0).astype(BF16)
            vs[s, pl.ds(512 * h, 512), 128:256] = jnp.where(head_v == h, 1.0, 0.0).astype(BF16)
        gates[s] = jax.nn.sigmoid(out[:, 640:768])
        return carry

    lax.fori_loop(0, 4, project, 0)

    def attend(step, carry):
        chunk = lax.rem(step + dap // 8, 4)
        here = pl.ds(pl.multiple_of(chunk * 128, 128), 128)
        bias_here = bias_all.at[:, here, :]
        drain(bias_here, bias_recv.at[chunk])
        ids = ids_ref[...].astype(F32)
        own_ids = jnp.transpose(jnp.broadcast_to(ids_ref[:, here].astype(F32), (128, 128)))
        same = (jnp.concatenate([own_ids] * 4, axis=-1) == ids).astype(F32)
        for h in range(2):
            chunk_bias[h] = (bias_here[h] + offset_ref[h] * same) * LOG2E
        outs = []
        for s in range(4):
            highs, lows = [], []
            for h in range(2):
                logits = dot(qs[s, h, here, :], ks[s], NT) + chunk_bias[h]
                weights = jnp.exp2(logits - jnp.max(logits, axis=-1, keepdims=True))
                high, low = split(weights)
                highs.append(high)
                lows.append(low)
            v = vs[s]
            total = dot(jnp.concatenate(highs, axis=-1), v) + dot(jnp.concatenate(lows, axis=-1), v)
            top = total[:, 0:128]
            top = top + pltpu.roll(top, 64, axis=1)
            outs.append(top / total[:, 128:256] * gates[s, here, :])
        left_lanes = lane_iota((128, 128)) < 64
        pair = [jnp.where(left_lanes, outs[s1], outs[2 + s1]).reshape(16, 8, 128) for s1 in range(2)]
        first, second = merge_halves(*pair)
        tiles = pl.ds(chunk * 16, 16)
        os[tiles, 0] = first
        os[tiles, 1] = second

        def send_o(k, carry):
            block = lax.rem(k + dap * 4 + grp, 32) + chunk * 32
            to_dap, to_grp = block // 4, lax.rem(block, 4)
            mine = (to_dap == dap) & (to_grp == grp)
            src = os.at[block // 2, lax.rem(block, 2)]
            dst = orr.at[grp * 32 + dap]

            @pl.when(mine)
            def _():
                pltpu.make_async_copy(src, dst, o_recv).start()

            @pl.when(jnp.logical_not(mine))
            def _():
                pltpu.make_async_remote_copy(
                    src_ref=src, dst_ref=dst, send_sem=o_send, recv_sem=o_recv,
                    device_id=(to_dap, to_grp), device_id_type=MESH,
                ).start()

            return carry

        lax.fori_loop(0, 32, send_o, 0)
        return carry

    lax.fori_loop(0, 4, attend, 0)

    drain(bias_all.at[:, 0:496, :], bias_send)
    drain(xs.at[0:31], x_send)
    drain(orr.at[0:127], o_send)
    drain(xr, x_recv)
    drain(orr, o_recv)
    drain(finals.at[0:192], final_send)
    drain(finals, final_recv)
    xr_ref[...] = xr[...]
    or_ref[...] = orr[...]
    finals_ref[...] = finals[...]


def column_kernel(
    xr_ref, or_ref, row_final_ref, live_ref, vertical_ref, final_ref, expand_ref, shrink_ref, tensor_ref,
    revised_ref, left_ref, right_ref,
    msa, proj, attended, units,
):
    zero = jnp.zeros((64, 256), F32)
    parts = split(jnp.concatenate([or_ref[pl.ds(32 * g, 32)].reshape(256, 128) for g in range(4)], axis=-1))
    for s2 in range(2):
        pieces = []
        for g in range(4):
            own = row_final_ref[64 * g:64 * g + 64, :]
            pieces += [own, zero] if s2 == 0 else [zero, own]
        out = dot3(parts, split(jnp.concatenate(pieces, axis=0)))
        msa[pl.ds(256 * s2, 256), :] = xr_ref[s2].reshape(256, 256) + out

    rows = split(normed(msa[...]))
    for m in range(4):
        w = vertical_ref[m]
        if m == 0:
            w = w * (LOG2E / math.sqrt(HEAD))
        out = dot3(rows, split(w))
        for part in range(2):
            proj[2 * m + part] = out[:, 128 * part:128 * part + 128]

    at = lax.broadcasted_iota(jnp.int32, (128, 128), 0)
    to = lax.broadcasted_iota(jnp.int32, (128, 128), 1)
    order = (at == 4 * lax.rem(to // 2, 32) + 2 * (to // 64) + lax.rem(to, 2)).astype(BF16)
    live = dot(live_ref[...].astype(F32).astype(BF16), order)
    live_total = jnp.sum(live)
    mask = (live - 1.0) * (1e9 * LOG2E)

    lane = lane_iota((128, 128))
    for r in range(4):
        for part in range(2):
            q, k, v, g = (proj[2 * m + part, pl.ds(r, 128, stride=4), :] for m in range(4))
            q_h, q_l = split(q)
            k_h, k_l = split(k)
            v_h, v_l = split(v)
            keys = jnp.concatenate([k_h, k_h, k_l], axis=-1)
            wide_q, wide_v = [], []
            for h in range(4):
                mine = lane // HEAD == h
                none = jnp.zeros((128, 128), BF16)
                qm_h, qm_l = jnp.where(mine, q_h, none), jnp.where(mine, q_l, none)
                wide_q.append(jnp.concatenate([qm_h, qm_l, qm_h], axis=-1))
                wide_v.append(jnp.concatenate(
                    [jnp.where(mine, v_h, none), jnp.where(mine, v_l, none), mine.astype(BF16)], axis=-1))
            logits = dot(jnp.concatenate(wide_q, axis=0), keys, NT) + mask
            weights = jnp.exp2(logits - jnp.max(logits, axis=-1, keepdims=True))
            high, low = split(weights)
            values = jnp.concatenate(wide_v, axis=0)

            def heads_in_lanes(a):
                return jnp.concatenate([a[128 * h:128 * h + 128] for h in range(4)], axis=-1)

            total = dot(heads_in_lanes(high), values) + dot(heads_in_lanes(low), values)
            out = (total[:, 0:128] + total[:, 128:256]) / total[:, 256:384]
            attended[part, pl.ds(r, 128, stride=4), :] = out * jax.nn.sigmoid(g)

    current = msa[...] + dot3(split(jnp.concatenate([attended[0], attended[1]], axis=-1)), split(final_ref[...]))
    hidden = jnp.maximum(dot3(split(normed(current)), split(expand_ref[...])), 0.0)
    revised = current + dot3(split(hidden), split(shrink_ref[...]))
    for s2 in range(2):
        revised_ref[:, s2] = revised[256 * s2:256 * s2 + 256].reshape(32, 8, 256)

    unit = normed(revised)
    for part in range(2):
        units[part] = unit[:, 128 * part:128 * part + 128]
    narrow = jnp.concatenate([tensor_ref[0], tensor_ref[1], jnp.zeros((256, 64), F32)], axis=-1)
    narrow = split(jnp.transpose(narrow)[0:64])
    for r in range(4):
        both = dot3(narrow, split(jnp.concatenate([units[part, pl.ds(r, 128, stride=4), :] for part in range(2)], axis=-1)), NT)
        left_ref[pl.ds(32 * r, 32), :] = both[0:32] * (live / live_total)
        right_ref[pl.ds(r, 32, stride=4), :] = both[32:64] * live


def pair_kernel(
    left_ref, right_ref, couple_ref, out_ref,
    left_all, right_all, right_sorted, outer_h, outer_l, couple_h, couple_l,
    left_send, left_recv, right_send, right_recv,
):
    dap = lax.axis_index("dap")
    grp = lax.axis_index("grp")

    left_to = left_all.at[pl.ds(pl.multiple_of(grp * 128, 128), 128)]
    pltpu.make_async_copy(left_ref, left_to, left_recv).start()
    for k in range(1, 4):
        pltpu.make_async_remote_copy(
            src_ref=left_ref, dst_ref=left_to, send_sem=left_send, recv_sem=left_recv,
            device_id=(dap, lax.rem(grp + k, 4)), device_id_type=MESH,
        ).start()

    to_grp = dap // 8
    slot = lax.rem(dap, 8) * 4 + grp
    right_to = right_all.at[slot]

    def send_right(k, carry):
        to = lax.rem(dap + k, 32)
        mine = (to == dap) & (to_grp == grp)

        @pl.when(mine)
        def _():
            pltpu.make_async_copy(right_ref, right_to, right_recv).start()

        @pl.when(jnp.logical_not(mine))
        def _():
            pltpu.make_async_remote_copy(
                src_ref=right_ref, dst_ref=right_to, send_sem=right_send, recv_sem=right_recv,
                device_id=(to, to_grp), device_id_type=MESH,
            ).start()

        return carry

    lax.fori_loop(0, 32, send_right, 0)

    for e in range(8):
        rows = jnp.concatenate([couple_ref[pl.ds(4 * e + i, 32, stride=32), :] for i in range(4)], axis=0)
        high, low = split(jnp.transpose(rows))
        couple_h[:, 128 * e:128 * e + 128] = high
        couple_l[:, 128 * e:128 * e + 128] = low

    drain(left_all, left_recv)
    drain(right_all, right_recv)
    left_h, left_l = split(left_all[...])
    left_wide = jnp.concatenate([left_h, left_l, left_h], axis=-1)

    def sort(e2, carry):
        for t in range(16):
            first, second = merge_halves(
                right_all[2 * t, pl.ds(e2 * 8, 8), :], right_all[2 * t + 1, pl.ds(e2 * 8, 8), :])
            right_sorted[2 * e2, pl.ds(8 * t, 8), :] = first
            right_sorted[2 * e2 + 1, pl.ds(8 * t, 8), :] = second
        return carry

    lax.fori_loop(0, 16, sort, 0)

    def outer(e2, carry):
        high, low = split(right_sorted[pl.ds(2 * e2, 2)].reshape(256, 128))
        right_wide = jnp.concatenate([high, high, low], axis=-1)
        product = dot(left_wide, right_wide, NT)
        high, low = split(product)
        for i in range(16):
            for e1 in range(2):
                at = pl.ds(pl.multiple_of(64 * e2 + 32 * e1, 32), 32)
                lanes = slice(128 * (i % 2), 128 * (i % 2) + 128)
                rows, cols = slice(32 * i, 32 * i + 32), slice(128 * e1, 128 * e1 + 128)
                outer_h[i // 2, at, lanes] = high[rows, cols]
                outer_l[i // 2, at, lanes] = low[rows, cols]
        return carry

    lax.fori_loop(0, 16, outer, 0)

    def finish(i2, carry):
        out = dot3((couple_h[...], couple_l[...]), (outer_h[i2], outer_l[i2]))
        for i1 in range(2):
            out_ref[2 * i2 + i1] = jnp.transpose(out[:, 128 * i1:128 * i1 + 128])
        return carry

    lax.fori_loop(0, 8, finish, 0)
    drain(left_all.at[0:384], left_send)
    own = to_grp == grp

    @pl.when(own)
    def _():
        drain(right_all.at[0:31], right_send)

    @pl.when(jnp.logical_not(own))
    def _():
        drain(right_all, right_send)


VM = pl.BlockSpec(memory_space=pltpu.VMEM)
SM = pl.BlockSpec(memory_space=pltpu.SMEM)
LIMIT = 56 * 1024 * 1024


def body(
    homolog_stack,
    couple_score_offset,
    strand_identity,
    strand_score_offset,
    homolog_presence,
    horizontal_matrix,
    horizontal_final_matrix,
    vertical_matrix,
    vertical_final_matrix,
    expand_matrix,
    shrink_matrix,
    tensor_matrix,
    couple_matrix,
):
    shape = jax.ShapeDtypeStruct
    dma = pltpu.SemaphoreType.DMA
    moved_x, moved_o, finals = pl.pallas_call(
        row_kernel,
        out_shape=[shape((2, 32, 8, 256), F32), shape((128, 8, 128), F32), shape((256, 256), F32)],
        in_specs=[VM, VM, VM, SM, VM, VM],
        out_specs=[VM] * 3,
        scratch_shapes=[
            pltpu.VMEM((2, 512, 512), F32),
            pltpu.VMEM((32, 2, 8, 256), F32),
            pltpu.VMEM((2, 32, 8, 256), F32),
            pltpu.VMEM((64, 2, 8, 128), F32),
            pltpu.VMEM((128, 8, 128), F32),
            pltpu.VMEM((256, 256), F32),
            pltpu.VMEM((256, 768), BF16),
            pltpu.VMEM((256, 768), BF16),
            pltpu.VMEM((4, 2, 512, 256), BF16),
            pltpu.VMEM((4, 512, 256), BF16),
            pltpu.VMEM((4, 1024, 256), BF16),
            pltpu.VMEM((4, 512, 128), F32),
            pltpu.VMEM((2, 128, 512), F32),
            dma, dma((4,)), dma, dma, dma, dma, dma, dma,
        ],
        compiler_params=pltpu.CompilerParams(has_side_effects=True, vmem_limit_bytes=LIMIT),
        name="row_attention",
    )(
        homolog_stack.reshape(4, 32, 2, 8, 256),
        couple_score_offset,
        strand_identity.reshape(1, 512),
        strand_score_offset,
        horizontal_matrix,
        horizontal_final_matrix,
    )
    revised, left, right = pl.pallas_call(
        column_kernel,
        out_shape=[shape((32, 2, 8, 256), F32), shape((128, 128), F32), shape((128, 128), F32)],
        in_specs=[VM] * 9,
        out_specs=[VM] * 3,
        scratch_shapes=[
            pltpu.VMEM((512, 256), F32),
            pltpu.VMEM((8, 512, 128), F32),
            pltpu.VMEM((2, 512, 128), F32),
            pltpu.VMEM((2, 512, 128), F32),
        ],
        compiler_params=pltpu.CompilerParams(vmem_limit_bytes=LIMIT),
        name="column_section",
    )(
        moved_x, moved_o, finals, homolog_presence.reshape(1, 128), vertical_matrix, vertical_final_matrix,
        expand_matrix, shrink_matrix, tensor_matrix,
    )
    pair = pl.pallas_call(
        pair_kernel,
        out_shape=shape((16, 128, 128), F32),
        in_specs=[VM] * 3,
        out_specs=VM,
        scratch_shapes=[
            pltpu.VMEM((512, 128), F32),
            pltpu.VMEM((32, 128, 128), F32),
            pltpu.VMEM((32, 128, 128), F32),
            pltpu.VMEM((8, 1024, 256), BF16),
            pltpu.VMEM((8, 1024, 256), BF16),
            pltpu.VMEM((128, 1024), BF16),
            pltpu.VMEM((128, 1024), BF16),
            dma, dma, dma, dma,
        ],
        compiler_params=pltpu.CompilerParams(has_side_effects=True, vmem_limit_bytes=LIMIT),
        name="pair_update",
    )(left, right, couple_matrix)
    return revised.reshape(128, 4, 256), pair


def solution(mesh):
    return jax.shard_map(
        body,
        mesh=mesh,
        in_specs=(
            P("dap", None, None),
            P("grp", "dap", None),
            P(),
            P("grp"),
            P(),
            P(None, None, "grp"),
            P("grp", None),
            P(),
            P(),
            P(),
            P(),
            P(),
            P(),
        ),
        out_specs=(P(None, ("dap", "grp"), None), P("dap", "grp", None)),
        check_vma=False,
    )
```

```python
import functools
import math

import jax
import jax.numpy as jnp
from jax import lax
from jax.experimental import pallas as pl
from jax.experimental.pallas import tpu as pltpu
from jax.sharding import PartitionSpec as P

F32 = jnp.float32
BF16 = jnp.bfloat16
MESH = pl.DeviceIdType.MESH
HEAD = 32
LOG2E = math.log2(math.e)
NN = (((1,), (0,)), ((), ()))
NT = (((1,), (1,)), ((), ()))


def split(a):
    high = a.astype(BF16)
    return high, (a - high.astype(F32)).astype(BF16)


def dot(a, b, dims=NN):
    return lax.dot_general(a, b, dims, preferred_element_type=F32)


def dot3(a, b, dims=NN):
    return dot(a[0], b[0], dims) + (dot(a[0], b[1], dims) + dot(a[1], b[0], dims))


def normed(rows):
    center = rows - jnp.mean(rows, axis=-1, keepdims=True)
    spread = jnp.mean(center * center, axis=-1, keepdims=True)
    return center * lax.rsqrt(spread + 1e-05)


def merge_halves(a, b):
    upper = lax.broadcasted_iota(jnp.int32, a.shape, a.ndim - 2) < 4
    first = jnp.where(upper, a, pltpu.roll(b, 4, axis=b.ndim - 2))
    second = jnp.where(upper, pltpu.roll(a, 4, axis=a.ndim - 2), b)
    return first, second


def lane_iota(shape):
    return lax.broadcasted_iota(jnp.int32, shape, len(shape) - 1)


def drain(ref, sem):
    pltpu.make_async_copy(ref, ref, sem).wait()


def signal(sem, device):
    pl.semaphore_signal(sem, inc=1, device_id=device, device_id_type=MESH)


def send(src, dst, send_sem, recv_sem, device):
    pltpu.make_async_remote_copy(
        src_ref=src, dst_ref=dst, send_sem=send_sem, recv_sem=recv_sem,
        device_id=device, device_id_type=MESH,
    ).start()


def kernel(
    x_ref, bias_ref, ids_ref, offset_ref, weight_ref, final_in_ref, live_ref, vertical_ref, final_ref,
    expand_ref, shrink_ref, tensor_ref, couple_ref,
    revised_ref, out_ref,
    bias_all, xs, xr, os, orr, finals, wide_h, wide_l, qs, ks, vs, gates, ids_col, chunk_bias,
    msa, proj, attended, units,
    left_own, right_own, left_all, right_all, right_sorted, outer_h, outer_l, couple_h, couple_l,
    bias_send, bias_recv, x_send, x_recv, o_send, o_recv, final_send, final_recv,
    left_send, left_recv, right_send, right_recv, near_z, near_x, near_y,
):
    dap = lax.axis_index("dap")
    grp = lax.axis_index("grp")
    y, x, z = dap // 16, lax.rem(dap // 4, 4), lax.rem(dap, 4)
    x_at = [lax.rem(x + i, 4) for i in range(4)]
    z_at = [lax.rem(z + i, 4) for i in range(4)]

    def along_x(i):
        return y * 16 + x_at[i % 4] * 4 + z, grp

    def along_z(i):
        return y * 16 + x * 4 + z_at[i % 4], grp

    across_y = ((1 - y) * 16 + x * 4 + z, grp)

    barrier = pltpu.get_barrier_semaphore()
    for i in range(1, 4):
        signal(barrier, along_x(i))
        signal(barrier, along_z(i))
        signal(barrier, (dap, lax.rem(grp + i, 4)))
    signal(barrier, across_y)

    zero = jnp.zeros((64, 256), F32)
    q_w = weight_ref[0] * (LOG2E / math.sqrt(HEAD))
    k_w, v_w, g_w = weight_ref[1], weight_ref[2], weight_ref[3]
    for at, parts in ((0, (q_w, q_w, q_w, zero)), (256, (k_w, k_w, k_w, zero)), (512, (v_w, v_w, g_w, g_w))):
        high, low = split(jnp.transpose(jnp.concatenate(parts, axis=0)))
        wide_h[:, at:at + 256] = high
        wide_l[:, at:at + 256] = low
    pl.semaphore_wait(barrier, 10)

    def unit(p, i, j, h=None):
        a, b = (x_at[j % 4], z_at[i % 4]) if p == 0 else (x_at[i % 4], z_at[j % 4])
        return bias_all.at[p, a, b] if h is None else bias_all.at[p, a, b, h]

    def line(p, j, h):
        return bias_all.at[0, x_at[j % 4], :, h] if p == 0 else bias_all.at[1, :, z_at[j % 4], h]

    def first_axis(p, i):
        return along_z(i) if p == 0 else along_x(i)

    def second_axis(p, i):
        return along_x(i) if p == 0 else along_z(i)

    steps = ((0, 1), (1, -1))
    own = bias_all.at[y, x, z]
    send(bias_ref, own, bias_send, bias_recv.at[0], across_y)
    pltpu.make_async_copy(bias_ref, own, bias_recv.at[21]).start()
    for i in range(1, 4):
        signal(near_z, along_z(i))
    drain(bias_ref, bias_recv.at[21])

    def spread(p):
        for k, sign in steps:
            send(unit(p, 0, 0), unit(p, 0, 0), bias_send, bias_recv.at[1 + 10 * p + k], first_axis(p, sign))

    for p in range(2):
        @pl.when(y == p)
        def _():
            spread(p)

    def project(s):
        rows = split(normed(x_ref[s].reshape(512, 256)))
        out = dot3(rows, (wide_h[...], wide_l[...]))
        lane = lane_iota((512, 256))
        head = lax.rem(lane, 64) // HEAD
        q_hi, q_lo = split(out[:, 0:256])
        q = jnp.where((lane >= 64) & (lane < 128), q_lo.astype(F32), q_hi.astype(F32))
        k_hi, k_lo = split(out[:, 256:512])
        k = jnp.where((lane >= 128) & (lane < 192), k_lo.astype(F32), k_hi.astype(F32))
        ks[s] = k.astype(BF16)
        lane_v = lane_iota((512, 128))
        head_v = lax.rem(lane_v, 64) // HEAD
        v_hi, v_lo = split(out[:, 512:640])
        v = jnp.where(lane_v >= 64, v_lo.astype(F32), v_hi.astype(F32))
        for h in range(2):
            qs[s, h] = jnp.where(head == h, q, 0.0).astype(BF16).reshape(32, 16, 256)
            vs[s, pl.ds(512 * h, 512), 0:128] = jnp.where(head_v == h, v, 0.0).astype(BF16)
            vs[s, pl.ds(512 * h, 512), 128:256] = jnp.where(head_v == h, 1.0, 0.0).astype(BF16)
        gates[s] = jax.nn.sigmoid(out[:, 640:768]).reshape(32, 16, 128)

    def project_and(s, carry):
        project(s)

        @pl.when(s == 0)
        def _():
            pl.semaphore_wait(near_z, 3)
            for i in range(1, 4):
                signal(near_x, along_x(i))
            drain(bias_ref, bias_recv.at[0])
            for p in range(2):
                @pl.when(y == 1 - p)
                def _():
                    spread(p)

        @pl.when(s == 1)
        def _():
            for p in range(2):
                for k, sign in steps:
                    drain(bias_ref, bias_recv.at[1 + 10 * p + k])
                    send(unit(p, -sign, 0, k), unit(p, -sign, 0, k), bias_send,
                         bias_recv.at[3 + 10 * p + k], first_axis(p, sign))
            pl.semaphore_wait(near_x, 3)
            signal(near_y, across_y)

        @pl.when(s == 2)
        def _():
            for p in range(2):
                for k in range(2):
                    drain(bias_ref.at[0], bias_recv.at[3 + 10 * p + k])
                for k, sign in steps:
                    send(line(p, 0, k), line(p, 0, k), bias_send, bias_recv.at[5 + 10 * p + k], second_axis(p, sign))
                for k, sign in steps:
                    send(line(p, 0, 1 - k), line(p, 0, 1 - k), bias_send,
                         bias_recv.at[7 + 10 * p + k], second_axis(p, sign))

        return carry

    lax.fori_loop(0, 4, project_and, 0)

    half = lax.rem(grp, 2)
    for s2 in range(2):
        first, second = merge_halves(x_ref[2 * s2, :, grp // 2], x_ref[2 * s2 + 1, :, grp // 2])
        xs[:, s2] = jnp.where(half == 0, first, second)
    for i in range(4):
        block = jnp.broadcast_to(ids_ref[:, 128 * i:128 * i + 128].astype(F32), (128, 128))
        ids_col[8 * i:8 * i + 8] = jnp.transpose(block).reshape(8, 16, 128)
    pl.semaphore_wait(near_y, 1)

    def attend(step, carry):
        turn = step + step // 2 - 2 * (step // 3)
        x_now, z_now = lax.rem(x + turn, 4), lax.rem(z + turn, 4)

        @pl.when(step == 1)
        def _():
            for p in range(2):
                for k, sign in steps:
                    drain(line(0, 0, 0), bias_recv.at[5 + 10 * p + k])
                    send(line(p, -sign, k), line(p, -sign, k), bias_send,
                         bias_recv.at[9 + 10 * p + k], second_axis(p, sign))
            pltpu.make_async_copy(xs.at[dap], xr.at[:, dap], x_recv).start()

            def send_x(k, carry):
                to = lax.rem(dap + k, 32)
                send(xs.at[to], xr.at[:, dap], x_send, x_recv, (to, grp))
                return carry

            lax.fori_loop(1, 32, send_x, 0)
            final_to = finals.at[pl.ds(pl.multiple_of(grp * 64, 64), 64)]
            pltpu.make_async_copy(final_in_ref, final_to, final_recv).start()
            for k in range(1, 4):
                send(final_in_ref, final_to, final_send, final_recv, (dap, lax.rem(grp + k, 4)))
            for p in range(2):
                drain(line(0, 0, 0), bias_recv.at[7 + 10 * p + 1])

        @pl.when(step == 2)
        def _():
            for p in range(2):
                drain(line(0, 0, 0), bias_recv.at[7 + 10 * p])

        @pl.when(step == 3)
        def _():
            for p in range(2):
                for k in range(2):
                    drain(line(0, 0, 0), bias_recv.at[9 + 10 * p + k])

        def rows_of(ref, *lead):
            shape = ref.shape[-2:]
            upper = ref[(*lead, pl.ds(4 * x_now, 4))].reshape(64, shape[-1])
            return jnp.concatenate([upper] + [ref[(*lead, 16 + 4 * i + z_now)] for i in range(4)], axis=0)

        own_ids = rows_of(ids_col)
        same = (jnp.concatenate([own_ids] * 4, axis=-1) == ids_ref[...].astype(F32)).astype(F32)
        for h in range(2):
            here = jnp.concatenate(
                [bias_all[0, x_now, :, h].reshape(64, 512), bias_all[1, :, z_now, h].reshape(64, 512)], axis=0)
            chunk_bias[h] = (here + offset_ref[h] * same) * LOG2E
        outs = []
        for s in range(4):
            highs, lows = [], []
            for h in range(2):
                logits = dot(rows_of(qs, s, h), ks[s], NT) + chunk_bias[h]
                weights = jnp.exp2(logits - jnp.max(logits, axis=-1, keepdims=True))
                high, low = split(weights)
                highs.append(high)
                lows.append(low)
            v = vs[s]
            total = dot(jnp.concatenate(highs, axis=-1), v) + dot(jnp.concatenate(lows, axis=-1), v)
            top = total[:, 0:128]
            top = top + pltpu.roll(top, 64, axis=1)
            outs.append(top / total[:, 128:256] * rows_of(gates, s))
        left_lanes = lane_iota((128, 128)) < 64
        pair = [jnp.where(left_lanes, outs[s1], outs[2 + s1]).reshape(16, 8, 128) for s1 in range(2)]
        for side, tiles in enumerate(merge_halves(*pair)):
            os[pl.ds(8 * x_now, 8), side] = tiles[0:8]
            for i in range(4):
                os[pl.ds(32 + 8 * i + 2 * z_now, 2), side] = tiles[8 + 2 * i:10 + 2 * i]

        def send_o(k, carry):
            turned = lax.rem(k + 4 * (x + z) + grp, 32)
            low_half = 1 - turned // 16
            place = lax.rem(turned // 4, 4)
            to_grp = lax.rem(turned, 4)
            to_dap = low_half * (4 * x_now + place) + (1 - low_half) * (16 + 4 * place + z_now)
            mine = (to_dap == dap) & (to_grp == grp)
            src = os.at[2 * to_dap + to_grp // 2, lax.rem(to_grp, 2)]
            dst = orr.at[grp * 32 + dap]

            @pl.when(mine)
            def _():
                pltpu.make_async_copy(src, dst, o_recv).start()

            @pl.when(jnp.logical_not(mine))
            def _():
                send(src, dst, o_send, o_recv, (to_dap, to_grp))

            return carry

        lax.fori_loop(0, 32, send_o, 0)
        return carry

    lax.fori_loop(0, 4, attend, 0)

    for e in range(8):
        rows = jnp.concatenate([couple_ref[pl.ds(4 * e + i, 32, stride=32), :] for i in range(4)], axis=0)
        high, low = split(jnp.transpose(rows))
        couple_h[:, 128 * e:128 * e + 128] = high
        couple_l[:, 128 * e:128 * e + 128] = low

    drain(xr, x_recv)
    drain(finals, final_recv)
    drain(orr, o_recv)

    zero = jnp.zeros((64, 256), F32)
    parts = split(jnp.concatenate([orr[pl.ds(32 * g, 32)].reshape(256, 128) for g in range(4)], axis=-1))
    for s2 in range(2):
        pieces = []
        for g in range(4):
            own = finals[64 * g:64 * g + 64, :]
            pieces += [own, zero] if s2 == 0 else [zero, own]
        out = dot3(parts, split(jnp.concatenate(pieces, axis=0)))
        msa[pl.ds(256 * s2, 256), :] = xr[s2].reshape(256, 256) + out

    rows = split(normed(msa[...]))
    for m in range(4):
        w = vertical_ref[m]
        if m == 0:
            w = w * (LOG2E / math.sqrt(HEAD))
        out = dot3(rows, split(w))
        for part in range(2):
            proj[2 * m + part] = out[:, 128 * part:128 * part + 128]

    at = lax.broadcasted_iota(jnp.int32, (128, 128), 0)
    to = lax.broadcasted_iota(jnp.int32, (128, 128), 1)
    order = (at == 4 * lax.rem(to // 2, 32) + 2 * (to // 64) + lax.rem(to, 2)).astype(BF16)
    live = dot(live_ref[...].astype(F32).astype(BF16), order)
    live_total = jnp.sum(live)
    mask = (live - 1.0) * (1e9 * LOG2E)

    lane = lane_iota((128, 128))
    for r in range(4):
        for part in range(2):
            q, k, v, g = (proj[2 * m + part, pl.ds(r, 128, stride=4), :] for m in range(4))
            q_h, q_l = split(q)
            k_h, k_l = split(k)
            v_h, v_l = split(v)
            keys = jnp.concatenate([k_h, k_h, k_l], axis=-1)
            wide_q, wide_v = [], []
            for h in range(4):
                mine = lane // HEAD == h
                none = jnp.zeros((128, 128), BF16)
                qm_h, qm_l = jnp.where(mine, q_h, none), jnp.where(mine, q_l, none)
                wide_q.append(jnp.concatenate([qm_h, qm_l, qm_h], axis=-1))
                wide_v.append(jnp.concatenate(
                    [jnp.where(mine, v_h, none), jnp.where(mine, v_l, none), mine.astype(BF16)], axis=-1))
            logits = dot(jnp.concatenate(wide_q, axis=0), keys, NT) + mask
            weights = jnp.exp2(logits - jnp.max(logits, axis=-1, keepdims=True))
            high, low = split(weights)
            values = jnp.concatenate(wide_v, axis=0)

            def heads_in_lanes(a):
                return jnp.concatenate([a[128 * h:128 * h + 128] for h in range(4)], axis=-1)

            total = dot(heads_in_lanes(high), values) + dot(heads_in_lanes(low), values)
            out = (total[:, 0:128] + total[:, 128:256]) / total[:, 256:384]
            attended[part, pl.ds(r, 128, stride=4), :] = out * jax.nn.sigmoid(g)

    current = msa[...] + dot3(split(jnp.concatenate([attended[0], attended[1]], axis=-1)), split(final_ref[...]))
    hidden = jnp.maximum(dot3(split(normed(current)), split(expand_ref[...])), 0.0)
    revised = current + dot3(split(hidden), split(shrink_ref[...]))
    for s2 in range(2):
        revised_ref[:, s2] = revised[256 * s2:256 * s2 + 256].reshape(32, 8, 256)

    unit = normed(revised)
    for part in range(2):
        units[part] = unit[:, 128 * part:128 * part + 128]
    narrow = split(tensor_ref[...].reshape(64, 256))
    for r in range(4):
        both = dot3(narrow, split(jnp.concatenate([units[part, pl.ds(r, 128, stride=4), :] for part in range(2)], axis=-1)), NT)
        left_own[pl.ds(32 * r, 32), :] = both[0:32] * (live / live_total)
        right_own[pl.ds(r, 32, stride=4), :] = both[32:64] * live

    left_to = left_all.at[pl.ds(pl.multiple_of(grp * 128, 128), 128)]
    pltpu.make_async_copy(left_own, left_to, left_recv).start()
    for k in range(1, 4):
        send(left_own, left_to, left_send, left_recv, (dap, lax.rem(grp + k, 4)))

    pass_grp = 2 * y + x // 2
    near = lax.rem(x, 2)
    slot = right_all.at[near, z, grp]
    for y_to in range(2):
        mine = (y == y_to) & (grp == pass_grp)

        @pl.when(mine)
        def _():
            pltpu.make_async_copy(right_own, slot, right_recv.at[0]).start()

        @pl.when(jnp.logical_not(mine))
        def _():
            send(right_own, slot, right_send, right_recv.at[0], (y_to * 16 + x * 4 + z, pass_grp))

    passing = lax.rem(grp, 2) == x // 2
    to_same = (y * 16 + lax.rem(x + 1 + 2 * near, 4) * 4 + z, grp)
    to_other = (y * 16 + lax.rem(x + 3 + 2 * near, 4) * 4 + z, grp)
    first_rows, last_rows = pl.ds(0, 64), pl.ds(64, 64)

    def by_x(p, row, part=None):
        rows = first_rows if p == 0 else last_rows
        which = pl.ds(0, 4) if part is None else pl.ds(2 * part, 2)
        if p == 0:
            return right_all.at[row, :, which, rows]
        return right_all.at[row, z, which, rows]

    def by_z(p, i, part=None):
        if p == 0:
            which = pl.ds(0, 4) if part is None else pl.ds(2 * part, 2)
            return right_all.at[near, z_at[i % 4], which, first_rows]
        which = pl.ds(0, 2) if part is None else part
        return right_all.at[which, z_at[i % 4], :, last_rows]

    def x_begin(p, sem):
        @pl.when(passing)
        def _():
            send(by_x(p, near), by_x(p, near), right_send, right_recv.at[sem], to_same)
            send(by_x(p, near), by_x(p, near), right_send, right_recv.at[sem], to_other)

    def x_forward(p, sem):
        drain(by_x(p, 0), right_recv.at[sem])

        @pl.when(passing)
        def _():
            send(by_x(p, 1 - near, 0), by_x(p, 1 - near, 0), right_send, right_recv.at[sem + 1], to_other)

        @pl.when(jnp.logical_not(passing))
        def _():
            send(by_x(p, 1 - near, 1), by_x(p, 1 - near, 1), right_send, right_recv.at[sem + 2], to_same)

    def x_end(p, sem):
        @pl.when(jnp.logical_not(passing))
        def _():
            drain(by_x(p, 0, 0), right_recv.at[sem + 1])
            drain(by_x(p, 0, 0), right_recv.at[sem + 2])

    def z_begin(p, sem):
        for k, sign in steps:
            send(by_z(p, 0), by_z(p, 0), right_send, right_recv.at[sem + k], along_z(sign))

    def z_forward(p, sem):
        for k, sign in steps:
            drain(by_z(p, 0), right_recv.at[sem + k])
            send(by_z(p, -sign, k), by_z(p, -sign, k), right_send, right_recv.at[sem + 2 + k], along_z(sign))

    def z_end(p, sem):
        for k in range(2):
            drain(by_z(p, 0, 0), right_recv.at[sem + 2 + k])

    @pl.when(passing)
    def _():
        drain(right_all.at[near, z], right_recv.at[0])
        z_begin(0, 1)
    x_begin(1, 5)

    @pl.when(passing)
    def _():
        z_forward(0, 1)
    x_forward(1, 5)

    @pl.when(passing)
    def _():
        z_end(0, 1)
    x_begin(0, 8)
    x_end(1, 5)
    z_begin(1, 11)
    x_forward(0, 8)
    z_forward(1, 11)
    x_end(0, 8)
    z_end(1, 11)
    drain(left_all, left_recv)

    def right_at(source, e2):
        return right_all[source // 16, (source // 4) % 4, source % 4, pl.ds(e2 * 8, 8), :]

    left_h, left_l = split(left_all[...])
    left_wide = jnp.concatenate([left_h, left_l, left_h], axis=-1)

    def sort(e2, carry):
        for t in range(16):
            first, second = merge_halves(
                right_at(2 * t, e2), right_at(2 * t + 1, e2))
            right_sorted[2 * e2, pl.ds(8 * t, 8), :] = first
            right_sorted[2 * e2 + 1, pl.ds(8 * t, 8), :] = second
        return carry

    lax.fori_loop(0, 16, sort, 0)

    def outer(e2, carry):
        high, low = split(right_sorted[pl.ds(2 * e2, 2)].reshape(256, 128))
        right_wide = jnp.concatenate([high, high, low], axis=-1)
        product = dot(left_wide, right_wide, NT)
        high, low = split(product)
        for i in range(16):
            for e1 in range(2):
                at = pl.ds(pl.multiple_of(64 * e2 + 32 * e1, 32), 32)
                lanes = slice(128 * (i % 2), 128 * (i % 2) + 128)
                rows, cols = slice(32 * i, 32 * i + 32), slice(128 * e1, 128 * e1 + 128)
                outer_h[i // 2, at, lanes] = high[rows, cols]
                outer_l[i // 2, at, lanes] = low[rows, cols]
        return carry

    lax.fori_loop(0, 16, outer, 0)

    def finish(i2, carry):
        out = dot3((couple_h[...], couple_l[...]), (outer_h[i2], outer_l[i2]))
        for i1 in range(2):
            out_ref[2 * i2 + i1] = jnp.transpose(out[:, 128 * i1:128 * i1 + 128])
        return carry

    lax.fori_loop(0, 8, finish, 0)

    for _ in range(31):
        drain(bias_ref, bias_send)
    drain(xs.at[0:31], x_send)
    drain(orr.at[0:127], o_send)
    drain(finals.at[0:192], final_send)
    drain(left_all.at[0:384], left_send)
    for y_to in range(2):
        @pl.when(jnp.logical_not((y == y_to) & (grp == pass_grp)))
        def _():
            drain(right_own, right_send)

    @pl.when(passing)
    def _():
        for _ in range(2):
            drain(by_z(0, 0), right_send)
            drain(by_z(0, 0, 0), right_send)
        for p in range(2):
            for _ in range(2):
                drain(by_x(p, 0), right_send)
    for p in range(2):
        drain(by_x(p, 0, 0), right_send)
    for _ in range(2):
        drain(by_z(1, 0), right_send)
        drain(by_z(1, 0, 0), right_send)


VM = pl.BlockSpec(memory_space=pltpu.VMEM)
SM = pl.BlockSpec(memory_space=pltpu.SMEM)
LIMIT = 58 * 1024 * 1024


def body(
    homolog_stack,
    couple_score_offset,
    strand_identity,
    strand_score_offset,
    homolog_presence,
    horizontal_matrix,
    horizontal_final_matrix,
    vertical_matrix,
    vertical_final_matrix,
    expand_matrix,
    shrink_matrix,
    tensor_matrix,
    couple_matrix,
):
    dma = pltpu.SemaphoreType.DMA
    regular = pltpu.SemaphoreType.REGULAR
    revised, pair = pl.pallas_call(
        kernel,
        out_shape=[
            jax.ShapeDtypeStruct((32, 2, 8, 256), F32),
            jax.ShapeDtypeStruct((16, 128, 128), F32),
        ],
        in_specs=[VM, VM, VM, SM] + [VM] * 9,
        out_specs=[VM, VM],
        scratch_shapes=[
            pltpu.VMEM((2, 4, 4, 2, 16, 512), F32),
            pltpu.VMEM((32, 2, 8, 256), F32),
            pltpu.VMEM((2, 32, 8, 256), F32),
            pltpu.VMEM((64, 2, 8, 128), F32),
            pltpu.VMEM((128, 8, 128), F32),
            pltpu.VMEM((256, 256), F32),
            pltpu.VMEM((256, 768), BF16),
            pltpu.VMEM((256, 768), BF16),
            pltpu.VMEM((4, 2, 32, 16, 256), BF16),
            pltpu.VMEM((4, 512, 256), BF16),
            pltpu.VMEM((4, 1024, 256), BF16),
            pltpu.VMEM((4, 32, 16, 128), F32),
            pltpu.VMEM((32, 16, 128), F32),
            pltpu.VMEM((2, 128, 512), F32),
            pltpu.VMEM((512, 256), F32),
            pltpu.VMEM((8, 512, 128), F32),
            pltpu.VMEM((2, 512, 128), F32),
            pltpu.VMEM((2, 512, 128), F32),
            pltpu.VMEM((128, 128), F32),
            pltpu.VMEM((128, 128), F32),
            pltpu.VMEM((512, 128), F32),
            pltpu.VMEM((2, 4, 4, 128, 128), F32),
            pltpu.VMEM((32, 128, 128), F32),
            pltpu.VMEM((8, 1024, 256), BF16),
            pltpu.VMEM((8, 1024, 256), BF16),
            pltpu.VMEM((128, 1024), BF16),
            pltpu.VMEM((128, 1024), BF16),
            dma, dma((22,)), dma, dma, dma, dma, dma, dma,
            dma, dma, dma, dma((15,)), regular, regular, regular,
        ],
        compiler_params=pltpu.CompilerParams(
            collective_id=0, has_side_effects=True, vmem_limit_bytes=LIMIT
        ),
        name="msa_block",
    )(
        homolog_stack.reshape(4, 32, 2, 8, 256),
        couple_score_offset,
        strand_identity.reshape(1, 512),
        strand_score_offset,
        jnp.swapaxes(horizontal_matrix, 1, 2),
        horizontal_final_matrix,
        homolog_presence.reshape(1, 128),
        vertical_matrix,
        vertical_final_matrix,
        expand_matrix,
        shrink_matrix,
        jnp.swapaxes(tensor_matrix, 1, 2),
        couple_matrix,
    )
    return revised.reshape(128, 4, 256), pair


def solution(mesh):
    return jax.shard_map(
        body,
        mesh=mesh,
        in_specs=(
            P("dap", None, None),
            P("grp", "dap", None),
            P(),
            P("grp"),
            P(),
            P(None, None, "grp"),
            P("grp", None),
            P(),
            P(),
            P(),
            P(),
            P(),
            P(),
        ),
        out_specs=(P(None, ("dap", "grp"), None), P("dap", "grp", None)),
        check_vma=False,
    )
```

```python
import functools
import math

import jax
import jax.numpy as jnp
from jax import lax
from jax.experimental import pallas as pl
from jax.experimental.pallas import tpu as pltpu
from jax.sharding import PartitionSpec as P

F32 = jnp.float32
BF16 = jnp.bfloat16
MESH = pl.DeviceIdType.MESH
HEAD = 32
LOG2E = math.log2(math.e)
NN = (((1,), (0,)), ((), ()))
NT = (((1,), (1,)), ((), ()))


def split(a):
    high = a.astype(BF16)
    return high, (a - high.astype(F32)).astype(BF16)


def dot(a, b, dims=NN):
    return lax.dot_general(a, b, dims, preferred_element_type=F32)


def dot3(a, b, dims=NN):
    return dot(a[0], b[0], dims) + (dot(a[0], b[1], dims) + dot(a[1], b[0], dims))


def normed(rows):
    center = rows - jnp.mean(rows, axis=-1, keepdims=True)
    spread = jnp.mean(center * center, axis=-1, keepdims=True)
    return center * lax.rsqrt(spread + 1e-05)


def merge_halves(a, b):
    upper = lax.broadcasted_iota(jnp.int32, a.shape, a.ndim - 2) < 4
    first = jnp.where(upper, a, pltpu.roll(b, 4, axis=b.ndim - 2))
    second = jnp.where(upper, pltpu.roll(a, 4, axis=a.ndim - 2), b)
    return first, second


def lane_iota(shape):
    return lax.broadcasted_iota(jnp.int32, shape, len(shape) - 1)


def drain(ref, sem):
    pltpu.make_async_copy(ref, ref, sem).wait()


def signal(sem, device):
    pl.semaphore_signal(sem, inc=1, device_id=device, device_id_type=MESH)


def send(src, dst, send_sem, recv_sem, device):
    pltpu.make_async_remote_copy(
        src_ref=src, dst_ref=dst, send_sem=send_sem, recv_sem=recv_sem,
        device_id=device, device_id_type=MESH,
    ).start()


def kernel(
    x_ref, bias_ref, ids_ref, offset_ref, weight_ref, final_in_ref, live_ref, tensor_ref,
    vertical_in, final_in, expand_in, shrink_in, couple_in,
    revised_ref, out_ref,
    bias_all, xs, xr, os, og, finals, join_h, join_l, wide_h, wide_l, qs, ks, vs, gates, ids_col, chunk_bias,
    msa, proj, attended, units,
    left_own, right_own, left_all, right_all, outer_h, outer_l, couple_h, couple_l,
    vertical_h, vertical_l, last_h, last_l, expand_h, expand_l, shrink_h, shrink_l,
    bias_send, bias_recv, x_send, x_recv, o_send, o_recv, final_send, final_recv,
    left_send, left_recv, right_send, right_recv, near_z, near_x, near_y,
    vertical_ref, final_ref, expand_ref, shrink_ref, couple_ref, fetch,
):
    dap = lax.axis_index("dap")
    grp = lax.axis_index("grp")
    y, x, z = dap // 16, lax.rem(dap // 4, 4), lax.rem(dap, 4)
    x_at = [lax.rem(x + i, 4) for i in range(4)]
    z_at = [lax.rem(z + i, 4) for i in range(4)]

    def along_x(i):
        return y * 16 + x_at[i % 4] * 4 + z, grp

    def along_z(i):
        return y * 16 + x * 4 + z_at[i % 4], grp

    across_y = ((1 - y) * 16 + x * 4 + z, grp)

    barrier = pltpu.get_barrier_semaphore()
    for i in range(1, 4):
        signal(barrier, along_x(i))
        signal(barrier, along_z(i))
        signal(barrier, (dap, lax.rem(grp + i, 4)))
    signal(barrier, across_y)

    late = (
        (vertical_in, vertical_ref), (final_in, final_ref), (expand_in, expand_ref),
        (shrink_in, shrink_ref), (couple_in, couple_ref),
    )
    for i, (src, dst) in enumerate(late):
        pltpu.make_async_copy(src, dst, fetch.at[i]).start()

    zero = jnp.zeros((64, 256), F32)
    q_w = weight_ref[0] * (LOG2E / math.sqrt(HEAD))
    k_w, v_w, g_w = weight_ref[1], weight_ref[2], weight_ref[3]
    for at, parts in ((0, (q_w, q_w, q_w, zero)), (256, (k_w, k_w, k_w, zero)), (512, (v_w, v_w, g_w, g_w))):
        high, low = split(jnp.transpose(jnp.concatenate(parts, axis=0)))
        wide_h[:, at:at + 256] = high
        wide_l[:, at:at + 256] = low
    pl.semaphore_wait(barrier, 10)

    def unit(p, i, j, h=None):
        a, b = (x_at[j % 4], z_at[i % 4]) if p == 0 else (x_at[i % 4], z_at[j % 4])
        return bias_all.at[p, a, b] if h is None else bias_all.at[p, a, b, h]

    def line(p, j, h):
        return bias_all.at[0, x_at[j % 4], :, h] if p == 0 else bias_all.at[1, :, z_at[j % 4], h]

    def first_axis(p, i):
        return along_z(i) if p == 0 else along_x(i)

    def second_axis(p, i):
        return along_x(i) if p == 0 else along_z(i)

    steps = ((0, 1), (1, -1))
    own = bias_all.at[y, x, z]
    send(bias_ref, own, bias_send, bias_recv.at[0], across_y)
    pltpu.make_async_copy(bias_ref, own, bias_recv.at[21]).start()
    for i in range(1, 4):
        signal(near_z, along_z(i))
    drain(bias_ref, bias_recv.at[21])

    def own_path(act):
        for p in range(2):
            @pl.when(y == p)
            def _():
                act(p)

    def other_path(act):
        for p in range(2):
            @pl.when(y == 1 - p)
            def _():
                act(p)

    def spread(p):
        for i in (1, 3, 2):
            send(unit(p, 0, 0), unit(p, 0, 0), bias_send, bias_recv.at[1 + 10 * p], first_axis(p, i))

    def spread_line(p):
        drain(bias_all.at[0, 0, 0:3], bias_recv.at[1 + 10 * p])
        for k, sign in steps:
            send(line(p, 0, k), line(p, 0, k), bias_send, bias_recv.at[5 + 10 * p + k], second_axis(p, sign))
        for k, sign in steps:
            send(line(p, 0, 1 - k), line(p, 0, 1 - k), bias_send,
                 bias_recv.at[7 + 10 * p + k], second_axis(p, sign))

    def forward_line(p):
        for k, sign in steps:
            drain(line(0, 0, 0), bias_recv.at[5 + 10 * p + k])
            send(line(p, -sign, k), line(p, -sign, k), bias_send,
                 bias_recv.at[9 + 10 * p + k], second_axis(p, sign))

    own_path(spread)

    final_to = finals.at[pl.ds(pl.multiple_of(grp * 64, 64), 64)]
    pltpu.make_async_copy(final_in_ref, final_to, final_recv).start()
    for k in range(1, 4):
        send(final_in_ref, final_to, final_send, final_recv, (dap, lax.rem(grp + k, 4)))

    def project(s):
        rows = split(normed(x_ref[s].reshape(512, 256)))
        out = dot3(rows, (wide_h[...], wide_l[...]))
        lane = lane_iota((512, 256))
        head = lax.rem(lane, 64) // HEAD
        q_hi, q_lo = split(out[:, 0:256])
        q = jnp.where((lane >= 64) & (lane < 128), q_lo.astype(F32), q_hi.astype(F32))
        k_hi, k_lo = split(out[:, 256:512])
        k = jnp.where((lane >= 128) & (lane < 192), k_lo.astype(F32), k_hi.astype(F32))
        ks[s] = k.astype(BF16)
        lane_v = lane_iota((512, 128))
        head_v = lax.rem(lane_v, 64) // HEAD
        v_hi, v_lo = split(out[:, 512:640])
        v = jnp.where(lane_v >= 64, v_lo.astype(F32), v_hi.astype(F32))
        for h in range(2):
            qs[s, h] = jnp.where(head == h, q, 0.0).astype(BF16).reshape(32, 16, 256)
            vs[s, pl.ds(512 * h, 512), 0:128] = jnp.where(head_v == h, v, 0.0).astype(BF16)
            vs[s, pl.ds(512 * h, 512), 128:256] = jnp.where(head_v == h, 1.0, 0.0).astype(BF16)
        gates[s] = jax.nn.sigmoid(out[:, 640:768]).reshape(32, 16, 128)

    def project_and(s, carry):
        project(s)

        @pl.when(s == 0)
        def _():
            pl.semaphore_wait(near_z, 3)
            for i in range(1, 4):
                signal(near_x, along_x(i))
            drain(bias_ref, bias_recv.at[0])
            other_path(spread)

        @pl.when(s == 1)
        def _():
            own_path(spread_line)
            pl.semaphore_wait(near_x, 3)
            signal(near_y, across_y)

        @pl.when(s == 2)
        def _():
            other_path(spread_line)

        return carry

    lax.fori_loop(0, 4, project_and, 0)

    half = lax.rem(grp, 2)
    for s2 in range(2):
        first, second = merge_halves(x_ref[2 * s2, :, grp // 2], x_ref[2 * s2 + 1, :, grp // 2])
        xs[:, s2] = jnp.where(half == 0, first, second)
    for i in range(4):
        block = jnp.broadcast_to(ids_ref[:, 128 * i:128 * i + 128].astype(F32), (128, 128))
        ids_col[8 * i:8 * i + 8] = jnp.transpose(block).reshape(8, 16, 128)
    pl.semaphore_wait(near_y, 1)

    drain(finals, final_recv)
    gap = jnp.zeros((64, 256), F32)
    for s2 in range(2):
        pieces = []
        for g in range(4):
            piece = finals[64 * g:64 * g + 64, :]
            pieces += [piece, gap] if s2 == 0 else [gap, piece]
        join_h[s2], join_l[s2] = split(jnp.concatenate(pieces, axis=0))

    for i, (src, dst) in enumerate(late):
        pltpu.make_async_copy(src, dst, fetch.at[i]).wait()

    for m in range(4):
        w = vertical_ref[m]
        if m == 0:
            w = w * (LOG2E / math.sqrt(HEAD))
        vertical_h[m], vertical_l[m] = split(w)
    last_h[...], last_l[...] = split(final_ref[...])
    expand_h[...], expand_l[...] = split(expand_ref[...])
    shrink_h[...], shrink_l[...] = split(shrink_ref[...])
    for odd in range(2):
        for b in range(4):
            rows = jnp.concatenate(
                [couple_ref[pl.ds(2 * (4 * b + i) + odd, 32, stride=32), :] for i in range(4)], axis=0)
            at = 512 * odd + 128 * b
            couple_h[:, at:at + 128], couple_l[:, at:at + 128] = split(jnp.transpose(rows))

    def turned(step):
        turn = step + step // 2 - 2 * (step // 3)
        return lax.rem(x + turn, 4), lax.rem(z + turn, 4)

    def settle(step):
        x_now, z_now = turned(step)
        drain(og.at[:, 0, 0:2], o_recv.at[step])
        rows = split(jnp.concatenate(
            [jnp.concatenate([og[g, 0, x_now].reshape(32, 128), og[g, 1, :, z_now].reshape(32, 128)], axis=0)
             for g in range(4)], axis=-1))
        for s2 in range(2):
            out = dot3(rows, (join_h[s2], join_l[s2])).reshape(8, 8, 256)
            for i in range(4):
                xs[4 * x_now + i, s2] += out[i]
                xs[16 + 4 * i + z_now, s2] += out[4 + i]

        def send_x(k, carry):
            low_half = 1 - k // 4
            place = lax.rem(k + x + z, 4)
            to = low_half * (4 * x_now + place) + (1 - low_half) * (16 + 4 * place + z_now)

            @pl.when(to == dap)
            def _():
                pltpu.make_async_copy(xs.at[to], xr.at[:, dap], x_recv).start()

            @pl.when(to != dap)
            def _():
                send(xs.at[to], xr.at[:, dap], x_send, x_recv, (to, grp))

            return carry

        lax.fori_loop(0, 8, send_x, 0)

    def attend(step, carry):
        x_now, z_now = turned(step)

        @pl.when(step == 1)
        def _():
            own_path(forward_line)
            other_path(forward_line)
            for p in range(2):
                drain(line(0, 0, 0), bias_recv.at[7 + 10 * p + 1])

        @pl.when(step == 2)
        def _():
            for p in range(2):
                drain(line(0, 0, 0), bias_recv.at[7 + 10 * p])

        @pl.when(step == 3)
        def _():
            for p in range(2):
                for k in range(2):
                    drain(line(0, 0, 0), bias_recv.at[9 + 10 * p + k])

        def rows_of(ref, *lead):
            shape = ref.shape[-2:]
            upper = ref[(*lead, pl.ds(4 * x_now, 4))].reshape(64, shape[-1])
            return jnp.concatenate([upper] + [ref[(*lead, 16 + 4 * i + z_now)] for i in range(4)], axis=0)

        own_ids = rows_of(ids_col)
        same = (jnp.concatenate([own_ids] * 4, axis=-1) == ids_ref[...].astype(F32)).astype(F32)
        for h in range(2):
            here = jnp.concatenate(
                [bias_all[0, x_now, :, h].reshape(64, 512), bias_all[1, :, z_now, h].reshape(64, 512)], axis=0)
            chunk_bias[h] = (here + offset_ref[h] * same) * LOG2E
        outs = []
        for s in range(4):
            highs, lows = [], []
            for h in range(2):
                logits = dot(rows_of(qs, s, h), ks[s], NT) + chunk_bias[h]
                weights = jnp.exp2(logits - jnp.max(logits, axis=-1, keepdims=True))
                high, low = split(weights)
                highs.append(high)
                lows.append(low)
            v = vs[s]
            total = dot(jnp.concatenate(highs, axis=-1), v) + dot(jnp.concatenate(lows, axis=-1), v)
            top = total[:, 0:128]
            top = top + pltpu.roll(top, 64, axis=1)
            outs.append(top / total[:, 128:256] * rows_of(gates, s))
        left_lanes = lane_iota((128, 128)) < 64
        pair = [jnp.where(left_lanes, outs[s1], outs[2 + s1]).reshape(16, 8, 128) for s1 in range(2)]
        for side, tiles in enumerate(merge_halves(*pair)):
            tiles = tiles.reshape(8, 2, 8, 128)
            for t in range(2):
                os[2 * t + side, 0, x_now] = tiles[0:4, t]
                for i in range(4):
                    os[2 * t + side, 1, i, z_now] = tiles[4 + i, t]
        pltpu.make_async_copy(os.at[grp, 0, x_now], og.at[grp, 0, x_now], o_recv.at[step]).start()
        pltpu.make_async_copy(os.at[grp, 1, :, z_now], og.at[grp, 1, :, z_now], o_recv.at[step]).start()
        for k in (2, 1, 3):
            to = lax.rem(grp + k, 4)
            send(os.at[to, 0, x_now], og.at[grp, 0, x_now], o_send, o_recv.at[step], (dap, to))
            send(os.at[to, 1, :, z_now], og.at[grp, 1, :, z_now], o_send, o_recv.at[step], (dap, to))

        @pl.when(step > 0)
        def _():
            settle(step - 1)

        return carry

    lax.fori_loop(0, 4, attend, 0)
    settle(3)

    drain(xr, x_recv)

    for s2 in range(2):
        stack = xr[s2].reshape(256, 256)
        for part in range(2):
            msa[part, pl.ds(256 * s2, 256), :] = stack[:, 128 * part:128 * part + 128]

    rows = split(normed(jnp.concatenate([msa[0], msa[1]], axis=-1)))
    for m in range(4):
        out = dot3(rows, (vertical_h[m], vertical_l[m]))
        for part in range(2):
            proj[2 * m + part] = out[:, 128 * part:128 * part + 128]

    at = lax.broadcasted_iota(jnp.int32, (128, 128), 0)
    to = lax.broadcasted_iota(jnp.int32, (128, 128), 1)
    order = (at == 4 * lax.rem(to // 2, 32) + 2 * (to // 64) + lax.rem(to, 2)).astype(BF16)
    live = dot(live_ref[...].astype(F32).astype(BF16), order)
    live_total = jnp.sum(live)
    mask = (live - 1.0) * (1e9 * LOG2E)

    lane = lane_iota((128, 128))
    def attend_column(r):
        for part in range(2):
            q, k, v, g = (proj[2 * m + part, pl.ds(r, 128, stride=4), :] for m in range(4))
            q_h, q_l = split(q)
            k_h, k_l = split(k)
            v_h, v_l = split(v)
            keys = jnp.concatenate([k_h, k_h, k_l], axis=-1)
            wide_q, wide_v = [], []
            for h in range(4):
                mine = lane // HEAD == h
                none = jnp.zeros((128, 128), BF16)
                qm_h, qm_l = jnp.where(mine, q_h, none), jnp.where(mine, q_l, none)
                wide_q.append(jnp.concatenate([qm_h, qm_l, qm_h], axis=-1))
                wide_v.append(jnp.concatenate(
                    [jnp.where(mine, v_h, none), jnp.where(mine, v_l, none), mine.astype(BF16)], axis=-1))
            logits = dot(jnp.concatenate(wide_q, axis=0), keys, NT) + mask
            weights = jnp.exp2(logits - jnp.max(logits, axis=-1, keepdims=True))
            high, low = split(weights)
            values = jnp.concatenate(wide_v, axis=0)

            def heads_in_lanes(a):
                return jnp.concatenate([a[128 * h:128 * h + 128] for h in range(4)], axis=-1)

            total = dot(heads_in_lanes(high), values) + dot(heads_in_lanes(low), values)
            out = (total[:, 0:128] + total[:, 128:256]) / total[:, 256:384]
            attended[part, pl.ds(128 * (r % 2), 128), :] = out * jax.nn.sigmoid(g)

    narrow = split(tensor_ref[...].reshape(64, 256))

    def finish_column(turn):
        here = [pl.ds(2 * turn + r2, 128, stride=4) for r2 in range(2)]
        before = jnp.concatenate(
            [jnp.concatenate([msa[part, rows, :] for rows in here], axis=0) for part in range(2)], axis=-1)
        gated = split(jnp.concatenate([attended[0], attended[1]], axis=-1))
        current = before + dot3(gated, (last_h[...], last_l[...]))
        hidden = jnp.maximum(dot3(split(normed(current)), (expand_h[...], expand_l[...])), 0.0)
        revised = current + dot3(split(hidden), (shrink_h[...], shrink_l[...]))
        unit_high, unit_low = split(normed(revised))
        for r2 in range(2):
            mine = slice(128 * r2, 128 * r2 + 128)
            for part in range(2):
                units[part, here[r2], :] = revised[mine, 128 * part:128 * part + 128]
            both = dot3(narrow, (unit_high[mine], unit_low[mine]), NT)
            left_own[pl.ds(64 * turn + 32 * r2, 32), :] = both[0:32] * (live / live_total)
            right_own[turn, pl.ds(32 * r2, 32), :] = both[32:64] * live

    pass_grp = 2 * y + x // 2
    near = lax.rem(x, 2)
    passing = lax.rem(grp, 2) == x // 2
    to_same = (y * 16 + lax.rem(x + 1 + 2 * near, 4) * 4 + z, grp)
    to_other = (y * 16 + lax.rem(x + 3 + 2 * near, 4) * 4 + z, grp)
    top, low = pl.ds(0, 32), pl.ds(32, 32)

    def right_begin(turn):
        slot = right_all.at[turn, near, z, grp]
        for y_to in range(2):
            mine = (y == y_to) & (grp == pass_grp)

            @pl.when(mine)
            def _():
                pltpu.make_async_copy(right_own.at[turn], slot, right_recv.at[turn, 0]).start()

            @pl.when(jnp.logical_not(mine))
            def _():
                send(right_own.at[turn], slot, right_send, right_recv.at[turn, 0],
                     (y_to * 16 + x * 4 + z, pass_grp))

    def right_first(turn):
        @pl.when(passing)
        def _():
            drain(right_all.at[turn, near, z], right_recv.at[turn, 0])
            along = right_all.at[turn, near, z, :, top]
            for i in (1, 3, 2):
                send(along, along, right_send, right_recv.at[turn, 1], along_z(i))
            along = right_all.at[turn, near, z, :, low]
            for to in (to_same, to_other, along_x(2)):
                send(along, along, right_send, right_recv.at[turn, 2], to)

    def x_column(turn, row, part=None):
        which = pl.ds(0, 4) if part is None else pl.ds(2 * part, 2)
        return right_all.at[turn, row, :, which, top]

    def z_column(turn, i, part=None):
        which = pl.ds(0, 2) if part is None else part
        return right_all.at[turn, which, z_at[i % 4], :, low]

    def right_second(turn):
        @pl.when(passing)
        def _():
            drain(right_all.at[turn, near, 0:3, :, top], right_recv.at[turn, 1])
            for to in (to_same, to_other):
                send(x_column(turn, near), x_column(turn, near), right_send, right_recv.at[turn, 3], to)
            drain(right_all.at[turn, 0, z, :, low], right_recv.at[turn, 2])

        @pl.when(jnp.logical_not(passing))
        def _():
            drain(right_all.at[turn, :, z, :, low], right_recv.at[turn, 2])

        for k, sign in steps:
            send(z_column(turn, 0), z_column(turn, 0), right_send, right_recv.at[turn, 6 + k], along_z(sign))

    def right_third(turn):
        drain(x_column(turn, 0), right_recv.at[turn, 3])

        @pl.when(passing)
        def _():
            piece = x_column(turn, 1 - near, 0)
            send(piece, piece, right_send, right_recv.at[turn, 4], to_other)

        @pl.when(jnp.logical_not(passing))
        def _():
            piece = x_column(turn, 1 - near, 1)
            send(piece, piece, right_send, right_recv.at[turn, 5], to_same)

        for k, sign in steps:
            drain(z_column(turn, 0), right_recv.at[turn, 6 + k])
            piece = z_column(turn, -sign, k)
            send(piece, piece, right_send, right_recv.at[turn, 8 + k], along_z(sign))

    def right_end(turn):
        @pl.when(jnp.logical_not(passing))
        def _():
            for k in range(2):
                drain(x_column(turn, 0, 0), right_recv.at[turn, 4 + k])
        for k in range(2):
            drain(z_column(turn, 0, 0), right_recv.at[turn, 8 + k])

    def right_sent(turn):
        for y_to in range(2):
            @pl.when(jnp.logical_not((y == y_to) & (grp == pass_grp)))
            def _():
                drain(right_own.at[turn], right_send)

        @pl.when(passing)
        def _():
            for _ in range(2):
                drain(right_all.at[turn, 0, 0:3, :, top], right_send)
                drain(x_column(turn, 0), right_send)

        drain(x_column(turn, 0, 0), right_send)
        for k in range(2):
            drain(z_column(turn, 0), right_send)
            drain(z_column(turn, 0, 0), right_send)

    lane_low = lane_iota((256, 128)) < 64

    def outer(turn):
        left_h, left_l = split(left_all[...].reshape(8, 2, 32, 128))
        left_wide = [
            jnp.concatenate([a[:, odd].reshape(256, 128) for a in (left_h, left_l, left_h)], axis=-1)
            for odd in range(2)
        ]
        right_flat = right_all.reshape(2 * 32 * 64, 128)

        def step(quad, carry):
            wide = []
            for e in range(4):
                high, low = split(jnp.concatenate(
                    [right_flat[pl.ds(2048 * turn + 32 * r2 + 4 * quad + e, 32, stride=64), :] for r2 in range(2)],
                    axis=0))
                wide.append(jnp.concatenate([high, high, low], axis=-1))
            even = dot(left_wide[0], jnp.concatenate(wide, axis=0), NT)
            odd = dot(left_wide[1], jnp.concatenate([wide[1], wide[0], wide[3], wide[2]], axis=0), NT)
            for m in range(2):
                lanes = slice(128 * m, 128 * m + 128)
                a, b = even[:, lanes], odd[:, lanes]
                for side, mixed in enumerate((jnp.where(lane_low, a, b), jnp.where(lane_low, b, a))):
                    high, low = split(mixed)
                    at = pl.ds(pl.multiple_of(512 * side + 64 * quad + 32 * m, 32), 32)
                    for i in range(8):
                        cols = slice(128 * (i % 2), 128 * (i % 2) + 128)
                        outer_h[i // 2, at, cols] = high[32 * i:32 * i + 32]
                        outer_l[i // 2, at, cols] = low[32 * i:32 * i + 32]
            return carry

        lax.fori_loop(0, 8, step, 0)

    def finish(turn):
        def step(i4, carry):
            total = []
            for side in range(2):
                at = slice(512 * side, 512 * side + 512)
                total.append(dot3((couple_h[:, at], couple_l[:, at]), (outer_h[i4, at, :], outer_l[i4, at, :])))
            for i2 in range(2):
                lanes = slice(128 * i2, 128 * i2 + 128)
                block = jnp.transpose(total[0][:, lanes] + pltpu.roll(total[1][:, lanes], 64, axis=1))
                for i1 in range(2):
                    for r2 in range(2):
                        at = 64 * i1 + 32 * r2
                        out_ref[4 * i4 + 2 * i2 + i1, pl.ds(2 * turn + r2, 32, stride=4), :] = block[at:at + 32]
            return carry

        lax.fori_loop(0, 4, step, 0)

    attend_column(0)
    attend_column(1)
    finish_column(0)
    right_begin(0)
    attend_column(2)
    attend_column(3)
    right_first(0)
    finish_column(1)
    right_begin(1)
    right_second(0)
    right_first(1)
    left_to = left_all.at[pl.ds(pl.multiple_of(grp * 128, 128), 128)]
    pltpu.make_async_copy(left_own, left_to, left_recv).start()
    for k in range(1, 4):
        send(left_own, left_to, left_send, left_recv, (dap, lax.rem(grp + k, 4)))
    right_third(0)
    right_second(1)
    for s2 in range(2):
        for part in range(2):
            revised_ref[:, s2, :, 128 * part:128 * part + 128] = units[part, pl.ds(256 * s2, 256), :].reshape(32, 8, 128)
    right_end(0)
    drain(left_all, left_recv)
    outer(0)
    right_third(1)
    finish(0)
    right_end(1)
    outer(1)
    finish(1)

    for _ in range(31):
        drain(bias_ref, bias_send)
    drain(xs.at[0:31], x_send)
    drain(og.at[0:3], o_send)
    drain(finals.at[0:192], final_send)
    drain(left_all.at[0:384], left_send)
    for turn in range(2):
        right_sent(turn)


VM = pl.BlockSpec(memory_space=pltpu.VMEM)
SM = pl.BlockSpec(memory_space=pltpu.SMEM)
LIMIT = 58 * 1024 * 1024


def body(
    homolog_stack,
    couple_score_offset,
    strand_identity,
    strand_score_offset,
    homolog_presence,
    horizontal_matrix,
    horizontal_final_matrix,
    vertical_matrix,
    vertical_final_matrix,
    expand_matrix,
    shrink_matrix,
    tensor_matrix,
    couple_matrix,
):
    dma = pltpu.SemaphoreType.DMA
    regular = pltpu.SemaphoreType.REGULAR
    revised, pair = pl.pallas_call(
        kernel,
        out_shape=[
            jax.ShapeDtypeStruct((32, 2, 8, 256), F32),
            jax.ShapeDtypeStruct((16, 128, 128), F32),
        ],
        in_specs=[VM, VM, VM, SM] + [VM] * 4 + [pl.BlockSpec(memory_space=pl.ANY)] * 5,
        out_specs=[VM, VM],
        scratch_shapes=[
            pltpu.VMEM((2, 4, 4, 2, 16, 512), F32),
            pltpu.VMEM((32, 2, 8, 256), F32),
            pltpu.VMEM((2, 32, 8, 256), F32),
            pltpu.VMEM((4, 2, 4, 4, 8, 128), F32),
            pltpu.VMEM((4, 2, 4, 4, 8, 128), F32),
            pltpu.VMEM((256, 256), F32),
            pltpu.VMEM((2, 512, 256), BF16),
            pltpu.VMEM((2, 512, 256), BF16),
            pltpu.VMEM((256, 768), BF16),
            pltpu.VMEM((256, 768), BF16),
            pltpu.VMEM((4, 2, 32, 16, 256), BF16),
            pltpu.VMEM((4, 512, 256), BF16),
            pltpu.VMEM((4, 1024, 256), BF16),
            pltpu.VMEM((4, 32, 16, 128), F32),
            pltpu.VMEM((32, 16, 128), F32),
            pltpu.VMEM((2, 128, 512), F32),
            pltpu.VMEM((2, 512, 128), F32),
            pltpu.VMEM((8, 512, 128), F32),
            pltpu.VMEM((2, 256, 128), F32),
            pltpu.VMEM((2, 512, 128), F32),
            pltpu.VMEM((128, 128), F32),
            pltpu.VMEM((2, 64, 128), F32),
            pltpu.VMEM((512, 128), F32),
            pltpu.VMEM((2, 2, 4, 4, 64, 128), F32),
            pltpu.VMEM((4, 1024, 256), BF16),
            pltpu.VMEM((4, 1024, 256), BF16),
            pltpu.VMEM((128, 1024), BF16),
            pltpu.VMEM((128, 1024), BF16),
            pltpu.VMEM((4, 256, 256), BF16),
            pltpu.VMEM((4, 256, 256), BF16),
            pltpu.VMEM((256, 256), BF16),
            pltpu.VMEM((256, 256), BF16),
            pltpu.VMEM((256, 1024), BF16),
            pltpu.VMEM((256, 1024), BF16),
            pltpu.VMEM((1024, 256), BF16),
            pltpu.VMEM((1024, 256), BF16),
            dma, dma((22,)), dma, dma, dma, dma((4,)), dma, dma,
            dma, dma, dma, dma((2, 10)), regular, regular, regular,
            pltpu.VMEM((4, 256, 256), F32),
            pltpu.VMEM((256, 256), F32),
            pltpu.VMEM((256, 1024), F32),
            pltpu.VMEM((1024, 256), F32),
            pltpu.VMEM((1024, 128), F32),
            dma((5,)),
        ],
        compiler_params=pltpu.CompilerParams(
            collective_id=0, has_side_effects=True, vmem_limit_bytes=LIMIT
        ),
        name="msa_block",
    )(
        homolog_stack.reshape(4, 32, 2, 8, 256),
        couple_score_offset,
        strand_identity.reshape(1, 512),
        strand_score_offset,
        jnp.swapaxes(horizontal_matrix, 1, 2),
        horizontal_final_matrix,
        homolog_presence.reshape(1, 128),
        jnp.swapaxes(tensor_matrix, 1, 2),
        vertical_matrix,
        vertical_final_matrix,
        expand_matrix,
        shrink_matrix,
        couple_matrix,
    )
    return revised.reshape(128, 4, 256), pair


def solution(mesh):
    return jax.shard_map(
        body,
        mesh=mesh,
        in_specs=(
            P("dap", None, None),
            P("grp", "dap", None),
            P(),
            P("grp"),
            P(),
            P(None, None, "grp"),
            P("grp", None),
            P(),
            P(),
            P(),
            P(),
            P(),
            P(),
        ),
        out_specs=(P(None, ("dap", "grp"), None), P("dap", "grp", None)),
        check_vma=False,
    )
```

```python
import functools
import math

import jax
import jax.numpy as jnp
from jax import lax
from jax.experimental import pallas as pl
from jax.experimental.pallas import tpu as pltpu
from jax.sharding import PartitionSpec as P

F32 = jnp.float32
BF16 = jnp.bfloat16
MESH = pl.DeviceIdType.MESH
HEAD = 32
LOG2E = math.log2(math.e)
NN = (((1,), (0,)), ((), ()))
NT = (((1,), (1,)), ((), ()))


def split(a):
    high = a.astype(BF16)
    return high, (a - high.astype(F32)).astype(BF16)


def dot(a, b, dims=NN):
    return lax.dot_general(a, b, dims, preferred_element_type=F32)


def dot3(a, b, dims=NN):
    rows = a[0].shape[0]
    both = dot(jnp.concatenate(a, axis=0), b[0], dims)
    return both[:rows] + (both[rows:] + dot(a[0], b[1], dims))


def normed(rows):
    center = rows - jnp.mean(rows, axis=-1, keepdims=True)
    spread = jnp.mean(center * center, axis=-1, keepdims=True)
    return center * lax.rsqrt(spread + 1e-05)


def merge_halves(a, b):
    upper = lax.broadcasted_iota(jnp.int32, a.shape, a.ndim - 2) < 4
    first = jnp.where(upper, a, pltpu.roll(b, 4, axis=b.ndim - 2))
    second = jnp.where(upper, pltpu.roll(a, 4, axis=a.ndim - 2), b)
    return first, second


def lane_iota(shape):
    return lax.broadcasted_iota(jnp.int32, shape, len(shape) - 1)


def drain(ref, sem):
    pltpu.make_async_copy(ref, ref, sem).wait()


def signal(sem, device):
    pl.semaphore_signal(sem, inc=1, device_id=device, device_id_type=MESH)


def send(src, dst, send_sem, recv_sem, device):
    pltpu.make_async_remote_copy(
        src_ref=src, dst_ref=dst, send_sem=send_sem, recv_sem=recv_sem,
        device_id=device, device_id_type=MESH,
    ).start()


def kernel(
    x_in, bias_ref, ids_ref, offset_ref, weight_ref, final_in_ref, live_ref, tensor_ref,
    vertical_in, final_in, expand_in, shrink_in, couple_in,
    revised_hbm, out_hbm,
    bias_all, xs, xr, os, og, finals, join_h, join_l, wide_h, wide_l, qs, ks, vs, gates, ids_col, chunk_bias,
    msa, proj, attended, units,
    left_own, right_own, left_all, right_all, outer_h, outer_l, couple_h, couple_l,
    vertical_h, vertical_l, last_h, last_l, expand_h, expand_l, shrink_h, shrink_l,
    bias_send, bias_recv, x_send, x_recv, o_send, o_recv, final_send, final_recv,
    left_send, left_recv, right_send, right_recv, near_z, near_x, near_y,
    vertical_ref, final_ref, expand_ref, shrink_ref, couple_ref, fetch,
    x_ref, x_fetch, revised_ref, out_ref, out_copy,
):
    dap = lax.axis_index("dap")
    grp = lax.axis_index("grp")
    y, x, z = dap // 16, lax.rem(dap // 4, 4), lax.rem(dap, 4)
    x_at = [lax.rem(x + i, 4) for i in range(4)]
    z_at = [lax.rem(z + i, 4) for i in range(4)]

    def along_x(i):
        return y * 16 + x_at[i % 4] * 4 + z, grp

    def along_z(i):
        return y * 16 + x * 4 + z_at[i % 4], grp

    across_y = ((1 - y) * 16 + x * 4 + z, grp)

    barrier = pltpu.get_barrier_semaphore()
    for i in range(1, 4):
        signal(barrier, along_x(i))
        signal(barrier, along_z(i))
        signal(barrier, (dap, lax.rem(grp + i, 4)))
    signal(barrier, across_y)

    late = (
        (vertical_in, vertical_ref), (final_in, final_ref), (expand_in, expand_ref),
        (shrink_in, shrink_ref), (couple_in, couple_ref),
    )
    for s in range(4):
        pltpu.make_async_copy(x_in.at[s], x_ref.at[s], x_fetch.at[s]).start()
    for i, (src, dst) in enumerate(late):
        pltpu.make_async_copy(src, dst, fetch.at[i]).start()

    zero = jnp.zeros((64, 256), F32)
    q_w = weight_ref[0] * (LOG2E / math.sqrt(HEAD))
    k_w, v_w, g_w = weight_ref[1], weight_ref[2], weight_ref[3]
    for at, parts in ((0, (q_w, q_w, q_w, zero)), (256, (k_w, k_w, k_w, zero)), (512, (v_w, v_w, g_w, g_w))):
        high, low = split(jnp.transpose(jnp.concatenate(parts, axis=0)))
        wide_h[:, at:at + 256] = high
        wide_l[:, at:at + 256] = low
    pl.semaphore_wait(barrier, 10)

    def unit(p, i, j, h=None):
        a, b = (x_at[j % 4], z_at[i % 4]) if p == 0 else (x_at[i % 4], z_at[j % 4])
        return bias_all.at[p, a, b] if h is None else bias_all.at[p, a, b, h]

    def line(p, j, h):
        return bias_all.at[0, x_at[j % 4], :, h] if p == 0 else bias_all.at[1, :, z_at[j % 4], h]

    def first_axis(p, i):
        return along_z(i) if p == 0 else along_x(i)

    def second_axis(p, i):
        return along_x(i) if p == 0 else along_z(i)

    steps = ((0, 1), (1, -1))
    own = bias_all.at[y, x, z]
    send(bias_ref, own, bias_send, bias_recv.at[0], across_y)
    pltpu.make_async_copy(bias_ref, own, bias_recv.at[21]).start()
    for i in range(1, 4):
        signal(near_z, along_z(i))
    drain(bias_ref, bias_recv.at[21])

    def own_path(act):
        for p in range(2):
            @pl.when(y == p)
            def _():
                act(p)

    def other_path(act):
        for p in range(2):
            @pl.when(y == 1 - p)
            def _():
                act(p)

    def spread(p):
        for i in (1, 3, 2):
            send(unit(p, 0, 0), unit(p, 0, 0), bias_send, bias_recv.at[1 + 10 * p], first_axis(p, i))

    def spread_line(p):
        drain(bias_all.at[0, 0, 0:3], bias_recv.at[1 + 10 * p])
        for k, sign in steps:
            send(line(p, 0, k), line(p, 0, k), bias_send, bias_recv.at[5 + 10 * p + k], second_axis(p, sign))
        for k, sign in steps:
            send(line(p, 0, 1 - k), line(p, 0, 1 - k), bias_send,
                 bias_recv.at[7 + 10 * p + k], second_axis(p, sign))

    def forward_line(p):
        for k, sign in steps:
            drain(line(0, 0, 0), bias_recv.at[5 + 10 * p + k])
            send(line(p, -sign, k), line(p, -sign, k), bias_send,
                 bias_recv.at[9 + 10 * p + k], second_axis(p, sign))

    own_path(spread)

    final_to = finals.at[pl.ds(pl.multiple_of(grp * 64, 64), 64)]
    pltpu.make_async_copy(final_in_ref, final_to, final_recv).start()
    for k in range(1, 4):
        send(final_in_ref, final_to, final_send, final_recv, (dap, lax.rem(grp + k, 4)))

    def project(s):
        pltpu.make_async_copy(x_in.at[s], x_ref.at[s], x_fetch.at[s]).wait()
        rows = split(normed(x_ref[s].reshape(512, 256)))
        out = dot3(rows, (wide_h[...], wide_l[...]))
        lane = lane_iota((512, 256))
        head = lax.rem(lane, 64) // HEAD
        q_hi, q_lo = split(out[:, 0:256])
        q = jnp.where((lane >= 64) & (lane < 128), q_lo.astype(F32), q_hi.astype(F32))
        k_hi, k_lo = split(out[:, 256:512])
        k = jnp.where((lane >= 128) & (lane < 192), k_lo.astype(F32), k_hi.astype(F32))
        ks[s] = k.astype(BF16)
        lane_v = lane_iota((512, 128))
        head_v = lax.rem(lane_v, 64) // HEAD
        v_hi, v_lo = split(out[:, 512:640])
        v = jnp.where(lane_v >= 64, v_lo.astype(F32), v_hi.astype(F32))
        for h in range(2):
            qs[s, h] = jnp.where(head == h, q, 0.0).astype(BF16).reshape(32, 16, 256)
            vs[s, pl.ds(512 * h, 512), 0:128] = jnp.where(head_v == h, v, 0.0).astype(BF16)
            vs[s, pl.ds(512 * h, 512), 128:256] = jnp.where(head_v == h, 1.0, 0.0).astype(BF16)
        gates[s] = jax.nn.sigmoid(out[:, 640:768]).reshape(32, 16, 128)

    def project_and(s, carry):
        project(s)

        @pl.when(s == 0)
        def _():
            pl.semaphore_wait(near_z, 3)
            for i in range(1, 4):
                signal(near_x, along_x(i))
            drain(bias_ref, bias_recv.at[0])
            other_path(spread)

        @pl.when(s == 1)
        def _():
            own_path(spread_line)
            pl.semaphore_wait(near_x, 3)
            signal(near_y, across_y)

        @pl.when(s == 2)
        def _():
            other_path(spread_line)

        return carry

    lax.fori_loop(0, 4, project_and, 0)

    half = lax.rem(grp, 2)
    for s2 in range(2):
        first, second = merge_halves(x_ref[2 * s2, :, grp // 2], x_ref[2 * s2 + 1, :, grp // 2])
        xs[:, s2] = jnp.where(half == 0, first, second)
    for i in range(4):
        block = jnp.broadcast_to(ids_ref[:, 128 * i:128 * i + 128].astype(F32), (128, 128))
        ids_col[8 * i:8 * i + 8] = jnp.transpose(block).reshape(8, 16, 128)
    pl.semaphore_wait(near_y, 1)

    drain(finals, final_recv)
    gap = jnp.zeros((64, 256), F32)
    for s2 in range(2):
        pieces = []
        for g in range(4):
            piece = finals[64 * g:64 * g + 64, :]
            pieces += [piece, gap] if s2 == 0 else [gap, piece]
        join_h[s2], join_l[s2] = split(jnp.concatenate(pieces, axis=0))

    for i, (src, dst) in enumerate(late):
        pltpu.make_async_copy(src, dst, fetch.at[i]).wait()

    for m in range(4):
        w = vertical_ref[m]
        if m == 0:
            w = w * (LOG2E / math.sqrt(HEAD))
        vertical_h[m], vertical_l[m] = split(w)
    last_h[...], last_l[...] = split(final_ref[...])
    expand_h[...], expand_l[...] = split(expand_ref[...])
    shrink_h[...], shrink_l[...] = split(shrink_ref[...])
    for odd in range(2):
        for b in range(4):
            rows = jnp.concatenate(
                [couple_ref[pl.ds(2 * (4 * b + i) + odd, 32, stride=32), :] for i in range(4)], axis=0)
            at = 512 * odd + 128 * b
            couple_h[:, at:at + 128], couple_l[:, at:at + 128] = split(jnp.transpose(rows))

    def turned(step):
        turn = step + step // 2 - 2 * (step // 3)
        return lax.rem(x + turn, 4), lax.rem(z + turn, 4)

    def settle(step):
        x_now, z_now = turned(step)
        drain(og.at[:, 0, 0:2], o_recv.at[step])
        rows = split(jnp.concatenate(
            [jnp.concatenate([og[g, 0, x_now].reshape(32, 128), og[g, 1, :, z_now].reshape(32, 128)], axis=0)
             for g in range(4)], axis=-1))
        for s2 in range(2):
            out = dot3(rows, (join_h[s2], join_l[s2])).reshape(8, 8, 256)
            for i in range(4):
                xs[4 * x_now + i, s2] += out[i]
                xs[16 + 4 * i + z_now, s2] += out[4 + i]

        def send_x(k, carry):
            low_half = 1 - k // 4
            place = lax.rem(k + x + z, 4)
            to = low_half * (4 * x_now + place) + (1 - low_half) * (16 + 4 * place + z_now)

            @pl.when(to == dap)
            def _():
                pltpu.make_async_copy(xs.at[to], xr.at[:, dap], x_recv).start()

            @pl.when(to != dap)
            def _():
                send(xs.at[to], xr.at[:, dap], x_send, x_recv, (to, grp))

            return carry

        lax.fori_loop(0, 8, send_x, 0)

    def attend(step, carry):
        x_now, z_now = turned(step)

        @pl.when(step == 1)
        def _():
            own_path(forward_line)
            other_path(forward_line)
            for p in range(2):
                drain(line(0, 0, 0), bias_recv.at[7 + 10 * p + 1])

        @pl.when(step == 2)
        def _():
            for p in range(2):
                drain(line(0, 0, 0), bias_recv.at[7 + 10 * p])

        @pl.when(step == 3)
        def _():
            for p in range(2):
                for k in range(2):
                    drain(line(0, 0, 0), bias_recv.at[9 + 10 * p + k])

        def rows_of(ref, *lead):
            shape = ref.shape[-2:]
            upper = ref[(*lead, pl.ds(4 * x_now, 4))].reshape(64, shape[-1])
            return jnp.concatenate([upper] + [ref[(*lead, 16 + 4 * i + z_now)] for i in range(4)], axis=0)

        own_ids = rows_of(ids_col)
        same = (jnp.concatenate([own_ids] * 4, axis=-1) == ids_ref[...].astype(F32)).astype(F32)
        for h in range(2):
            here = jnp.concatenate(
                [bias_all[0, x_now, :, h].reshape(64, 512), bias_all[1, :, z_now, h].reshape(64, 512)], axis=0)
            chunk_bias[h] = (here + offset_ref[h] * same) * LOG2E
        outs = []
        for s in range(4):
            highs, lows = [], []
            both = dot(jnp.concatenate([rows_of(qs, s, h) for h in range(2)], axis=0), ks[s], NT)
            for h in range(2):
                logits = both[128 * h:128 * h + 128] + chunk_bias[h]
                weights = jnp.exp2(logits - jnp.max(logits, axis=-1, keepdims=True))
                high, low = split(weights)
                highs.append(high)
                lows.append(low)
            v = vs[s]
            total = dot(jnp.concatenate([jnp.concatenate(a, axis=-1) for a in (highs, lows)], axis=0), v)
            total = total[0:128] + total[128:256]
            top = total[:, 0:128]
            top = top + pltpu.roll(top, 64, axis=1)
            outs.append(top / total[:, 128:256] * rows_of(gates, s))
        left_lanes = lane_iota((128, 128)) < 64
        pair = [jnp.where(left_lanes, outs[s1], outs[2 + s1]).reshape(16, 8, 128) for s1 in range(2)]
        for side, tiles in enumerate(merge_halves(*pair)):
            tiles = tiles.reshape(8, 2, 8, 128)
            for t in range(2):
                os[2 * t + side, 0, x_now] = tiles[0:4, t]
                for i in range(4):
                    os[2 * t + side, 1, i, z_now] = tiles[4 + i, t]
        pltpu.make_async_copy(os.at[grp, 0, x_now], og.at[grp, 0, x_now], o_recv.at[step]).start()
        pltpu.make_async_copy(os.at[grp, 1, :, z_now], og.at[grp, 1, :, z_now], o_recv.at[step]).start()
        for k in (2, 1, 3):
            to = lax.rem(grp + k, 4)
            send(os.at[to, 0, x_now], og.at[grp, 0, x_now], o_send, o_recv.at[step], (dap, to))
            send(os.at[to, 1, :, z_now], og.at[grp, 1, :, z_now], o_send, o_recv.at[step], (dap, to))

        @pl.when(step > 0)
        def _():
            settle(step - 1)

        return carry

    lax.fori_loop(0, 4, attend, 0)
    settle(3)

    drain(xr, x_recv)

    for s2 in range(2):
        stack = xr[s2].reshape(256, 256)
        for part in range(2):
            msa[part, pl.ds(256 * s2, 256), :] = stack[:, 128 * part:128 * part + 128]

    rows = split(normed(jnp.concatenate([msa[0], msa[1]], axis=-1)))
    for m in range(4):
        out = dot3(rows, (vertical_h[m], vertical_l[m]))
        for part in range(2):
            proj[2 * m + part] = out[:, 128 * part:128 * part + 128]

    at = lax.broadcasted_iota(jnp.int32, (128, 128), 0)
    to = lax.broadcasted_iota(jnp.int32, (128, 128), 1)
    order = (at == 4 * lax.rem(to // 2, 32) + 2 * (to // 64) + lax.rem(to, 2)).astype(BF16)
    live = dot(live_ref[...].astype(F32).astype(BF16), order)
    live_total = jnp.sum(live)
    mask = (live - 1.0) * (1e9 * LOG2E)

    lane = lane_iota((128, 128))
    def attend_column(r):
        for part in range(2):
            q, k, v, g = (proj[2 * m + part, pl.ds(r, 128, stride=4), :] for m in range(4))
            q_h, q_l = split(q)
            k_h, k_l = split(k)
            v_h, v_l = split(v)
            keys = jnp.concatenate([k_h, k_h, k_l], axis=-1)
            wide_q, wide_v = [], []
            for h in range(4):
                mine = lane // HEAD == h
                none = jnp.zeros((128, 128), BF16)
                qm_h, qm_l = jnp.where(mine, q_h, none), jnp.where(mine, q_l, none)
                wide_q.append(jnp.concatenate([qm_h, qm_l, qm_h], axis=-1))
                wide_v.append(jnp.concatenate(
                    [jnp.where(mine, v_h, none), jnp.where(mine, v_l, none), mine.astype(BF16)], axis=-1))
            logits = dot(jnp.concatenate(wide_q, axis=0), keys, NT) + mask
            weights = jnp.exp2(logits - jnp.max(logits, axis=-1, keepdims=True))
            high, low = split(weights)
            values = jnp.concatenate(wide_v, axis=0)

            def heads_in_lanes(a):
                return jnp.concatenate([a[128 * h:128 * h + 128] for h in range(4)], axis=-1)

            total = dot(jnp.concatenate([heads_in_lanes(high), heads_in_lanes(low)], axis=0), values)
            total = total[0:128] + total[128:256]
            out = (total[:, 0:128] + total[:, 128:256]) / total[:, 256:384]
            attended[part, pl.ds(128 * (r % 2), 128), :] = out * jax.nn.sigmoid(g)

    narrow = split(tensor_ref[...].reshape(64, 256))

    def finish_column(turn):
        here = [pl.ds(2 * turn + r2, 128, stride=4) for r2 in range(2)]
        before = jnp.concatenate(
            [jnp.concatenate([msa[part, rows, :] for rows in here], axis=0) for part in range(2)], axis=-1)
        gated = split(jnp.concatenate([attended[0], attended[1]], axis=-1))
        current = before + dot3(gated, (last_h[...], last_l[...]))
        hidden = jnp.maximum(dot3(split(normed(current)), (expand_h[...], expand_l[...])), 0.0)
        revised = current + dot3(split(hidden), (shrink_h[...], shrink_l[...]))
        unit_high, unit_low = split(normed(revised))
        for r2 in range(2):
            mine = slice(128 * r2, 128 * r2 + 128)
            for part in range(2):
                units[part, here[r2], :] = revised[mine, 128 * part:128 * part + 128]
            both = dot3(narrow, (unit_high[mine], unit_low[mine]), NT)
            left_own[pl.ds(64 * turn + 32 * r2, 32), :] = both[0:32] * (live / live_total)
            right_own[turn, pl.ds(32 * r2, 32), :] = both[32:64] * live

    pass_grp = 2 * y + x // 2
    near = lax.rem(x, 2)
    passing = lax.rem(grp, 2) == x // 2
    to_same = (y * 16 + lax.rem(x + 1 + 2 * near, 4) * 4 + z, grp)
    to_other = (y * 16 + lax.rem(x + 3 + 2 * near, 4) * 4 + z, grp)
    top, low = pl.ds(0, 32), pl.ds(32, 32)

    def right_begin(turn):
        slot = right_all.at[turn, near, z, grp]
        for y_to in range(2):
            mine = (y == y_to) & (grp == pass_grp)

            @pl.when(mine)
            def _():
                pltpu.make_async_copy(right_own.at[turn], slot, right_recv.at[turn, 0]).start()

            @pl.when(jnp.logical_not(mine))
            def _():
                send(right_own.at[turn], slot, right_send, right_recv.at[turn, 0],
                     (y_to * 16 + x * 4 + z, pass_grp))

    def right_first(turn):
        @pl.when(passing)
        def _():
            drain(right_all.at[turn, near, z], right_recv.at[turn, 0])
            along = right_all.at[turn, near, z, :, top]
            for i in (1, 3, 2):
                send(along, along, right_send, right_recv.at[turn, 1], along_z(i))
            along = right_all.at[turn, near, z, :, low]
            for to in (to_same, to_other, along_x(2)):
                send(along, along, right_send, right_recv.at[turn, 2], to)

    def x_column(turn, row, part=None):
        which = pl.ds(0, 4) if part is None else pl.ds(2 * part, 2)
        return right_all.at[turn, row, :, which, top]

    def z_column(turn, i, part=None):
        which = pl.ds(0, 2) if part is None else part
        return right_all.at[turn, which, z_at[i % 4], :, low]

    def right_second(turn):
        @pl.when(passing)
        def _():
            drain(right_all.at[turn, near, 0:3, :, top], right_recv.at[turn, 1])
            for to in (to_same, to_other):
                send(x_column(turn, near), x_column(turn, near), right_send, right_recv.at[turn, 3], to)
            drain(right_all.at[turn, 0, z, :, low], right_recv.at[turn, 2])

        @pl.when(jnp.logical_not(passing))
        def _():
            drain(right_all.at[turn, :, z, :, low], right_recv.at[turn, 2])

        for k, sign in steps:
            send(z_column(turn, 0), z_column(turn, 0), right_send, right_recv.at[turn, 6 + k], along_z(sign))

    def right_third(turn):
        drain(x_column(turn, 0), right_recv.at[turn, 3])

        @pl.when(passing)
        def _():
            piece = x_column(turn, 1 - near, 0)
            send(piece, piece, right_send, right_recv.at[turn, 4], to_other)

        @pl.when(jnp.logical_not(passing))
        def _():
            piece = x_column(turn, 1 - near, 1)
            send(piece, piece, right_send, right_recv.at[turn, 5], to_same)

        for k, sign in steps:
            drain(z_column(turn, 0), right_recv.at[turn, 6 + k])
            piece = z_column(turn, -sign, k)
            send(piece, piece, right_send, right_recv.at[turn, 8 + k], along_z(sign))

    def right_end(turn):
        @pl.when(jnp.logical_not(passing))
        def _():
            for k in range(2):
                drain(x_column(turn, 0, 0), right_recv.at[turn, 4 + k])
        for k in range(2):
            drain(z_column(turn, 0, 0), right_recv.at[turn, 8 + k])

    def right_sent(turn):
        for y_to in range(2):
            @pl.when(jnp.logical_not((y == y_to) & (grp == pass_grp)))
            def _():
                drain(right_own.at[turn], right_send)

        @pl.when(passing)
        def _():
            for _ in range(2):
                drain(right_all.at[turn, 0, 0:3, :, top], right_send)
                drain(x_column(turn, 0), right_send)

        drain(x_column(turn, 0, 0), right_send)
        for k in range(2):
            drain(z_column(turn, 0), right_send)
            drain(z_column(turn, 0, 0), right_send)

    lane_low = lane_iota((256, 128)) < 64

    def outer(turn):
        left_h, left_l = split(left_all[...].reshape(8, 2, 32, 128))
        left_wide = [
            jnp.concatenate([a[:, odd].reshape(256, 128) for a in (left_h, left_l, left_h)], axis=-1)
            for odd in range(2)
        ]
        right_flat = right_all.reshape(2 * 32 * 64, 128)

        def step(quad, carry):
            wide = []
            for e in range(4):
                high, low = split(jnp.concatenate(
                    [right_flat[pl.ds(2048 * turn + 32 * r2 + 4 * quad + e, 32, stride=64), :] for r2 in range(2)],
                    axis=0))
                wide.append(jnp.concatenate([high, high, low], axis=-1))
            even = dot(left_wide[0], jnp.concatenate(wide, axis=0), NT)
            odd = dot(left_wide[1], jnp.concatenate([wide[1], wide[0], wide[3], wide[2]], axis=0), NT)
            for m in range(2):
                lanes = slice(128 * m, 128 * m + 128)
                a, b = even[:, lanes], odd[:, lanes]
                for side, mixed in enumerate((jnp.where(lane_low, a, b), jnp.where(lane_low, b, a))):
                    high, low = split(mixed)
                    at = pl.ds(pl.multiple_of(512 * side + 64 * quad + 32 * m, 32), 32)
                    for i in range(8):
                        cols = slice(128 * (i % 2), 128 * (i % 2) + 128)
                        outer_h[i // 2, at, cols] = high[32 * i:32 * i + 32]
                        outer_l[i // 2, at, cols] = low[32 * i:32 * i + 32]
            return carry

        lax.fori_loop(0, 8, step, 0, unroll=2)

    def finish(turn):
        def step(i4, carry):
            total = []
            for side in range(2):
                at = slice(512 * side, 512 * side + 512)
                total.append(dot3((couple_h[:, at], couple_l[:, at]), (outer_h[i4, at, :], outer_l[i4, at, :])))
            for i2 in range(2):
                lanes = slice(128 * i2, 128 * i2 + 128)
                block = jnp.transpose(total[0][:, lanes] + pltpu.roll(total[1][:, lanes], 64, axis=1))
                for i1 in range(2):
                    for r2 in range(2):
                        at = 64 * i1 + 32 * r2
                        out_ref[4 * i4 + 2 * i2 + i1, pl.ds(2 * turn + r2, 32, stride=4), :] = block[at:at + 32]
            if turn == 1:
                four = pl.ds(4 * i4, 4)
                pltpu.make_async_copy(out_ref.at[four], out_hbm.at[four], out_copy.at[i4]).start()
            return carry

        lax.fori_loop(0, 4, step, 0, unroll=2)

    attend_column(0)
    attend_column(1)
    finish_column(0)
    right_begin(0)
    attend_column(2)
    attend_column(3)
    right_first(0)
    finish_column(1)
    right_begin(1)
    right_second(0)
    right_first(1)
    left_to = left_all.at[pl.ds(pl.multiple_of(grp * 128, 128), 128)]
    pltpu.make_async_copy(left_own, left_to, left_recv).start()
    for k in range(1, 4):
        send(left_own, left_to, left_send, left_recv, (dap, lax.rem(grp + k, 4)))
    right_third(0)
    right_second(1)
    for s2 in range(2):
        for part in range(2):
            tiles = units[part, pl.ds(256 * s2, 256), :].reshape(32, 8, 128)
            for s1 in range(2):
                revised_ref[:, s2, s1, :, 128 * part:128 * part + 128] = tiles[:, 4 * s1:4 * s1 + 4]
    pltpu.make_async_copy(revised_ref, revised_hbm, out_copy.at[4]).start()
    right_end(0)
    drain(left_all, left_recv)
    outer(0)
    right_third(1)
    finish(0)
    right_end(1)
    outer(1)
    finish(1)

    for i in range(4):
        four = pl.ds(4 * i, 4)
        pltpu.make_async_copy(out_ref.at[four], out_hbm.at[four], out_copy.at[i]).wait()
    pltpu.make_async_copy(revised_ref, revised_hbm, out_copy.at[4]).wait()
    for _ in range(31):
        drain(bias_ref, bias_send)
    drain(xs.at[0:31], x_send)
    drain(og.at[0:3], o_send)
    drain(finals.at[0:192], final_send)
    drain(left_all.at[0:384], left_send)
    for turn in range(2):
        right_sent(turn)


def emit_kernel(revised_in, pair_in, revised_out, pair_out, revised, pair, sems):
    copies = [(revised_in, revised, revised_out)]
    for i in range(4):
        four = pl.ds(4 * i, 4)
        copies.append((pair_in.at[four], pair.at[four], pair_out.at[four]))
    for i, (src, here, dst) in enumerate(copies):
        pltpu.make_async_copy(src, here, sems.at[0, i]).start()
    for i, (src, here, dst) in enumerate(copies):
        pltpu.make_async_copy(src, here, sems.at[0, i]).wait()
        pltpu.make_async_copy(here, dst, sems.at[1, i]).start()
    for i, (src, here, dst) in enumerate(copies):
        pltpu.make_async_copy(here, dst, sems.at[1, i]).wait()


VM = pl.BlockSpec(memory_space=pltpu.VMEM)
SM = pl.BlockSpec(memory_space=pltpu.SMEM)
ANY = pl.BlockSpec(memory_space=pl.ANY)
LIMIT = 58 * 1024 * 1024


def body(
    homolog_stack,
    couple_score_offset,
    strand_identity,
    strand_score_offset,
    homolog_presence,
    horizontal_matrix,
    horizontal_final_matrix,
    vertical_matrix,
    vertical_final_matrix,
    expand_matrix,
    shrink_matrix,
    tensor_matrix,
    couple_matrix,
):
    dma = pltpu.SemaphoreType.DMA
    regular = pltpu.SemaphoreType.REGULAR
    revised, pair = pl.pallas_call(
        kernel,
        out_shape=[
            jax.ShapeDtypeStruct((32, 2, 2, 4, 256), F32),
            jax.ShapeDtypeStruct((16, 128, 128), F32),
        ],
        in_specs=[ANY, VM, VM, SM] + [VM] * 4 + [ANY] * 5,
        out_specs=[ANY, ANY],
        scratch_shapes=[
            pltpu.VMEM((2, 4, 4, 2, 16, 512), F32),
            pltpu.VMEM((32, 2, 8, 256), F32),
            pltpu.VMEM((2, 32, 8, 256), F32),
            pltpu.VMEM((4, 2, 4, 4, 8, 128), F32),
            pltpu.VMEM((4, 2, 4, 4, 8, 128), F32),
            pltpu.VMEM((256, 256), F32),
            pltpu.VMEM((2, 512, 256), BF16),
            pltpu.VMEM((2, 512, 256), BF16),
            pltpu.VMEM((256, 768), BF16),
            pltpu.VMEM((256, 768), BF16),
            pltpu.VMEM((4, 2, 32, 16, 256), BF16),
            pltpu.VMEM((4, 512, 256), BF16),
            pltpu.VMEM((4, 1024, 256), BF16),
            pltpu.VMEM((4, 32, 16, 128), F32),
            pltpu.VMEM((32, 16, 128), F32),
            pltpu.VMEM((2, 128, 512), F32),
            pltpu.VMEM((2, 512, 128), F32),
            pltpu.VMEM((8, 512, 128), F32),
            pltpu.VMEM((2, 256, 128), F32),
            pltpu.VMEM((2, 512, 128), F32),
            pltpu.VMEM((128, 128), F32),
            pltpu.VMEM((2, 64, 128), F32),
            pltpu.VMEM((512, 128), F32),
            pltpu.VMEM((2, 2, 4, 4, 64, 128), F32),
            pltpu.VMEM((4, 1024, 256), BF16),
            pltpu.VMEM((4, 1024, 256), BF16),
            pltpu.VMEM((128, 1024), BF16),
            pltpu.VMEM((128, 1024), BF16),
            pltpu.VMEM((4, 256, 256), BF16),
            pltpu.VMEM((4, 256, 256), BF16),
            pltpu.VMEM((256, 256), BF16),
            pltpu.VMEM((256, 256), BF16),
            pltpu.VMEM((256, 1024), BF16),
            pltpu.VMEM((256, 1024), BF16),
            pltpu.VMEM((1024, 256), BF16),
            pltpu.VMEM((1024, 256), BF16),
            dma, dma((22,)), dma, dma, dma, dma((4,)), dma, dma,
            dma, dma, dma, dma((2, 10)), regular, regular, regular,
            pltpu.VMEM((4, 256, 256), F32),
            pltpu.VMEM((256, 256), F32),
            pltpu.VMEM((256, 1024), F32),
            pltpu.VMEM((1024, 256), F32),
            pltpu.VMEM((1024, 128), F32),
            dma((5,)),
            pltpu.VMEM((4, 32, 2, 8, 256), F32),
            dma((4,)),
            pltpu.VMEM((32, 2, 2, 4, 256), F32),
            pltpu.VMEM((16, 128, 128), F32),
            dma((5,)),
        ],
        compiler_params=pltpu.CompilerParams(
            collective_id=0, has_side_effects=True, vmem_limit_bytes=LIMIT
        ),
        name="msa_block",
    )(
        homolog_stack.reshape(4, 32, 2, 8, 256),
        couple_score_offset,
        strand_identity.reshape(1, 512),
        strand_score_offset,
        jnp.swapaxes(horizontal_matrix, 1, 2),
        horizontal_final_matrix,
        homolog_presence.reshape(1, 128),
        jnp.swapaxes(tensor_matrix, 1, 2),
        vertical_matrix,
        vertical_final_matrix,
        expand_matrix,
        shrink_matrix,
        couple_matrix,
    )
    revised, pair = pl.pallas_call(
        emit_kernel,
        out_shape=[
            jax.ShapeDtypeStruct((32, 2, 2, 4, 256), F32),
            jax.ShapeDtypeStruct((16, 128, 128), F32),
        ],
        in_specs=[ANY, ANY],
        out_specs=[ANY, ANY],
        scratch_shapes=[
            pltpu.VMEM((32, 2, 2, 4, 256), F32), pltpu.VMEM((16, 128, 128), F32), dma((2, 5)),
        ],
        name="emit",
    )(revised, pair)
    return revised.reshape(128, 4, 256), pair


def solution(mesh):
    return jax.shard_map(
        body,
        mesh=mesh,
        in_specs=(
            P("dap", None, None),
            P("grp", "dap", None),
            P(),
            P("grp"),
            P(),
            P(None, None, "grp"),
            P("grp", None),
            P(),
            P(),
            P(),
            P(),
            P(),
            P(),
        ),
        out_specs=(P(None, ("dap", "grp"), None), P("dap", "grp", None)),
        check_vma=False,
    )
```

```python
import functools
import math

import jax
import jax.numpy as jnp
from jax import lax
from jax.experimental import pallas as pl
from jax.experimental.pallas import tpu as pltpu
from jax.sharding import PartitionSpec as P

F32 = jnp.float32
BF16 = jnp.bfloat16
MESH = pl.DeviceIdType.MESH
HEAD = 32
LOG2E = math.log2(math.e)
NN = (((1,), (0,)), ((), ()))
NT = (((1,), (1,)), ((), ()))


def split(a):
    high = a.astype(BF16)
    return high, (a - high.astype(F32)).astype(BF16)


def dot(a, b, dims=NN):
    return lax.dot_general(a, b, dims, preferred_element_type=F32)


def dot3(a, b, dims=NN):
    rows = a[0].shape[0]
    both = dot(jnp.concatenate(a, axis=0), b[0], dims)
    return both[:rows] + (both[rows:] + dot(a[0], b[1], dims))


def normed(rows):
    center = rows - jnp.mean(rows, axis=-1, keepdims=True)
    spread = jnp.mean(center * center, axis=-1, keepdims=True)
    return center * lax.rsqrt(spread + 1e-05)


def merge_halves(a, b):
    upper = lax.broadcasted_iota(jnp.int32, a.shape, a.ndim - 2) < 4
    first = jnp.where(upper, a, pltpu.roll(b, 4, axis=b.ndim - 2))
    second = jnp.where(upper, pltpu.roll(a, 4, axis=a.ndim - 2), b)
    return first, second


def lane_iota(shape):
    return lax.broadcasted_iota(jnp.int32, shape, len(shape) - 1)


def drain(ref, sem):
    pltpu.make_async_copy(ref, ref, sem).wait()


def signal(sem, device):
    pl.semaphore_signal(sem, inc=1, device_id=device, device_id_type=MESH)


def send(src, dst, send_sem, recv_sem, device):
    pltpu.make_async_remote_copy(
        src_ref=src, dst_ref=dst, send_sem=send_sem, recv_sem=recv_sem,
        device_id=device, device_id_type=MESH,
    ).start()


def kernel(
    x_in, bias_ref, ids_ref, offset_ref, weight_ref, final_in_ref, live_ref, tensor_ref,
    vertical_in, final_in, expand_in, shrink_in, couple_in,
    revised_hbm, out_hbm,
    bias_all, xs, xr, os, og, finals, join_h, join_l, wide_h, wide_l, qs, ks, vs, gates, ids_col, chunk_bias,
    msa, proj, attended, units,
    left_own, right_own, left_all, right_all, outer_h, outer_l, couple_h, couple_l,
    vertical_h, vertical_l, last_h, last_l, expand_h, expand_l, shrink_h, shrink_l,
    bias_send, bias_recv, x_send, x_recv, o_send, o_recv, final_send, final_recv,
    left_send, left_recv, right_send, right_recv, near_z, near_x, near_y,
    vertical_ref, final_ref, expand_ref, shrink_ref, couple_ref, fetch,
    x_ref, x_fetch, revised_ref, out_ref, out_copy,
):
    dap = lax.axis_index("dap")
    grp = lax.axis_index("grp")
    y, x, z = dap // 16, lax.rem(dap // 4, 4), lax.rem(dap, 4)
    x_at = [lax.rem(x + i, 4) for i in range(4)]
    z_at = [lax.rem(z + i, 4) for i in range(4)]

    def along_x(i):
        return y * 16 + x_at[i % 4] * 4 + z, grp

    def along_z(i):
        return y * 16 + x * 4 + z_at[i % 4], grp

    across_y = ((1 - y) * 16 + x * 4 + z, grp)

    barrier = pltpu.get_barrier_semaphore()
    for i in range(1, 4):
        signal(barrier, along_x(i))
        signal(barrier, along_z(i))
        signal(barrier, (dap, lax.rem(grp + i, 4)))
    signal(barrier, across_y)

    late = (
        (vertical_in, vertical_ref), (final_in, final_ref), (expand_in, expand_ref),
        (shrink_in, shrink_ref), (couple_in, couple_ref),
    )
    for s in range(4):
        pltpu.make_async_copy(x_in.at[s], x_ref.at[s], x_fetch.at[s]).start()
    for i, (src, dst) in enumerate(late):
        pltpu.make_async_copy(src, dst, fetch.at[i]).start()

    zero = jnp.zeros((64, 256), F32)
    q_w = weight_ref[0] * (LOG2E / math.sqrt(HEAD))
    k_w, v_w, g_w = weight_ref[1], weight_ref[2], weight_ref[3]
    for at, parts in ((0, (q_w, q_w, q_w, zero)), (256, (k_w, k_w, k_w, zero)), (512, (v_w, v_w, g_w, g_w))):
        high, low = split(jnp.transpose(jnp.concatenate(parts, axis=0)))
        wide_h[:, at:at + 256] = high
        wide_l[:, at:at + 256] = low
    pl.semaphore_wait(barrier, 10)

    def unit(p, i, j, h=None):
        a, b = (x_at[j % 4], z_at[i % 4]) if p == 0 else (x_at[i % 4], z_at[j % 4])
        return bias_all.at[p, a, b] if h is None else bias_all.at[p, a, b, h]

    def line(p, j, h):
        return bias_all.at[0, x_at[j % 4], :, h] if p == 0 else bias_all.at[1, :, z_at[j % 4], h]

    def first_axis(p, i):
        return along_z(i) if p == 0 else along_x(i)

    def second_axis(p, i):
        return along_x(i) if p == 0 else along_z(i)

    steps = ((0, 1), (1, -1))
    own = bias_all.at[y, x, z]
    send(bias_ref, own, bias_send, bias_recv.at[0], across_y)
    pltpu.make_async_copy(bias_ref, own, bias_recv.at[21]).start()
    for i in range(1, 4):
        signal(near_z, along_z(i))
    drain(bias_ref, bias_recv.at[21])

    def own_path(act):
        for p in range(2):
            @pl.when(y == p)
            def _():
                act(p)

    def other_path(act):
        for p in range(2):
            @pl.when(y == 1 - p)
            def _():
                act(p)

    def spread(p):
        for i in (1, 3, 2):
            send(unit(p, 0, 0), unit(p, 0, 0), bias_send, bias_recv.at[1 + 10 * p], first_axis(p, i))

    def spread_line(p):
        drain(bias_all.at[0, 0, 0:3], bias_recv.at[1 + 10 * p])
        for k, sign in steps:
            send(line(p, 0, k), line(p, 0, k), bias_send, bias_recv.at[5 + 10 * p + k], second_axis(p, sign))
        for k, sign in steps:
            send(line(p, 0, 1 - k), line(p, 0, 1 - k), bias_send,
                 bias_recv.at[7 + 10 * p + k], second_axis(p, sign))

    def forward_line(p):
        for k, sign in steps:
            drain(line(0, 0, 0), bias_recv.at[5 + 10 * p + k])
            send(line(p, -sign, k), line(p, -sign, k), bias_send,
                 bias_recv.at[9 + 10 * p + k], second_axis(p, sign))

    own_path(spread)

    final_to = finals.at[pl.ds(pl.multiple_of(grp * 64, 64), 64)]
    pltpu.make_async_copy(final_in_ref, final_to, final_recv).start()
    for k in range(1, 4):
        send(final_in_ref, final_to, final_send, final_recv, (dap, lax.rem(grp + k, 4)))

    def project(s):
        pltpu.make_async_copy(x_in.at[s], x_ref.at[s], x_fetch.at[s]).wait()
        rows = split(normed(x_ref[s].reshape(512, 256)))
        out = dot3(rows, (wide_h[...], wide_l[...]))
        lane = lane_iota((512, 256))
        head = lax.rem(lane, 64) // HEAD
        q_hi, q_lo = split(out[:, 0:256])
        q = jnp.where((lane >= 64) & (lane < 128), q_lo.astype(F32), q_hi.astype(F32))
        k_hi, k_lo = split(out[:, 256:512])
        k = jnp.where((lane >= 128) & (lane < 192), k_lo.astype(F32), k_hi.astype(F32))
        ks[s] = k.astype(BF16)
        lane_v = lane_iota((512, 128))
        head_v = lax.rem(lane_v, 64) // HEAD
        v_hi, v_lo = split(out[:, 512:640])
        v = jnp.where(lane_v >= 64, v_lo.astype(F32), v_hi.astype(F32))
        for h in range(2):
            qs[s, h] = jnp.where(head == h, q, 0.0).astype(BF16).reshape(32, 16, 256)
            vs[s, pl.ds(512 * h, 512), 0:128] = jnp.where(head_v == h, v, 0.0).astype(BF16)
            vs[s, pl.ds(512 * h, 512), 128:256] = jnp.where(head_v == h, 1.0, 0.0).astype(BF16)
        gates[s] = jax.nn.sigmoid(out[:, 640:768]).reshape(32, 16, 128)

    def project_and(s, carry):
        project(s)

        @pl.when(s == 0)
        def _():
            pl.semaphore_wait(near_z, 3)
            for i in range(1, 4):
                signal(near_x, along_x(i))
            drain(bias_ref, bias_recv.at[0])
            other_path(spread)

        @pl.when(s == 1)
        def _():
            own_path(spread_line)
            pl.semaphore_wait(near_x, 3)
            signal(near_y, across_y)

        @pl.when(s == 2)
        def _():
            other_path(spread_line)

        return carry

    lax.fori_loop(0, 4, project_and, 0)

    half = lax.rem(grp, 2)
    for s2 in range(2):
        first, second = merge_halves(x_ref[2 * s2, :, grp // 2], x_ref[2 * s2 + 1, :, grp // 2])
        xs[:, s2] = jnp.where(half == 0, first, second)
    for i in range(4):
        block = jnp.broadcast_to(ids_ref[:, 128 * i:128 * i + 128].astype(F32), (128, 128))
        ids_col[8 * i:8 * i + 8] = jnp.transpose(block).reshape(8, 16, 128)
    pl.semaphore_wait(near_y, 1)

    drain(finals, final_recv)
    gap = jnp.zeros((64, 256), F32)
    for s2 in range(2):
        pieces = []
        for g in range(4):
            piece = finals[64 * g:64 * g + 64, :]
            pieces += [piece, gap] if s2 == 0 else [gap, piece]
        join_h[s2], join_l[s2] = split(jnp.concatenate(pieces, axis=0))

    for i, (src, dst) in enumerate(late):
        pltpu.make_async_copy(src, dst, fetch.at[i]).wait()

    for m in range(4):
        w = vertical_ref[m]
        if m == 0:
            w = w * (LOG2E / math.sqrt(HEAD))
        vertical_h[m], vertical_l[m] = split(w)
    last_h[...], last_l[...] = split(final_ref[...])
    expand_h[...], expand_l[...] = split(expand_ref[...])
    shrink_h[...], shrink_l[...] = split(shrink_ref[...])
    for odd in range(2):
        for b in range(4):
            rows = jnp.concatenate(
                [couple_ref[pl.ds(2 * (4 * b + i) + odd, 32, stride=32), :] for i in range(4)], axis=0)
            at = 512 * odd + 128 * b
            couple_h[:, at:at + 128], couple_l[:, at:at + 128] = split(jnp.transpose(rows))

    def turned(step):
        turn = step + step // 2 - 2 * (step // 3)
        return lax.rem(x + turn, 4), lax.rem(z + turn, 4)

    def settle(step):
        x_now, z_now = turned(step)
        drain(og.at[:, 0, 0:2], o_recv.at[step])
        rows = split(jnp.concatenate(
            [jnp.concatenate([og[g, 0, x_now].reshape(32, 128), og[g, 1, :, z_now].reshape(32, 128)], axis=0)
             for g in range(4)], axis=-1))
        for s2 in range(2):
            out = dot3(rows, (join_h[s2], join_l[s2])).reshape(8, 8, 256)
            for i in range(4):
                xs[4 * x_now + i, s2] += out[i]
                xs[16 + 4 * i + z_now, s2] += out[4 + i]

        def send_x(k, carry):
            low_half = 1 - k // 4
            place = lax.rem(k + x + z, 4)
            to = low_half * (4 * x_now + place) + (1 - low_half) * (16 + 4 * place + z_now)

            @pl.when(to == dap)
            def _():
                pltpu.make_async_copy(xs.at[to], xr.at[:, dap], x_recv).start()

            @pl.when(to != dap)
            def _():
                send(xs.at[to], xr.at[:, dap], x_send, x_recv, (to, grp))

            return carry

        lax.fori_loop(0, 8, send_x, 0)

    def attend(step, carry):
        x_now, z_now = turned(step)

        @pl.when(step == 1)
        def _():
            own_path(forward_line)
            other_path(forward_line)
            for p in range(2):
                drain(line(0, 0, 0), bias_recv.at[7 + 10 * p + 1])

        @pl.when(step == 2)
        def _():
            for p in range(2):
                drain(line(0, 0, 0), bias_recv.at[7 + 10 * p])

        @pl.when(step == 3)
        def _():
            for p in range(2):
                for k in range(2):
                    drain(line(0, 0, 0), bias_recv.at[9 + 10 * p + k])

        def rows_of(ref, *lead):
            shape = ref.shape[-2:]
            upper = ref[(*lead, pl.ds(4 * x_now, 4))].reshape(64, shape[-1])
            return jnp.concatenate([upper] + [ref[(*lead, 16 + 4 * i + z_now)] for i in range(4)], axis=0)

        own_ids = rows_of(ids_col)
        same = (jnp.concatenate([own_ids] * 4, axis=-1) == ids_ref[...].astype(F32)).astype(F32)
        for h in range(2):
            here = jnp.concatenate(
                [bias_all[0, x_now, :, h].reshape(64, 512), bias_all[1, :, z_now, h].reshape(64, 512)], axis=0)
            chunk_bias[h] = (here + offset_ref[h] * same) * LOG2E
        outs = []
        for s in range(4):
            highs, lows = [], []
            both = dot(jnp.concatenate([rows_of(qs, s, h) for h in range(2)], axis=0), ks[s], NT)
            for h in range(2):
                logits = both[128 * h:128 * h + 128] + chunk_bias[h]
                weights = jnp.exp2(logits - jnp.max(logits, axis=-1, keepdims=True))
                high, low = split(weights)
                highs.append(high)
                lows.append(low)
            v = vs[s]
            total = dot(jnp.concatenate([jnp.concatenate(a, axis=-1) for a in (highs, lows)], axis=0), v)
            total = total[0:128] + total[128:256]
            top = total[:, 0:128]
            top = top + pltpu.roll(top, 64, axis=1)
            outs.append(top / total[:, 128:256] * rows_of(gates, s))
        left_lanes = lane_iota((128, 128)) < 64
        pair = [jnp.where(left_lanes, outs[s1], outs[2 + s1]).reshape(16, 8, 128) for s1 in range(2)]
        for side, tiles in enumerate(merge_halves(*pair)):
            tiles = tiles.reshape(8, 2, 8, 128)
            for t in range(2):
                os[2 * t + side, 0, x_now] = tiles[0:4, t]
                for i in range(4):
                    os[2 * t + side, 1, i, z_now] = tiles[4 + i, t]
        pltpu.make_async_copy(os.at[grp, 0, x_now], og.at[grp, 0, x_now], o_recv.at[step]).start()
        pltpu.make_async_copy(os.at[grp, 1, :, z_now], og.at[grp, 1, :, z_now], o_recv.at[step]).start()
        for k in (2, 1, 3):
            to = lax.rem(grp + k, 4)
            send(os.at[to, 0, x_now], og.at[grp, 0, x_now], o_send, o_recv.at[step], (dap, to))
            send(os.at[to, 1, :, z_now], og.at[grp, 1, :, z_now], o_send, o_recv.at[step], (dap, to))

        @pl.when(step > 0)
        def _():
            settle(step - 1)

        return carry

    lax.fori_loop(0, 4, attend, 0)
    settle(3)

    drain(xr, x_recv)

    for s2 in range(2):
        stack = xr[s2].reshape(256, 256)
        for part in range(2):
            msa[part, pl.ds(256 * s2, 256), :] = stack[:, 128 * part:128 * part + 128]

    rows = split(normed(jnp.concatenate([msa[0], msa[1]], axis=-1)))
    for m in range(4):
        out = dot3(rows, (vertical_h[m], vertical_l[m]))
        for part in range(2):
            proj[2 * m + part] = out[:, 128 * part:128 * part + 128]

    at = lax.broadcasted_iota(jnp.int32, (128, 128), 0)
    to = lax.broadcasted_iota(jnp.int32, (128, 128), 1)
    order = (at == 4 * lax.rem(to // 2, 32) + 2 * (to // 64) + lax.rem(to, 2)).astype(BF16)
    live = dot(live_ref[...].astype(F32).astype(BF16), order)
    live_total = jnp.sum(live)
    mask = (live - 1.0) * (1e9 * LOG2E)

    lane = lane_iota((128, 128))
    def attend_column(r):
        for part in range(2):
            q, k, v, g = (proj[2 * m + part, pl.ds(r, 128, stride=4), :] for m in range(4))
            q_h, q_l = split(q)
            k_h, k_l = split(k)
            v_h, v_l = split(v)
            keys = jnp.concatenate([k_h, k_h, k_l], axis=-1)
            wide_q, wide_v = [], []
            for h in range(4):
                mine = lane // HEAD == h
                none = jnp.zeros((128, 128), BF16)
                qm_h, qm_l = jnp.where(mine, q_h, none), jnp.where(mine, q_l, none)
                wide_q.append(jnp.concatenate([qm_h, qm_l, qm_h], axis=-1))
                wide_v.append(jnp.concatenate(
                    [jnp.where(mine, v_h, none), jnp.where(mine, v_l, none), mine.astype(BF16)], axis=-1))
            logits = dot(jnp.concatenate(wide_q, axis=0), keys, NT) + mask
            weights = jnp.exp2(logits - jnp.max(logits, axis=-1, keepdims=True))
            high, low = split(weights)
            values = jnp.concatenate(wide_v, axis=0)

            def heads_in_lanes(a):
                return jnp.concatenate([a[128 * h:128 * h + 128] for h in range(4)], axis=-1)

            total = dot(jnp.concatenate([heads_in_lanes(high), heads_in_lanes(low)], axis=0), values)
            total = total[0:128] + total[128:256]
            out = (total[:, 0:128] + total[:, 128:256]) / total[:, 256:384]
            attended[part] = out * jax.nn.sigmoid(g)

    narrow = split(tensor_ref[...].reshape(64, 256))

    def finish_column(turn):
        here = pl.ds(turn, 128, stride=4)
        before = jnp.concatenate([msa[part, here, :] for part in range(2)], axis=-1)
        gated = split(jnp.concatenate([attended[0], attended[1]], axis=-1))
        current = before + dot3(gated, (last_h[...], last_l[...]))
        hidden = jnp.maximum(dot3(split(normed(current)), (expand_h[...], expand_l[...])), 0.0)
        revised = current + dot3(split(hidden), (shrink_h[...], shrink_l[...]))
        for part in range(2):
            units[part, here, :] = revised[:, 128 * part:128 * part + 128]
        both = dot3(narrow, split(normed(revised)), NT)
        left_own[pl.ds(32 * turn, 32), :] = both[0:32] * (live / live_total)
        right_own[turn] = both[32:64] * live

    pass_grp = 2 * y + x // 2
    near = lax.rem(x, 2)
    passing = lax.rem(grp, 2) == x // 2
    to_same = (y * 16 + lax.rem(x + 1 + 2 * near, 4) * 4 + z, grp)
    to_other = (y * 16 + lax.rem(x + 3 + 2 * near, 4) * 4 + z, grp)
    top, low = pl.ds(0, 16), pl.ds(16, 16)

    def right_begin(turn):
        slot = right_all.at[turn, near, z, grp]
        for y_to in range(2):
            mine = (y == y_to) & (grp == pass_grp)

            @pl.when(mine)
            def _():
                pltpu.make_async_copy(right_own.at[turn], slot, right_recv.at[turn, 0]).start()

            @pl.when(jnp.logical_not(mine))
            def _():
                send(right_own.at[turn], slot, right_send, right_recv.at[turn, 0],
                     (y_to * 16 + x * 4 + z, pass_grp))

    def right_first(turn):
        @pl.when(passing)
        def _():
            drain(right_all.at[turn, near, z], right_recv.at[turn, 0])
            along = right_all.at[turn, near, z, :, top]
            for i in (1, 3, 2):
                send(along, along, right_send, right_recv.at[turn, 1], along_z(i))
            along = right_all.at[turn, near, z, :, low]
            for to in (to_same, to_other, along_x(2)):
                send(along, along, right_send, right_recv.at[turn, 2], to)

    def x_column(turn, row, part=None):
        which = pl.ds(0, 4) if part is None else pl.ds(2 * part, 2)
        return right_all.at[turn, row, :, which, top]

    def z_column(turn, i, part=None):
        which = pl.ds(0, 2) if part is None else part
        return right_all.at[turn, which, z_at[i % 4], :, low]

    def right_second(turn):
        @pl.when(passing)
        def _():
            drain(right_all.at[turn, near, 0:3, :, top], right_recv.at[turn, 1])
            for to in (to_same, to_other):
                send(x_column(turn, near), x_column(turn, near), right_send, right_recv.at[turn, 3], to)
            drain(right_all.at[turn, 0, z, :, low], right_recv.at[turn, 2])

        @pl.when(jnp.logical_not(passing))
        def _():
            drain(right_all.at[turn, :, z, :, low], right_recv.at[turn, 2])

        for k, sign in steps:
            send(z_column(turn, 0), z_column(turn, 0), right_send, right_recv.at[turn, 6 + k], along_z(sign))

    def right_third(turn):
        drain(x_column(turn, 0), right_recv.at[turn, 3])

        @pl.when(passing)
        def _():
            piece = x_column(turn, 1 - near, 0)
            send(piece, piece, right_send, right_recv.at[turn, 4], to_other)

        @pl.when(jnp.logical_not(passing))
        def _():
            piece = x_column(turn, 1 - near, 1)
            send(piece, piece, right_send, right_recv.at[turn, 5], to_same)

        for k, sign in steps:
            drain(z_column(turn, 0), right_recv.at[turn, 6 + k])
            piece = z_column(turn, -sign, k)
            send(piece, piece, right_send, right_recv.at[turn, 8 + k], along_z(sign))

    def right_end(turn):
        @pl.when(jnp.logical_not(passing))
        def _():
            for k in range(2):
                drain(x_column(turn, 0, 0), right_recv.at[turn, 4 + k])
        for k in range(2):
            drain(z_column(turn, 0, 0), right_recv.at[turn, 8 + k])

    def right_sent(turn):
        for y_to in range(2):
            @pl.when(jnp.logical_not((y == y_to) & (grp == pass_grp)))
            def _():
                drain(right_own.at[turn], right_send)

        @pl.when(passing)
        def _():
            for _ in range(2):
                drain(right_all.at[turn, 0, 0:3, :, top], right_send)
                drain(x_column(turn, 0), right_send)

        drain(x_column(turn, 0, 0), right_send)
        for k in range(2):
            drain(z_column(turn, 0), right_send)
            drain(z_column(turn, 0, 0), right_send)

    lane_low = lane_iota((256, 128)) < 64

    def outer(turn):
        left_h, left_l = split(left_all[...].reshape(8, 2, 32, 128))
        left_wide = [
            jnp.concatenate([a[:, odd].reshape(256, 128) for a in (left_h, left_l, left_h)], axis=-1)
            for odd in range(2)
        ]
        right_flat = right_all.reshape(4 * 32 * 32, 128)

        def step(quad, carry):
            wide = []
            for e in range(4):
                high, low = split(jnp.concatenate(
                    [right_flat[pl.ds(1024 * (2 * turn + r2) + 4 * quad + e, 32, stride=32), :] for r2 in range(2)],
                    axis=0))
                wide.append(jnp.concatenate([high, high, low], axis=-1))
            even = dot(left_wide[0], jnp.concatenate(wide, axis=0), NT)
            odd = dot(left_wide[1], jnp.concatenate([wide[1], wide[0], wide[3], wide[2]], axis=0), NT)
            for m in range(2):
                lanes = slice(128 * m, 128 * m + 128)
                a, b = even[:, lanes], odd[:, lanes]
                for side, mixed in enumerate((jnp.where(lane_low, a, b), jnp.where(lane_low, b, a))):
                    high, low = split(mixed)
                    at = pl.ds(pl.multiple_of(512 * side + 64 * quad + 32 * m, 32), 32)
                    for i in range(8):
                        cols = slice(128 * (i % 2), 128 * (i % 2) + 128)
                        outer_h[i // 2, at, cols] = high[32 * i:32 * i + 32]
                        outer_l[i // 2, at, cols] = low[32 * i:32 * i + 32]
            return carry

        lax.fori_loop(0, 8, step, 0, unroll=4)

    def finish(turn):
        def step(i4, carry):
            total = []
            for side in range(2):
                at = slice(512 * side, 512 * side + 512)
                total.append(dot3((couple_h[:, at], couple_l[:, at]), (outer_h[i4, at, :], outer_l[i4, at, :])))
            for i2 in range(2):
                lanes = slice(128 * i2, 128 * i2 + 128)
                block = jnp.transpose(total[0][:, lanes] + pltpu.roll(total[1][:, lanes], 64, axis=1))
                for i1 in range(2):
                    for r2 in range(2):
                        at = 64 * i1 + 32 * r2
                        out_ref[4 * i4 + 2 * i2 + i1, pl.ds(2 * turn + r2, 32, stride=4), :] = block[at:at + 32]
            if turn == 1:
                four = pl.ds(4 * i4, 4)
                pltpu.make_async_copy(out_ref.at[four], out_hbm.at[four], out_copy.at[i4]).start()
            return carry

        lax.fori_loop(0, 4, step, 0, unroll=4)

    attend_column(0)
    finish_column(0)
    right_begin(0)
    attend_column(1)
    finish_column(1)
    right_begin(1)
    attend_column(2)
    right_first(0)
    finish_column(2)
    right_begin(2)
    attend_column(3)
    right_first(1)
    finish_column(3)
    right_begin(3)
    right_second(0)
    right_first(2)
    right_second(1)
    right_first(3)
    left_to = left_all.at[pl.ds(pl.multiple_of(grp * 128, 128), 128)]
    pltpu.make_async_copy(left_own, left_to, left_recv).start()
    for k in range(1, 4):
        send(left_own, left_to, left_send, left_recv, (dap, lax.rem(grp + k, 4)))
    right_second(2)
    right_third(0)
    right_second(3)
    right_third(1)
    for s2 in range(2):
        for part in range(2):
            tiles = units[part, pl.ds(256 * s2, 256), :].reshape(32, 8, 128)
            for s1 in range(2):
                revised_ref[:, s2, s1, :, 128 * part:128 * part + 128] = tiles[:, 4 * s1:4 * s1 + 4]
    pltpu.make_async_copy(revised_ref, revised_hbm, out_copy.at[4]).start()
    right_third(2)
    right_end(0)
    right_end(1)
    drain(left_all, left_recv)
    right_third(3)
    outer(0)
    finish(0)
    right_end(2)
    right_end(3)
    outer(1)
    finish(1)

    for i in range(4):
        four = pl.ds(4 * i, 4)
        pltpu.make_async_copy(out_ref.at[four], out_hbm.at[four], out_copy.at[i]).wait()
    pltpu.make_async_copy(revised_ref, revised_hbm, out_copy.at[4]).wait()
    for _ in range(31):
        drain(bias_ref, bias_send)
    drain(xs.at[0:31], x_send)
    drain(og.at[0:3], o_send)
    drain(finals.at[0:192], final_send)
    drain(left_all.at[0:384], left_send)
    for turn in range(4):
        right_sent(turn)


def emit_kernel(revised_in, pair_in, revised_out, pair_out, revised, pair, sems):
    copies = [(revised_in, revised, revised_out)]
    for i in range(4):
        four = pl.ds(4 * i, 4)
        copies.append((pair_in.at[four], pair.at[four], pair_out.at[four]))
    for i, (src, here, dst) in enumerate(copies):
        pltpu.make_async_copy(src, here, sems.at[0, i]).start()
    for i, (src, here, dst) in enumerate(copies):
        pltpu.make_async_copy(src, here, sems.at[0, i]).wait()
        pltpu.make_async_copy(here, dst, sems.at[1, i]).start()
    for i, (src, here, dst) in enumerate(copies):
        pltpu.make_async_copy(here, dst, sems.at[1, i]).wait()


VM = pl.BlockSpec(memory_space=pltpu.VMEM)
SM = pl.BlockSpec(memory_space=pltpu.SMEM)
ANY = pl.BlockSpec(memory_space=pl.ANY)
LIMIT = 58 * 1024 * 1024


def body(
    homolog_stack,
    couple_score_offset,
    strand_identity,
    strand_score_offset,
    homolog_presence,
    horizontal_matrix,
    horizontal_final_matrix,
    vertical_matrix,
    vertical_final_matrix,
    expand_matrix,
    shrink_matrix,
    tensor_matrix,
    couple_matrix,
):
    dma = pltpu.SemaphoreType.DMA
    regular = pltpu.SemaphoreType.REGULAR
    revised, pair = pl.pallas_call(
        kernel,
        out_shape=[
            jax.ShapeDtypeStruct((32, 2, 2, 4, 256), F32),
            jax.ShapeDtypeStruct((16, 128, 128), F32),
        ],
        in_specs=[ANY, VM, VM, SM] + [VM] * 4 + [ANY] * 5,
        out_specs=[ANY, ANY],
        scratch_shapes=[
            pltpu.VMEM((2, 4, 4, 2, 16, 512), F32),
            pltpu.VMEM((32, 2, 8, 256), F32),
            pltpu.VMEM((2, 32, 8, 256), F32),
            pltpu.VMEM((4, 2, 4, 4, 8, 128), F32),
            pltpu.VMEM((4, 2, 4, 4, 8, 128), F32),
            pltpu.VMEM((256, 256), F32),
            pltpu.VMEM((2, 512, 256), BF16),
            pltpu.VMEM((2, 512, 256), BF16),
            pltpu.VMEM((256, 768), BF16),
            pltpu.VMEM((256, 768), BF16),
            pltpu.VMEM((4, 2, 32, 16, 256), BF16),
            pltpu.VMEM((4, 512, 256), BF16),
            pltpu.VMEM((4, 1024, 256), BF16),
            pltpu.VMEM((4, 32, 16, 128), F32),
            pltpu.VMEM((32, 16, 128), F32),
            pltpu.VMEM((2, 128, 512), F32),
            pltpu.VMEM((2, 512, 128), F32),
            pltpu.VMEM((8, 512, 128), F32),
            pltpu.VMEM((2, 128, 128), F32),
            pltpu.VMEM((2, 512, 128), F32),
            pltpu.VMEM((128, 128), F32),
            pltpu.VMEM((4, 32, 128), F32),
            pltpu.VMEM((512, 128), F32),
            pltpu.VMEM((4, 2, 4, 4, 32, 128), F32),
            pltpu.VMEM((4, 1024, 256), BF16),
            pltpu.VMEM((4, 1024, 256), BF16),
            pltpu.VMEM((128, 1024), BF16),
            pltpu.VMEM((128, 1024), BF16),
            pltpu.VMEM((4, 256, 256), BF16),
            pltpu.VMEM((4, 256, 256), BF16),
            pltpu.VMEM((256, 256), BF16),
            pltpu.VMEM((256, 256), BF16),
            pltpu.VMEM((256, 1024), BF16),
            pltpu.VMEM((256, 1024), BF16),
            pltpu.VMEM((1024, 256), BF16),
            pltpu.VMEM((1024, 256), BF16),
            dma, dma((22,)), dma, dma, dma, dma((4,)), dma, dma,
            dma, dma, dma, dma((4, 10)), regular, regular, regular,
            pltpu.VMEM((4, 256, 256), F32),
            pltpu.VMEM((256, 256), F32),
            pltpu.VMEM((256, 1024), F32),
            pltpu.VMEM((1024, 256), F32),
            pltpu.VMEM((1024, 128), F32),
            dma((5,)),
            pltpu.VMEM((4, 32, 2, 8, 256), F32),
            dma((4,)),
            pltpu.VMEM((32, 2, 2, 4, 256), F32),
            pltpu.VMEM((16, 128, 128), F32),
            dma((5,)),
        ],
        compiler_params=pltpu.CompilerParams(
            collective_id=0, has_side_effects=True, vmem_limit_bytes=LIMIT
        ),
        name="msa_block",
    )(
        homolog_stack.reshape(4, 32, 2, 8, 256),
        couple_score_offset,
        strand_identity.reshape(1, 512),
        strand_score_offset,
        jnp.swapaxes(horizontal_matrix, 1, 2),
        horizontal_final_matrix,
        homolog_presence.reshape(1, 128),
        jnp.swapaxes(tensor_matrix, 1, 2),
        vertical_matrix,
        vertical_final_matrix,
        expand_matrix,
        shrink_matrix,
        couple_matrix,
    )
    revised, pair = pl.pallas_call(
        emit_kernel,
        out_shape=[
            jax.ShapeDtypeStruct((32, 2, 2, 4, 256), F32),
            jax.ShapeDtypeStruct((16, 128, 128), F32),
        ],
        in_specs=[ANY, ANY],
        out_specs=[ANY, ANY],
        scratch_shapes=[
            pltpu.VMEM((32, 2, 2, 4, 256), F32), pltpu.VMEM((16, 128, 128), F32), dma((2, 5)),
        ],
        name="emit",
    )(revised, pair)
    return revised.reshape(128, 4, 256), pair


def solution(mesh):
    return jax.shard_map(
        body,
        mesh=mesh,
        in_specs=(
            P("dap", None, None),
            P("grp", "dap", None),
            P(),
            P("grp"),
            P(),
            P(None, None, "grp"),
            P("grp", None),
            P(),
            P(),
            P(),
            P(),
            P(),
            P(),
        ),
        out_specs=(P(None, ("dap", "grp"), None), P("dap", "grp", None)),
        check_vma=False,
    )
```

```python
import functools
import math

import jax
import jax.numpy as jnp
from jax import lax
from jax.experimental import pallas as pl
from jax.experimental.pallas import tpu as pltpu
from jax.sharding import PartitionSpec as P

F32 = jnp.float32
BF16 = jnp.bfloat16
MESH = pl.DeviceIdType.MESH
HEAD = 32
LOG2E = math.log2(math.e)
NN = (((1,), (0,)), ((), ()))
NT = (((1,), (1,)), ((), ()))


def split(a):
    high = a.astype(BF16)
    return high, (a - high.astype(F32)).astype(BF16)


def dot(a, b, dims=NN):
    return lax.dot_general(a, b, dims, preferred_element_type=F32)


def dot3(a, b, dims=NN):
    rows = a[0].shape[0]
    both = dot(jnp.concatenate(a, axis=0), b[0], dims)
    return both[:rows] + (both[rows:] + dot(a[0], b[1], dims))


def normed(rows):
    center = rows - jnp.mean(rows, axis=-1, keepdims=True)
    spread = jnp.mean(center * center, axis=-1, keepdims=True)
    return center * lax.rsqrt(spread + 1e-05)


def merge_halves(a, b):
    upper = lax.broadcasted_iota(jnp.int32, a.shape, a.ndim - 2) < 4
    first = jnp.where(upper, a, pltpu.roll(b, 4, axis=b.ndim - 2))
    second = jnp.where(upper, pltpu.roll(a, 4, axis=a.ndim - 2), b)
    return first, second


def lane_iota(shape):
    return lax.broadcasted_iota(jnp.int32, shape, len(shape) - 1)


def drain(ref, sem):
    pltpu.make_async_copy(ref, ref, sem).wait()


def signal(sem, device):
    pl.semaphore_signal(sem, inc=1, device_id=device, device_id_type=MESH)


def send(src, dst, send_sem, recv_sem, device):
    pltpu.make_async_remote_copy(
        src_ref=src, dst_ref=dst, send_sem=send_sem, recv_sem=recv_sem,
        device_id=device, device_id_type=MESH,
    ).start()


def kernel(
    x_in, bias_ref, ids_ref, offset_ref, weight_ref, final_in_ref, live_ref, tensor_ref,
    vertical_in, final_in, expand_in, shrink_in, couple_in,
    revised_hbm, out_hbm,
    bias_all, xs, xr, os, og, finals, join_h, join_l, wide_h, wide_l, qs, ks, vs, gates, ids_col, chunk_bias,
    msa, proj, attended, units,
    left_own, right_own, left_all, right_all, outer_h, outer_l, couple_h, couple_l,
    vertical_h, vertical_l, last_h, last_l, expand_h, expand_l, shrink_h, shrink_l,
    bias_send, bias_recv, x_send, x_recv, o_send, o_recv, final_send, final_recv,
    left_send, left_recv, right_send, right_recv, near_z, near_x, near_y,
    vertical_ref, final_ref, expand_ref, shrink_ref, couple_ref, fetch,
    x_ref, x_fetch, revised_ref, out_ref, out_copy,
):
    dap = lax.axis_index("dap")
    grp = lax.axis_index("grp")
    y, x, z = dap // 16, lax.rem(dap // 4, 4), lax.rem(dap, 4)
    x_at = [lax.rem(x + i, 4) for i in range(4)]
    z_at = [lax.rem(z + i, 4) for i in range(4)]

    def along_x(i):
        return y * 16 + x_at[i % 4] * 4 + z, grp

    def along_z(i):
        return y * 16 + x * 4 + z_at[i % 4], grp

    across_y = ((1 - y) * 16 + x * 4 + z, grp)

    barrier = pltpu.get_barrier_semaphore()
    for i in range(1, 4):
        signal(barrier, along_x(i))
        signal(barrier, along_z(i))
        signal(barrier, (dap, lax.rem(grp + i, 4)))
    signal(barrier, across_y)

    late = (
        (vertical_in, vertical_ref), (final_in, final_ref), (expand_in, expand_ref),
        (shrink_in, shrink_ref), (couple_in, couple_ref),
    )
    for s in range(4):
        pltpu.make_async_copy(x_in.at[s], x_ref.at[s], x_fetch.at[s]).start()
    for i, (src, dst) in enumerate(late):
        pltpu.make_async_copy(src, dst, fetch.at[i]).start()

    zero = jnp.zeros((64, 256), F32)
    q_w = weight_ref[0] * (LOG2E / math.sqrt(HEAD))
    k_w, v_w, g_w = weight_ref[1], weight_ref[2], weight_ref[3]
    for at, parts in ((0, (q_w, q_w, q_w, zero)), (256, (k_w, k_w, k_w, zero)), (512, (v_w, v_w, g_w, g_w))):
        high, low = split(jnp.transpose(jnp.concatenate(parts, axis=0)))
        wide_h[:, at:at + 256] = high
        wide_l[:, at:at + 256] = low
    pl.semaphore_wait(barrier, 10)

    def unit(p, i, j, h=None):
        a, b = (x_at[j % 4], z_at[i % 4]) if p == 0 else (x_at[i % 4], z_at[j % 4])
        return bias_all.at[p, a, b] if h is None else bias_all.at[p, a, b, h]

    def line(p, j, h):
        return bias_all.at[0, x_at[j % 4], :, h] if p == 0 else bias_all.at[1, :, z_at[j % 4], h]

    def first_axis(p, i):
        return along_z(i) if p == 0 else along_x(i)

    def second_axis(p, i):
        return along_x(i) if p == 0 else along_z(i)

    steps = ((0, 1), (1, -1))
    own = bias_all.at[y, x, z]
    send(bias_ref, own, bias_send, bias_recv.at[0], across_y)
    pltpu.make_async_copy(bias_ref, own, bias_recv.at[21]).start()
    for i in range(1, 4):
        signal(near_z, along_z(i))
    drain(bias_ref, bias_recv.at[21])

    def own_path(act):
        for p in range(2):
            @pl.when(y == p)
            def _():
                act(p)

    def other_path(act):
        for p in range(2):
            @pl.when(y == 1 - p)
            def _():
                act(p)

    def spread(p):
        for i in (1, 3, 2):
            send(unit(p, 0, 0), unit(p, 0, 0), bias_send, bias_recv.at[1 + 10 * p], first_axis(p, i))
        for k, sign in steps:
            send(unit(p, 0, 0), unit(p, 0, 0), bias_send, bias_recv.at[3 + 10 * p + k], second_axis(p, sign))

    def spread_line(p):
        drain(bias_all.at[0, 0, 0:3], bias_recv.at[1 + 10 * p])
        for base, other in ((5, 0), (7, 1)):
            for i in (1, 3, 2):
                for k, sign in steps:
                    piece = unit(p, i, 0, (k + other) % 2)
                    send(piece, piece, bias_send, bias_recv.at[base + 10 * p + k], second_axis(p, sign))

    three = bias_all.at[0, 0, 0:3, 0]

    def forward_line(p):
        for k, sign in steps:
            drain(bias_ref, bias_recv.at[3 + 10 * p + k])
            drain(three, bias_recv.at[5 + 10 * p + k])
            send(line(p, -sign, k), line(p, -sign, k), bias_send,
                 bias_recv.at[9 + 10 * p + k], second_axis(p, sign))

    own_path(spread)

    final_to = finals.at[pl.ds(pl.multiple_of(grp * 64, 64), 64)]
    pltpu.make_async_copy(final_in_ref, final_to, final_recv).start()
    for k in range(1, 4):
        send(final_in_ref, final_to, final_send, final_recv, (dap, lax.rem(grp + k, 4)))

    def project(s):
        pltpu.make_async_copy(x_in.at[s], x_ref.at[s], x_fetch.at[s]).wait()
        rows = split(normed(x_ref[s].reshape(512, 256)))
        out = dot3(rows, (wide_h[...], wide_l[...]))
        lane = lane_iota((512, 256))
        head = lax.rem(lane, 64) // HEAD
        q_hi, q_lo = split(out[:, 0:256])
        q = jnp.where((lane >= 64) & (lane < 128), q_lo.astype(F32), q_hi.astype(F32))
        k_hi, k_lo = split(out[:, 256:512])
        k = jnp.where((lane >= 128) & (lane < 192), k_lo.astype(F32), k_hi.astype(F32))
        ks[s] = k.astype(BF16)
        lane_v = lane_iota((512, 128))
        head_v = lax.rem(lane_v, 64) // HEAD
        v_hi, v_lo = split(out[:, 512:640])
        v = jnp.where(lane_v >= 64, v_lo.astype(F32), v_hi.astype(F32))
        for h in range(2):
            qs[s, h] = jnp.where(head == h, q, 0.0).astype(BF16).reshape(32, 16, 256)
            vs[s, pl.ds(512 * h, 512), 0:128] = jnp.where(head_v == h, v, 0.0).astype(BF16)
            vs[s, pl.ds(512 * h, 512), 128:256] = jnp.where(head_v == h, 1.0, 0.0).astype(BF16)
        gates[s] = jax.nn.sigmoid(out[:, 640:768]).reshape(32, 16, 128)

    def project_and(s, carry):
        project(s)

        @pl.when(s == 0)
        def _():
            pl.semaphore_wait(near_z, 3)
            for i in range(1, 4):
                signal(near_x, along_x(i))
            drain(bias_ref, bias_recv.at[0])
            other_path(spread)

        @pl.when(s == 1)
        def _():
            own_path(spread_line)
            pl.semaphore_wait(near_x, 3)
            signal(near_y, across_y)

        @pl.when(s == 2)
        def _():
            other_path(spread_line)

        return carry

    lax.fori_loop(0, 4, project_and, 0)

    half = lax.rem(grp, 2)
    for s2 in range(2):
        first, second = merge_halves(x_ref[2 * s2, :, grp // 2], x_ref[2 * s2 + 1, :, grp // 2])
        xs[:, s2] = jnp.where(half == 0, first, second)
    for i in range(4):
        block = jnp.broadcast_to(ids_ref[:, 128 * i:128 * i + 128].astype(F32), (128, 128))
        ids_col[8 * i:8 * i + 8] = jnp.transpose(block).reshape(8, 16, 128)
    pl.semaphore_wait(near_y, 1)

    drain(finals, final_recv)
    gap = jnp.zeros((64, 256), F32)
    for s2 in range(2):
        pieces = []
        for g in range(4):
            piece = finals[64 * g:64 * g + 64, :]
            pieces += [piece, gap] if s2 == 0 else [gap, piece]
        join_h[s2], join_l[s2] = split(jnp.concatenate(pieces, axis=0))

    own_path(forward_line)
    for i, (src, dst) in enumerate(late):
        pltpu.make_async_copy(src, dst, fetch.at[i]).wait()

    for m in range(4):
        w = vertical_ref[m]
        if m == 0:
            w = w * (LOG2E / math.sqrt(HEAD))
        vertical_h[m], vertical_l[m] = split(w)
    last_h[...], last_l[...] = split(final_ref[...])
    expand_h[...], expand_l[...] = split(expand_ref[...])
    shrink_h[...], shrink_l[...] = split(shrink_ref[...])
    for odd in range(2):
        for b in range(4):
            rows = jnp.concatenate(
                [couple_ref[pl.ds(2 * (4 * b + i) + odd, 32, stride=32), :] for i in range(4)], axis=0)
            at = 512 * odd + 128 * b
            couple_h[:, at:at + 128], couple_l[:, at:at + 128] = split(jnp.transpose(rows))

    def turned(step):
        turn = step + step // 2 - 2 * (step // 3)
        return lax.rem(x + turn, 4), lax.rem(z + turn, 4)

    def settle(step):
        x_now, z_now = turned(step)
        drain(og.at[:, 0, 0:2], o_recv.at[step])
        rows = split(jnp.concatenate(
            [jnp.concatenate([og[g, 0, x_now].reshape(32, 128), og[g, 1, :, z_now].reshape(32, 128)], axis=0)
             for g in range(4)], axis=-1))
        for s2 in range(2):
            out = dot3(rows, (join_h[s2], join_l[s2])).reshape(8, 8, 256)
            for i in range(4):
                xs[4 * x_now + i, s2] += out[i]
                xs[16 + 4 * i + z_now, s2] += out[4 + i]

        def send_x(k, carry):
            low_half = 1 - k // 4
            place = lax.rem(k + x + z, 4)
            to = low_half * (4 * x_now + place) + (1 - low_half) * (16 + 4 * place + z_now)

            @pl.when(to == dap)
            def _():
                pltpu.make_async_copy(xs.at[to], xr.at[:, dap], x_recv).start()

            @pl.when(to != dap)
            def _():
                send(xs.at[to], xr.at[:, dap], x_send, x_recv, (to, grp))

            return carry

        lax.fori_loop(0, 8, send_x, 0)

    def attend(step, carry):
        x_now, z_now = turned(step)

        @pl.when(step == 1)
        def _():
            other_path(forward_line)
            for p in range(2):
                drain(three, bias_recv.at[7 + 10 * p + 1])

        @pl.when(step == 2)
        def _():
            for p in range(2):
                drain(three, bias_recv.at[7 + 10 * p])

        @pl.when(step == 3)
        def _():
            for p in range(2):
                for k in range(2):
                    drain(line(0, 0, 0), bias_recv.at[9 + 10 * p + k])

        def rows_of(ref, *lead):
            shape = ref.shape[-2:]
            upper = ref[(*lead, pl.ds(4 * x_now, 4))].reshape(64, shape[-1])
            return jnp.concatenate([upper] + [ref[(*lead, 16 + 4 * i + z_now)] for i in range(4)], axis=0)

        own_ids = rows_of(ids_col)
        same = (jnp.concatenate([own_ids] * 4, axis=-1) == ids_ref[...].astype(F32)).astype(F32)
        for h in range(2):
            here = jnp.concatenate(
                [bias_all[0, x_now, :, h].reshape(64, 512), bias_all[1, :, z_now, h].reshape(64, 512)], axis=0)
            chunk_bias[h] = (here + offset_ref[h] * same) * LOG2E
        outs = []
        for s in range(4):
            highs, lows = [], []
            both = dot(jnp.concatenate([rows_of(qs, s, h) for h in range(2)], axis=0), ks[s], NT)
            for h in range(2):
                logits = both[128 * h:128 * h + 128] + chunk_bias[h]
                weights = jnp.exp2(logits - jnp.max(logits, axis=-1, keepdims=True))
                high, low = split(weights)
                highs.append(high)
                lows.append(low)
            v = vs[s]
            total = dot(jnp.concatenate([jnp.concatenate(a, axis=-1) for a in (highs, lows)], axis=0), v)
            total = total[0:128] + total[128:256]
            top = total[:, 0:128]
            top = top + pltpu.roll(top, 64, axis=1)
            outs.append(top / total[:, 128:256] * rows_of(gates, s))
        left_lanes = lane_iota((128, 128)) < 64
        pair = [jnp.where(left_lanes, outs[s1], outs[2 + s1]).reshape(16, 8, 128) for s1 in range(2)]
        for side, tiles in enumerate(merge_halves(*pair)):
            tiles = tiles.reshape(8, 2, 8, 128)
            for t in range(2):
                os[2 * t + side, 0, x_now] = tiles[0:4, t]
                for i in range(4):
                    os[2 * t + side, 1, i, z_now] = tiles[4 + i, t]
        pltpu.make_async_copy(os.at[grp, 0, x_now], og.at[grp, 0, x_now], o_recv.at[step]).start()
        pltpu.make_async_copy(os.at[grp, 1, :, z_now], og.at[grp, 1, :, z_now], o_recv.at[step]).start()
        for k in (2, 1, 3):
            to = lax.rem(grp + k, 4)
            send(os.at[to, 0, x_now], og.at[grp, 0, x_now], o_send, o_recv.at[step], (dap, to))
            send(os.at[to, 1, :, z_now], og.at[grp, 1, :, z_now], o_send, o_recv.at[step], (dap, to))

        @pl.when(step > 0)
        def _():
            settle(step - 1)

        return carry

    lax.fori_loop(0, 4, attend, 0)
    settle(3)

    drain(xr, x_recv)

    for s2 in range(2):
        stack = xr[s2].reshape(256, 256)
        for part in range(2):
            msa[part, pl.ds(256 * s2, 256), :] = stack[:, 128 * part:128 * part + 128]

    rows = split(normed(jnp.concatenate([msa[0], msa[1]], axis=-1)))
    for m in range(4):
        out = dot3(rows, (vertical_h[m], vertical_l[m]))
        for part in range(2):
            proj[2 * m + part] = out[:, 128 * part:128 * part + 128]

    at = lax.broadcasted_iota(jnp.int32, (128, 128), 0)
    to = lax.broadcasted_iota(jnp.int32, (128, 128), 1)
    order = (at == 4 * lax.rem(to // 2, 32) + 2 * (to // 64) + lax.rem(to, 2)).astype(BF16)
    live = dot(live_ref[...].astype(F32).astype(BF16), order)
    live_total = jnp.sum(live)
    mask = (live - 1.0) * (1e9 * LOG2E)

    lane = lane_iota((128, 128))
    def attend_column(r):
        for part in range(2):
            q, k, v, g = (proj[2 * m + part, pl.ds(r, 128, stride=4), :] for m in range(4))
            q_h, q_l = split(q)
            k_h, k_l = split(k)
            v_h, v_l = split(v)
            keys = jnp.concatenate([k_h, k_h, k_l], axis=-1)
            wide_q, wide_v = [], []
            for h in range(4):
                mine = lane // HEAD == h
                none = jnp.zeros((128, 128), BF16)
                qm_h, qm_l = jnp.where(mine, q_h, none), jnp.where(mine, q_l, none)
                wide_q.append(jnp.concatenate([qm_h, qm_l, qm_h], axis=-1))
                wide_v.append(jnp.concatenate(
                    [jnp.where(mine, v_h, none), jnp.where(mine, v_l, none), mine.astype(BF16)], axis=-1))
            logits = dot(jnp.concatenate(wide_q, axis=0), keys, NT) + mask
            weights = jnp.exp2(logits - jnp.max(logits, axis=-1, keepdims=True))
            high, low = split(weights)
            values = jnp.concatenate(wide_v, axis=0)

            def heads_in_lanes(a):
                return jnp.concatenate([a[128 * h:128 * h + 128] for h in range(4)], axis=-1)

            total = dot(jnp.concatenate([heads_in_lanes(high), heads_in_lanes(low)], axis=0), values)
            total = total[0:128] + total[128:256]
            out = (total[:, 0:128] + total[:, 128:256]) / total[:, 256:384]
            attended[part] = out * jax.nn.sigmoid(g)

    narrow = split(tensor_ref[...].reshape(64, 256))

    def finish_column(turn):
        here = pl.ds(turn, 128, stride=4)
        before = jnp.concatenate([msa[part, here, :] for part in range(2)], axis=-1)
        gated = split(jnp.concatenate([attended[0], attended[1]], axis=-1))
        current = before + dot3(gated, (last_h[...], last_l[...]))
        hidden = jnp.maximum(dot3(split(normed(current)), (expand_h[...], expand_l[...])), 0.0)
        revised = current + dot3(split(hidden), (shrink_h[...], shrink_l[...]))
        for part in range(2):
            units[part, here, :] = revised[:, 128 * part:128 * part + 128]
        both = dot3(narrow, split(normed(revised)), NT)
        left_own[pl.ds(32 * turn, 32), :] = both[0:32] * (live / live_total)
        right_own[turn] = both[32:64] * live

    pass_grp = 2 * y + x // 2
    near = lax.rem(x, 2)
    passing = lax.rem(grp, 2) == x // 2
    to_same = (y * 16 + lax.rem(x + 1 + 2 * near, 4) * 4 + z, grp)
    to_other = (y * 16 + lax.rem(x + 3 + 2 * near, 4) * 4 + z, grp)
    top, low = pl.ds(0, 16), pl.ds(16, 16)

    def right_begin(turn):
        slot = right_all.at[turn, near, z, grp]
        for y_to in range(2):
            mine = (y == y_to) & (grp == pass_grp)

            @pl.when(mine)
            def _():
                pltpu.make_async_copy(right_own.at[turn], slot, right_recv.at[turn, 0]).start()

            @pl.when(jnp.logical_not(mine))
            def _():
                send(right_own.at[turn], slot, right_send, right_recv.at[turn, 0],
                     (y_to * 16 + x * 4 + z, pass_grp))

    def right_first(turn):
        @pl.when(passing)
        def _():
            drain(right_all.at[turn, near, z], right_recv.at[turn, 0])
            along = right_all.at[turn, near, z, :, top]
            for i in (1, 3, 2):
                send(along, along, right_send, right_recv.at[turn, 1], along_z(i))
            along = right_all.at[turn, near, z, :, low]
            for to in (to_same, to_other, along_x(2)):
                send(along, along, right_send, right_recv.at[turn, 2], to)

    def x_column(turn, row, part=None):
        which = pl.ds(0, 4) if part is None else pl.ds(2 * part, 2)
        return right_all.at[turn, row, :, which, top]

    def z_column(turn, i, part=None):
        which = pl.ds(0, 2) if part is None else part
        return right_all.at[turn, which, z_at[i % 4], :, low]

    def right_second(turn):
        @pl.when(passing)
        def _():
            drain(right_all.at[turn, near, 0:3, :, top], right_recv.at[turn, 1])
            for to in (to_same, to_other):
                send(x_column(turn, near), x_column(turn, near), right_send, right_recv.at[turn, 3], to)
            drain(right_all.at[turn, 0, z, :, low], right_recv.at[turn, 2])

        @pl.when(jnp.logical_not(passing))
        def _():
            drain(right_all.at[turn, :, z, :, low], right_recv.at[turn, 2])

        for k, sign in steps:
            send(z_column(turn, 0), z_column(turn, 0), right_send, right_recv.at[turn, 6 + k], along_z(sign))

    def right_third(turn):
        drain(x_column(turn, 0), right_recv.at[turn, 3])

        @pl.when(passing)
        def _():
            piece = x_column(turn, 1 - near, 0)
            send(piece, piece, right_send, right_recv.at[turn, 4], to_other)

        @pl.when(jnp.logical_not(passing))
        def _():
            piece = x_column(turn, 1 - near, 1)
            send(piece, piece, right_send, right_recv.at[turn, 5], to_same)

        for k, sign in steps:
            drain(z_column(turn, 0), right_recv.at[turn, 6 + k])
            piece = z_column(turn, -sign, k)
            send(piece, piece, right_send, right_recv.at[turn, 8 + k], along_z(sign))

    def right_end(turn):
        @pl.when(jnp.logical_not(passing))
        def _():
            for k in range(2):
                drain(x_column(turn, 0, 0), right_recv.at[turn, 4 + k])
        for k in range(2):
            drain(z_column(turn, 0, 0), right_recv.at[turn, 8 + k])

    def right_sent(turn):
        for y_to in range(2):
            @pl.when(jnp.logical_not((y == y_to) & (grp == pass_grp)))
            def _():
                drain(right_own.at[turn], right_send)

        @pl.when(passing)
        def _():
            for _ in range(2):
                drain(right_all.at[turn, 0, 0:3, :, top], right_send)
                drain(x_column(turn, 0), right_send)

        drain(x_column(turn, 0, 0), right_send)
        for k in range(2):
            drain(z_column(turn, 0), right_send)
            drain(z_column(turn, 0, 0), right_send)

    lane_low = lane_iota((256, 128)) < 64

    def outer(turn):
        left_h, left_l = split(left_all[...].reshape(8, 2, 32, 128))
        left_wide = [
            jnp.concatenate([a[:, odd].reshape(256, 128) for a in (left_h, left_l, left_h)], axis=-1)
            for odd in range(2)
        ]
        right_flat = right_all.reshape(4 * 32 * 32, 128)

        def step(quad, carry):
            wide = []
            for e in range(4):
                high, low = split(jnp.concatenate(
                    [right_flat[pl.ds(1024 * (2 * turn + r2) + 4 * quad + e, 32, stride=32), :] for r2 in range(2)],
                    axis=0))
                wide.append(jnp.concatenate([high, high, low], axis=-1))
            even = dot(left_wide[0], jnp.concatenate(wide, axis=0), NT)
            odd = dot(left_wide[1], jnp.concatenate([wide[1], wide[0], wide[3], wide[2]], axis=0), NT)
            for m in range(2):
                lanes = slice(128 * m, 128 * m + 128)
                a, b = even[:, lanes], odd[:, lanes]
                for side, mixed in enumerate((jnp.where(lane_low, a, b), jnp.where(lane_low, b, a))):
                    high, low = split(mixed)
                    at = pl.ds(pl.multiple_of(512 * side + 64 * quad + 32 * m, 32), 32)
                    for i in range(8):
                        cols = slice(128 * (i % 2), 128 * (i % 2) + 128)
                        outer_h[i // 2, at, cols] = high[32 * i:32 * i + 32]
                        outer_l[i // 2, at, cols] = low[32 * i:32 * i + 32]
            return carry

        lax.fori_loop(0, 8, step, 0, unroll=4)

    def finish(turn):
        def step(i4, carry):
            total = []
            for side in range(2):
                at = slice(512 * side, 512 * side + 512)
                total.append(dot3((couple_h[:, at], couple_l[:, at]), (outer_h[i4, at, :], outer_l[i4, at, :])))
            for i2 in range(2):
                lanes = slice(128 * i2, 128 * i2 + 128)
                block = jnp.transpose(total[0][:, lanes] + pltpu.roll(total[1][:, lanes], 64, axis=1))
                for i1 in range(2):
                    for r2 in range(2):
                        at = 64 * i1 + 32 * r2
                        out_ref[4 * i4 + 2 * i2 + i1, pl.ds(2 * turn + r2, 32, stride=4), :] = block[at:at + 32]
            if turn == 1:
                four = pl.ds(4 * i4, 4)
                pltpu.make_async_copy(out_ref.at[four], out_hbm.at[four], out_copy.at[i4]).start()
            return carry

        lax.fori_loop(0, 4, step, 0, unroll=4)

    attend_column(0)
    finish_column(0)
    right_begin(0)
    attend_column(1)
    finish_column(1)
    right_begin(1)
    attend_column(2)
    right_first(0)
    finish_column(2)
    right_begin(2)
    attend_column(3)
    right_first(1)
    finish_column(3)
    right_begin(3)
    right_second(0)
    right_first(2)
    right_second(1)
    right_first(3)
    left_to = left_all.at[pl.ds(pl.multiple_of(grp * 128, 128), 128)]
    pltpu.make_async_copy(left_own, left_to, left_recv).start()
    for k in range(1, 4):
        send(left_own, left_to, left_send, left_recv, (dap, lax.rem(grp + k, 4)))
    right_second(2)
    right_third(0)
    right_second(3)
    right_third(1)
    for s2 in range(2):
        for part in range(2):
            tiles = units[part, pl.ds(256 * s2, 256), :].reshape(32, 8, 128)
            for s1 in range(2):
                revised_ref[:, s2, s1, :, 128 * part:128 * part + 128] = tiles[:, 4 * s1:4 * s1 + 4]
    pltpu.make_async_copy(revised_ref, revised_hbm, out_copy.at[4]).start()
    right_third(2)
    right_end(0)
    right_end(1)
    drain(left_all, left_recv)
    right_third(3)
    outer(0)
    finish(0)
    right_end(2)
    right_end(3)
    outer(1)
    finish(1)

    for i in range(4):
        four = pl.ds(4 * i, 4)
        pltpu.make_async_copy(out_ref.at[four], out_hbm.at[four], out_copy.at[i]).wait()
    pltpu.make_async_copy(revised_ref, revised_hbm, out_copy.at[4]).wait()
    for _ in range(31):
        drain(bias_ref, bias_send)
    drain(xs.at[0:31], x_send)
    drain(og.at[0:3], o_send)
    drain(finals.at[0:192], final_send)
    drain(left_all.at[0:384], left_send)
    for turn in range(4):
        right_sent(turn)


def emit_kernel(revised_in, pair_in, revised_out, pair_out, revised, pair, sems):
    copies = [(revised_in, revised, revised_out)]
    for i in range(4):
        four = pl.ds(4 * i, 4)
        copies.append((pair_in.at[four], pair.at[four], pair_out.at[four]))
    for i, (src, here, dst) in enumerate(copies):
        pltpu.make_async_copy(src, here, sems.at[0, i]).start()
    for i, (src, here, dst) in enumerate(copies):
        pltpu.make_async_copy(src, here, sems.at[0, i]).wait()
        pltpu.make_async_copy(here, dst, sems.at[1, i]).start()
    for i, (src, here, dst) in enumerate(copies):
        pltpu.make_async_copy(here, dst, sems.at[1, i]).wait()


VM = pl.BlockSpec(memory_space=pltpu.VMEM)
SM = pl.BlockSpec(memory_space=pltpu.SMEM)
ANY = pl.BlockSpec(memory_space=pl.ANY)
LIMIT = 58 * 1024 * 1024


def body(
    homolog_stack,
    couple_score_offset,
    strand_identity,
    strand_score_offset,
    homolog_presence,
    horizontal_matrix,
    horizontal_final_matrix,
    vertical_matrix,
    vertical_final_matrix,
    expand_matrix,
    shrink_matrix,
    tensor_matrix,
    couple_matrix,
):
    dma = pltpu.SemaphoreType.DMA
    regular = pltpu.SemaphoreType.REGULAR
    revised, pair = pl.pallas_call(
        kernel,
        out_shape=[
            jax.ShapeDtypeStruct((32, 2, 2, 4, 256), F32),
            jax.ShapeDtypeStruct((16, 128, 128), F32),
        ],
        in_specs=[ANY, VM, VM, SM] + [VM] * 4 + [ANY] * 5,
        out_specs=[ANY, ANY],
        scratch_shapes=[
            pltpu.VMEM((2, 4, 4, 2, 16, 512), F32),
            pltpu.VMEM((32, 2, 8, 256), F32),
            pltpu.VMEM((2, 32, 8, 256), F32),
            pltpu.VMEM((4, 2, 4, 4, 8, 128), F32),
            pltpu.VMEM((4, 2, 4, 4, 8, 128), F32),
            pltpu.VMEM((256, 256), F32),
            pltpu.VMEM((2, 512, 256), BF16),
            pltpu.VMEM((2, 512, 256), BF16),
            pltpu.VMEM((256, 768), BF16),
            pltpu.VMEM((256, 768), BF16),
            pltpu.VMEM((4, 2, 32, 16, 256), BF16),
            pltpu.VMEM((4, 512, 256), BF16),
            pltpu.VMEM((4, 1024, 256), BF16),
            pltpu.VMEM((4, 32, 16, 128), F32),
            pltpu.VMEM((32, 16, 128), F32),
            pltpu.VMEM((2, 128, 512), F32),
            pltpu.VMEM((2, 512, 128), F32),
            pltpu.VMEM((8, 512, 128), F32),
            pltpu.VMEM((2, 128, 128), F32),
            pltpu.VMEM((2, 512, 128), F32),
            pltpu.VMEM((128, 128), F32),
            pltpu.VMEM((4, 32, 128), F32),
            pltpu.VMEM((512, 128), F32),
            pltpu.VMEM((4, 2, 4, 4, 32, 128), F32),
            pltpu.VMEM((4, 1024, 256), BF16),
            pltpu.VMEM((4, 1024, 256), BF16),
            pltpu.VMEM((128, 1024), BF16),
            pltpu.VMEM((128, 1024), BF16),
            pltpu.VMEM((4, 256, 256), BF16),
            pltpu.VMEM((4, 256, 256), BF16),
            pltpu.VMEM((256, 256), BF16),
            pltpu.VMEM((256, 256), BF16),
            pltpu.VMEM((256, 1024), BF16),
            pltpu.VMEM((256, 1024), BF16),
            pltpu.VMEM((1024, 256), BF16),
            pltpu.VMEM((1024, 256), BF16),
            dma, dma((22,)), dma, dma, dma, dma((4,)), dma, dma,
            dma, dma, dma, dma((4, 10)), regular, regular, regular,
            pltpu.VMEM((4, 256, 256), F32),
            pltpu.VMEM((256, 256), F32),
            pltpu.VMEM((256, 1024), F32),
            pltpu.VMEM((1024, 256), F32),
            pltpu.VMEM((1024, 128), F32),
            dma((5,)),
            pltpu.VMEM((4, 32, 2, 8, 256), F32),
            dma((4,)),
            pltpu.VMEM((32, 2, 2, 4, 256), F32),
            pltpu.VMEM((16, 128, 128), F32),
            dma((5,)),
        ],
        compiler_params=pltpu.CompilerParams(
            collective_id=0, has_side_effects=True, vmem_limit_bytes=LIMIT
        ),
        name="msa_block",
    )(
        homolog_stack.reshape(4, 32, 2, 8, 256),
        couple_score_offset,
        strand_identity.reshape(1, 512),
        strand_score_offset,
        jnp.swapaxes(horizontal_matrix, 1, 2),
        horizontal_final_matrix,
        homolog_presence.reshape(1, 128),
        jnp.swapaxes(tensor_matrix, 1, 2),
        vertical_matrix,
        vertical_final_matrix,
        expand_matrix,
        shrink_matrix,
        couple_matrix,
    )
    revised, pair = pl.pallas_call(
        emit_kernel,
        out_shape=[
            jax.ShapeDtypeStruct((32, 2, 2, 4, 256), F32),
            jax.ShapeDtypeStruct((16, 128, 128), F32),
        ],
        in_specs=[ANY, ANY],
        out_specs=[ANY, ANY],
        scratch_shapes=[
            pltpu.VMEM((32, 2, 2, 4, 256), F32), pltpu.VMEM((16, 128, 128), F32), dma((2, 5)),
        ],
        name="emit",
    )(revised, pair)
    return revised.reshape(128, 4, 256), pair


def solution(mesh):
    return jax.shard_map(
        body,
        mesh=mesh,
        in_specs=(
            P("dap", None, None),
            P("grp", "dap", None),
            P(),
            P("grp"),
            P(),
            P(None, None, "grp"),
            P("grp", None),
            P(),
            P(),
            P(),
            P(),
            P(),
            P(),
        ),
        out_specs=(P(None, ("dap", "grp"), None), P("dap", "grp", None)),
        check_vma=False,
    )
```

```python
import functools
import math

import jax
import jax.numpy as jnp
from jax import lax
from jax.experimental import pallas as pl
from jax.experimental.pallas import tpu as pltpu
from jax.sharding import PartitionSpec as P

F32 = jnp.float32
BF16 = jnp.bfloat16
MESH = pl.DeviceIdType.MESH
HEAD = 32
LOG2E = math.log2(math.e)
NN = (((1,), (0,)), ((), ()))
NT = (((1,), (1,)), ((), ()))


def split(a):
    high = a.astype(BF16)
    return high, (a - high.astype(F32)).astype(BF16)


def dot(a, b, dims=NN):
    return lax.dot_general(a, b, dims, preferred_element_type=F32)


def dot3(a, b, dims=NN):
    rows = a[0].shape[0]
    both = dot(jnp.concatenate(a, axis=0), b[0], dims)
    return both[:rows] + (both[rows:] + dot(a[0], b[1], dims))


def normed(rows):
    center = rows - jnp.mean(rows, axis=-1, keepdims=True)
    spread = jnp.mean(center * center, axis=-1, keepdims=True)
    return center * lax.rsqrt(spread + 1e-05)


def merge_halves(a, b):
    upper = lax.broadcasted_iota(jnp.int32, a.shape, a.ndim - 2) < 4
    first = jnp.where(upper, a, pltpu.roll(b, 4, axis=b.ndim - 2))
    second = jnp.where(upper, pltpu.roll(a, 4, axis=a.ndim - 2), b)
    return first, second


def lane_iota(shape):
    return lax.broadcasted_iota(jnp.int32, shape, len(shape) - 1)


def drain(ref, sem):
    pltpu.make_async_copy(ref, ref, sem).wait()


def signal(sem, device):
    pl.semaphore_signal(sem, inc=1, device_id=device, device_id_type=MESH)


def send(src, dst, send_sem, recv_sem, device):
    pltpu.make_async_remote_copy(
        src_ref=src, dst_ref=dst, send_sem=send_sem, recv_sem=recv_sem,
        device_id=device, device_id_type=MESH,
    ).start()


def kernel(
    x_in, bias_ref, ids_ref, offset_ref, weight_ref, final_in_ref, live_ref, tensor_ref,
    vertical_in, final_in, expand_in, shrink_in, couple_in,
    revised_hbm, out_hbm,
    bias_all, xs, xr, os, og, finals, join_h, join_l, wide_h, wide_l, qs, ks, vs, gates, ids_col, chunk_bias,
    msa, proj, attended, units,
    left_own, right_own, left_all, right_all, outer_h, outer_l, couple_h, couple_l,
    vertical_h, vertical_l, last_h, last_l, expand_h, expand_l, shrink_h, shrink_l,
    bias_send, bias_recv, x_send, x_recv, o_send, o_recv, final_send, final_recv,
    left_send, left_recv, right_send, right_recv, near_z, near_x, near_y,
    vertical_ref, final_ref, expand_ref, shrink_ref, couple_ref, fetch,
    x_ref, x_fetch, revised_ref, out_ref, out_copy,
):
    dap = lax.axis_index("dap")
    grp = lax.axis_index("grp")
    y, x, z = dap // 16, lax.rem(dap // 4, 4), lax.rem(dap, 4)
    x_at = [lax.rem(x + i, 4) for i in range(4)]
    z_at = [lax.rem(z + i, 4) for i in range(4)]

    def along_x(i):
        return y * 16 + x_at[i % 4] * 4 + z, grp

    def along_z(i):
        return y * 16 + x * 4 + z_at[i % 4], grp

    across_y = ((1 - y) * 16 + x * 4 + z, grp)

    barrier = pltpu.get_barrier_semaphore()
    for i in range(1, 4):
        signal(barrier, along_x(i))
        signal(barrier, along_z(i))
        signal(barrier, (dap, lax.rem(grp + i, 4)))
    signal(barrier, across_y)

    late = (
        (vertical_in, vertical_ref), (final_in, final_ref), (expand_in, expand_ref),
        (shrink_in, shrink_ref), (couple_in, couple_ref),
    )
    for s in range(4):
        pltpu.make_async_copy(x_in.at[s], x_ref.at[s], x_fetch.at[s]).start()
    for i, (src, dst) in enumerate(late):
        pltpu.make_async_copy(src, dst, fetch.at[i]).start()

    zero = jnp.zeros((64, 256), F32)
    q_w = weight_ref[0] * (LOG2E / math.sqrt(HEAD))
    k_w, v_w, g_w = weight_ref[1], weight_ref[2], weight_ref[3]
    for at, parts in ((0, (q_w, q_w, q_w, zero)), (256, (k_w, k_w, k_w, zero)), (512, (v_w, v_w, g_w, g_w))):
        high, low = split(jnp.transpose(jnp.concatenate(parts, axis=0)))
        wide_h[:, at:at + 256] = high
        wide_l[:, at:at + 256] = low
    pl.semaphore_wait(barrier, 10)

    def unit(p, i, j, h=None):
        a, b = (x_at[j % 4], z_at[i % 4]) if p == 0 else (x_at[i % 4], z_at[j % 4])
        return bias_all.at[p, a, b] if h is None else bias_all.at[p, a, b, h]

    def line(p, j, h):
        return bias_all.at[0, x_at[j % 4], :, h] if p == 0 else bias_all.at[1, :, z_at[j % 4], h]

    def first_axis(p, i):
        return along_z(i) if p == 0 else along_x(i)

    def second_axis(p, i):
        return along_x(i) if p == 0 else along_z(i)

    steps = ((0, 1), (1, -1))
    own = bias_all.at[y, x, z]
    send(bias_ref, own, bias_send, bias_recv.at[0], across_y)
    pltpu.make_async_copy(bias_ref, own, bias_recv.at[21]).start()
    for i in range(1, 4):
        signal(near_z, along_z(i))
    drain(bias_ref, bias_recv.at[21])

    def own_path(act):
        for p in range(2):
            @pl.when(y == p)
            def _():
                act(p)

    def other_path(act):
        for p in range(2):
            @pl.when(y == 1 - p)
            def _():
                act(p)

    def spread(p):
        for i in (1, 3, 2):
            send(unit(p, 0, 0), unit(p, 0, 0), bias_send, bias_recv.at[1 + 10 * p], first_axis(p, i))
        for k, sign in steps:
            send(unit(p, 0, 0), unit(p, 0, 0), bias_send, bias_recv.at[3 + 10 * p + k], second_axis(p, sign))

    def spread_line(p):
        drain(bias_all.at[0, 0, 0:3], bias_recv.at[1 + 10 * p])
        for base, other in ((5, 0), (7, 1)):
            for i in (1, 3, 2):
                for k, sign in steps:
                    piece = unit(p, i, 0, (k + other) % 2)
                    send(piece, piece, bias_send, bias_recv.at[base + 10 * p + k], second_axis(p, sign))

    three = bias_all.at[0, 0, 0:3, 0]

    def forward_line(p):
        for k, sign in steps:
            drain(bias_ref, bias_recv.at[3 + 10 * p + k])
            drain(three, bias_recv.at[5 + 10 * p + k])
            send(line(p, -sign, k), line(p, -sign, k), bias_send,
                 bias_recv.at[9 + 10 * p + k], second_axis(p, sign))

    own_path(spread)

    final_to = finals.at[pl.ds(pl.multiple_of(grp * 64, 64), 64)]
    pltpu.make_async_copy(final_in_ref, final_to, final_recv).start()
    for k in range(1, 4):
        send(final_in_ref, final_to, final_send, final_recv, (dap, lax.rem(grp + k, 4)))

    def project(s):
        pltpu.make_async_copy(x_in.at[s], x_ref.at[s], x_fetch.at[s]).wait()
        rows = split(normed(x_ref[s].reshape(512, 256)))
        out = dot3(rows, (wide_h[...], wide_l[...]))
        lane = lane_iota((512, 256))
        head = lax.rem(lane, 64) // HEAD
        q_hi, q_lo = split(out[:, 0:256])
        q = jnp.where((lane >= 64) & (lane < 128), q_lo.astype(F32), q_hi.astype(F32))
        k_hi, k_lo = split(out[:, 256:512])
        k = jnp.where((lane >= 128) & (lane < 192), k_lo.astype(F32), k_hi.astype(F32))
        ks[s] = k.astype(BF16)
        lane_v = lane_iota((512, 128))
        head_v = lax.rem(lane_v, 64) // HEAD
        v_hi, v_lo = split(out[:, 512:640])
        v = jnp.where(lane_v >= 64, v_lo.astype(F32), v_hi.astype(F32))
        for h in range(2):
            qs[s, h] = jnp.where(head == h, q, 0.0).astype(BF16).reshape(32, 16, 256)
            vs[s, pl.ds(512 * h, 512), 0:128] = jnp.where(head_v == h, v, 0.0).astype(BF16)
            vs[s, pl.ds(512 * h, 512), 128:256] = jnp.where(head_v == h, 1.0, 0.0).astype(BF16)
        gates[s] = jax.nn.sigmoid(out[:, 640:768]).reshape(32, 16, 128)

    def project_and(s, carry):
        project(s)

        @pl.when(s == 0)
        def _():
            pl.semaphore_wait(near_z, 3)
            for i in range(1, 4):
                signal(near_x, along_x(i))
            drain(bias_ref, bias_recv.at[0])
            other_path(spread)

        @pl.when(s == 1)
        def _():
            own_path(spread_line)
            pl.semaphore_wait(near_x, 3)
            signal(near_y, across_y)

        @pl.when(s == 2)
        def _():
            other_path(spread_line)

        return carry

    lax.fori_loop(0, 4, project_and, 0)

    half = lax.rem(grp, 2)
    for s2 in range(2):
        first, second = merge_halves(x_ref[2 * s2, :, grp // 2], x_ref[2 * s2 + 1, :, grp // 2])
        xs[:, s2] = jnp.where(half == 0, first, second)
    for i in range(4):
        block = jnp.broadcast_to(ids_ref[:, 128 * i:128 * i + 128].astype(F32), (128, 128))
        ids_col[8 * i:8 * i + 8] = jnp.transpose(block).reshape(8, 16, 128)
    pl.semaphore_wait(near_y, 1)

    drain(finals, final_recv)
    gap = jnp.zeros((64, 256), F32)
    for s2 in range(2):
        pieces = []
        for g in range(4):
            piece = finals[64 * g:64 * g + 64, :]
            pieces += [piece, gap] if s2 == 0 else [gap, piece]
        join_h[s2], join_l[s2] = split(jnp.concatenate(pieces, axis=0))

    own_path(forward_line)
    for i, (src, dst) in enumerate(late):
        pltpu.make_async_copy(src, dst, fetch.at[i]).wait()

    for m in range(4):
        w = vertical_ref[m]
        if m == 0:
            w = w * (LOG2E / math.sqrt(HEAD))
        vertical_h[m], vertical_l[m] = split(w)
    last_h[...], last_l[...] = split(final_ref[...])
    expand_h[...], expand_l[...] = split(expand_ref[...])
    shrink_h[...], shrink_l[...] = split(shrink_ref[...])
    for odd in range(2):
        for b in range(4):
            rows = jnp.concatenate(
                [couple_ref[pl.ds(2 * (4 * b + i) + odd, 32, stride=32), :] for i in range(4)], axis=0)
            at = 512 * odd + 128 * b
            couple_h[:, at:at + 128], couple_l[:, at:at + 128] = split(jnp.transpose(rows))

    def turned(step):
        turn = step + step // 2 - 2 * (step // 3)
        return lax.rem(x + turn, 4), lax.rem(z + turn, 4)

    def settle(step):
        x_now, z_now = turned(step)
        drain(og.at[:, 0, 0:2], o_recv.at[step])
        rows = split(jnp.concatenate(
            [jnp.concatenate([og[g, 0, x_now].reshape(32, 128), og[g, 1, :, z_now].reshape(32, 128)], axis=0)
             for g in range(4)], axis=-1))
        for s2 in range(2):
            out = dot3(rows, (join_h[s2], join_l[s2])).reshape(8, 8, 256)
            for i in range(4):
                xs[4 * x_now + i, s2] += out[i]
                xs[16 + 4 * i + z_now, s2] += out[4 + i]

        def send_x(k, carry):
            low_half = 1 - k // 4
            place = lax.rem(k + x + z, 4)
            to = low_half * (4 * x_now + place) + (1 - low_half) * (16 + 4 * place + z_now)

            @pl.when(to == dap)
            def _():
                pltpu.make_async_copy(xs.at[to], xr.at[:, dap], x_recv).start()

            @pl.when(to != dap)
            def _():
                send(xs.at[to], xr.at[:, dap], x_send, x_recv, (to, grp))

            return carry

        lax.fori_loop(0, 8, send_x, 0, unroll=True)

    def attend(step, carry):
        x_now, z_now = turned(step)

        @pl.when(step == 1)
        def _():
            other_path(forward_line)
            for p in range(2):
                drain(three, bias_recv.at[7 + 10 * p + 1])

        @pl.when(step == 2)
        def _():
            for p in range(2):
                drain(three, bias_recv.at[7 + 10 * p])

        @pl.when(step == 3)
        def _():
            for p in range(2):
                for k in range(2):
                    drain(line(0, 0, 0), bias_recv.at[9 + 10 * p + k])

        def rows_of(ref, *lead):
            shape = ref.shape[-2:]
            upper = ref[(*lead, pl.ds(4 * x_now, 4))].reshape(64, shape[-1])
            return jnp.concatenate([upper] + [ref[(*lead, 16 + 4 * i + z_now)] for i in range(4)], axis=0)

        own_ids = rows_of(ids_col)
        same = (jnp.concatenate([own_ids] * 4, axis=-1) == ids_ref[...].astype(F32)).astype(F32)
        for h in range(2):
            here = jnp.concatenate(
                [bias_all[0, x_now, :, h].reshape(64, 512), bias_all[1, :, z_now, h].reshape(64, 512)], axis=0)
            chunk_bias[h] = (here + offset_ref[h] * same) * LOG2E
        outs = []
        for s in range(4):
            highs, lows = [], []
            both = dot(jnp.concatenate([rows_of(qs, s, h) for h in range(2)], axis=0), ks[s], NT)
            for h in range(2):
                logits = both[128 * h:128 * h + 128] + chunk_bias[h]
                weights = jnp.exp2(logits - jnp.max(logits, axis=-1, keepdims=True))
                high, low = split(weights)
                highs.append(high)
                lows.append(low)
            v = vs[s]
            total = dot(jnp.concatenate([jnp.concatenate(a, axis=-1) for a in (highs, lows)], axis=0), v)
            total = total[0:128] + total[128:256]
            top = total[:, 0:128]
            top = top + pltpu.roll(top, 64, axis=1)
            outs.append(top / total[:, 128:256] * rows_of(gates, s))
        left_lanes = lane_iota((128, 128)) < 64
        pair = [jnp.where(left_lanes, outs[s1], outs[2 + s1]).reshape(16, 8, 128) for s1 in range(2)]
        for side, tiles in enumerate(merge_halves(*pair)):
            tiles = tiles.reshape(8, 2, 8, 128)
            for t in range(2):
                os[2 * t + side, 0, x_now] = tiles[0:4, t]
                for i in range(4):
                    os[2 * t + side, 1, i, z_now] = tiles[4 + i, t]
        pltpu.make_async_copy(os.at[grp, 0, x_now], og.at[grp, 0, x_now], o_recv.at[step]).start()
        pltpu.make_async_copy(os.at[grp, 1, :, z_now], og.at[grp, 1, :, z_now], o_recv.at[step]).start()
        for k in (2, 1, 3):
            to = lax.rem(grp + k, 4)
            send(os.at[to, 0, x_now], og.at[grp, 0, x_now], o_send, o_recv.at[step], (dap, to))
            send(os.at[to, 1, :, z_now], og.at[grp, 1, :, z_now], o_send, o_recv.at[step], (dap, to))

        @pl.when(step > 0)
        def _():
            settle(step - 1)

        return carry

    lax.fori_loop(0, 4, attend, 0)
    settle(3)

    drain(xr, x_recv)

    for s2 in range(2):
        stack = xr[s2].reshape(256, 256)
        for part in range(2):
            msa[part, pl.ds(256 * s2, 256), :] = stack[:, 128 * part:128 * part + 128]

    rows = split(normed(jnp.concatenate([msa[0], msa[1]], axis=-1)))
    for m in range(4):
        out = dot3(rows, (vertical_h[m], vertical_l[m]))
        for part in range(2):
            proj[2 * m + part] = out[:, 128 * part:128 * part + 128]

    at = lax.broadcasted_iota(jnp.int32, (128, 128), 0)
    to = lax.broadcasted_iota(jnp.int32, (128, 128), 1)
    order = (at == 4 * lax.rem(to // 2, 32) + 2 * (to // 64) + lax.rem(to, 2)).astype(BF16)
    live = dot(live_ref[...].astype(F32).astype(BF16), order)
    live_total = jnp.sum(live)
    mask = (live - 1.0) * (1e9 * LOG2E)

    lane = lane_iota((128, 128))
    def attend_column(r):
        for part in range(2):
            q, k, v, g = (proj[2 * m + part, pl.ds(r, 128, stride=4), :] for m in range(4))
            q_h, q_l = split(q)
            k_h, k_l = split(k)
            v_h, v_l = split(v)
            keys = jnp.concatenate([k_h, k_h, k_l], axis=-1)
            wide_q, wide_v = [], []
            for h in range(4):
                mine = lane // HEAD == h
                none = jnp.zeros((128, 128), BF16)
                qm_h, qm_l = jnp.where(mine, q_h, none), jnp.where(mine, q_l, none)
                wide_q.append(jnp.concatenate([qm_h, qm_l, qm_h], axis=-1))
                wide_v.append(jnp.concatenate(
                    [jnp.where(mine, v_h, none), jnp.where(mine, v_l, none), mine.astype(BF16)], axis=-1))
            logits = dot(jnp.concatenate(wide_q, axis=0), keys, NT) + mask
            weights = jnp.exp2(logits - jnp.max(logits, axis=-1, keepdims=True))
            high, low = split(weights)
            values = jnp.concatenate(wide_v, axis=0)

            def heads_in_lanes(a):
                return jnp.concatenate([a[128 * h:128 * h + 128] for h in range(4)], axis=-1)

            total = dot(jnp.concatenate([heads_in_lanes(high), heads_in_lanes(low)], axis=0), values)
            total = total[0:128] + total[128:256]
            out = (total[:, 0:128] + total[:, 128:256]) / total[:, 256:384]
            attended[part] = out * jax.nn.sigmoid(g)

    narrow = split(tensor_ref[...].reshape(64, 256))

    def finish_column(turn):
        here = pl.ds(turn, 128, stride=4)
        before = jnp.concatenate([msa[part, here, :] for part in range(2)], axis=-1)
        gated = split(jnp.concatenate([attended[0], attended[1]], axis=-1))
        current = before + dot3(gated, (last_h[...], last_l[...]))
        hidden = jnp.maximum(dot3(split(normed(current)), (expand_h[...], expand_l[...])), 0.0)
        revised = current + dot3(split(hidden), (shrink_h[...], shrink_l[...]))
        for part in range(2):
            units[part, here, :] = revised[:, 128 * part:128 * part + 128]
        both = dot3(narrow, split(normed(revised)), NT)
        left_own[pl.ds(32 * turn, 32), :] = both[0:32] * (live / live_total)
        right_own[turn] = both[32:64] * live

    pass_grp = 2 * y + x // 2
    near = lax.rem(x, 2)
    passing = lax.rem(grp, 2) == x // 2
    to_same = (y * 16 + lax.rem(x + 1 + 2 * near, 4) * 4 + z, grp)
    to_other = (y * 16 + lax.rem(x + 3 + 2 * near, 4) * 4 + z, grp)
    top, low = pl.ds(0, 16), pl.ds(16, 16)

    def right_begin(turn):
        slot = right_all.at[turn, near, z, grp]
        for y_to in range(2):
            mine = (y == y_to) & (grp == pass_grp)

            @pl.when(mine)
            def _():
                pltpu.make_async_copy(right_own.at[turn], slot, right_recv.at[turn, 0]).start()

            @pl.when(jnp.logical_not(mine))
            def _():
                send(right_own.at[turn], slot, right_send, right_recv.at[turn, 0],
                     (y_to * 16 + x * 4 + z, pass_grp))

    def right_first(turn):
        @pl.when(passing)
        def _():
            drain(right_all.at[turn, near, z], right_recv.at[turn, 0])
            along = right_all.at[turn, near, z, :, top]
            for i in (1, 3, 2):
                send(along, along, right_send, right_recv.at[turn, 1], along_z(i))
            along = right_all.at[turn, near, z, :, low]
            for to in (to_same, to_other, along_x(2)):
                send(along, along, right_send, right_recv.at[turn, 2], to)

    def x_column(turn, row, part=None):
        which = pl.ds(0, 4) if part is None else pl.ds(2 * part, 2)
        return right_all.at[turn, row, :, which, top]

    def z_column(turn, i, part=None):
        which = pl.ds(0, 2) if part is None else part
        return right_all.at[turn, which, z_at[i % 4], :, low]

    def right_second(turn):
        @pl.when(passing)
        def _():
            drain(right_all.at[turn, near, 0:3, :, top], right_recv.at[turn, 1])
            for to in (to_same, to_other):
                send(x_column(turn, near), x_column(turn, near), right_send, right_recv.at[turn, 3], to)
            drain(right_all.at[turn, 0, z, :, low], right_recv.at[turn, 2])

        @pl.when(jnp.logical_not(passing))
        def _():
            drain(right_all.at[turn, :, z, :, low], right_recv.at[turn, 2])

        for k, sign in steps:
            send(z_column(turn, 0), z_column(turn, 0), right_send, right_recv.at[turn, 6 + k], along_z(sign))

    def right_third(turn):
        drain(x_column(turn, 0), right_recv.at[turn, 3])

        @pl.when(passing)
        def _():
            piece = x_column(turn, 1 - near, 0)
            send(piece, piece, right_send, right_recv.at[turn, 4], to_other)

        @pl.when(jnp.logical_not(passing))
        def _():
            piece = x_column(turn, 1 - near, 1)
            send(piece, piece, right_send, right_recv.at[turn, 5], to_same)

        for k, sign in steps:
            drain(z_column(turn, 0), right_recv.at[turn, 6 + k])
            piece = z_column(turn, -sign, k)
            send(piece, piece, right_send, right_recv.at[turn, 8 + k], along_z(sign))

    def right_end(turn):
        @pl.when(jnp.logical_not(passing))
        def _():
            for k in range(2):
                drain(x_column(turn, 0, 0), right_recv.at[turn, 4 + k])
        for k in range(2):
            drain(z_column(turn, 0, 0), right_recv.at[turn, 8 + k])

    def right_sent(turn):
        for y_to in range(2):
            @pl.when(jnp.logical_not((y == y_to) & (grp == pass_grp)))
            def _():
                drain(right_own.at[turn], right_send)

        @pl.when(passing)
        def _():
            for _ in range(2):
                drain(right_all.at[turn, 0, 0:3, :, top], right_send)
                drain(x_column(turn, 0), right_send)

        drain(x_column(turn, 0, 0), right_send)
        for k in range(2):
            drain(z_column(turn, 0), right_send)
            drain(z_column(turn, 0, 0), right_send)

    lane_low = lane_iota((256, 128)) < 64

    def outer(turn):
        left_h, left_l = split(left_all[...].reshape(8, 2, 32, 128))
        left_wide = [
            jnp.concatenate([a[:, odd].reshape(256, 128) for a in (left_h, left_l, left_h)], axis=-1)
            for odd in range(2)
        ]
        right_flat = right_all.reshape(4 * 32 * 32, 128)

        def step(quad, carry):
            wide = []
            for e in range(4):
                high, low = split(jnp.concatenate(
                    [right_flat[pl.ds(1024 * (2 * turn + r2) + 4 * quad + e, 32, stride=32), :] for r2 in range(2)],
                    axis=0))
                wide.append(jnp.concatenate([high, high, low], axis=-1))
            even = dot(left_wide[0], jnp.concatenate(wide, axis=0), NT)
            odd = dot(left_wide[1], jnp.concatenate([wide[1], wide[0], wide[3], wide[2]], axis=0), NT)
            for m in range(2):
                lanes = slice(128 * m, 128 * m + 128)
                a, b = even[:, lanes], odd[:, lanes]
                for side, mixed in enumerate((jnp.where(lane_low, a, b), jnp.where(lane_low, b, a))):
                    high, low = split(mixed)
                    at = pl.ds(pl.multiple_of(512 * side + 64 * quad + 32 * m, 32), 32)
                    for i in range(8):
                        cols = slice(128 * (i % 2), 128 * (i % 2) + 128)
                        outer_h[i // 2, at, cols] = high[32 * i:32 * i + 32]
                        outer_l[i // 2, at, cols] = low[32 * i:32 * i + 32]
            return carry

        lax.fori_loop(0, 8, step, 0, unroll=4)

    def finish(turn):
        def step(i4, carry):
            total = []
            for side in range(2):
                at = slice(512 * side, 512 * side + 512)
                total.append(dot3((couple_h[:, at], couple_l[:, at]), (outer_h[i4, at, :], outer_l[i4, at, :])))
            for i2 in range(2):
                lanes = slice(128 * i2, 128 * i2 + 128)
                block = jnp.transpose(total[0][:, lanes] + pltpu.roll(total[1][:, lanes], 64, axis=1))
                for i1 in range(2):
                    for r2 in range(2):
                        at = 64 * i1 + 32 * r2
                        out_ref[4 * i4 + 2 * i2 + i1, pl.ds(2 * turn + r2, 32, stride=4), :] = block[at:at + 32]
            if turn == 1:
                four = pl.ds(4 * i4, 4)
                pltpu.make_async_copy(out_ref.at[four], out_hbm.at[four], out_copy.at[i4]).start()
            return carry

        lax.fori_loop(0, 4, step, 0, unroll=4)

    attend_column(0)
    finish_column(0)
    right_begin(0)
    attend_column(1)
    finish_column(1)
    right_begin(1)
    attend_column(2)
    right_first(0)
    finish_column(2)
    right_begin(2)
    attend_column(3)
    right_first(1)
    finish_column(3)
    right_begin(3)
    right_second(0)
    right_first(2)
    right_second(1)
    right_first(3)
    left_to = left_all.at[pl.ds(pl.multiple_of(grp * 128, 128), 128)]
    pltpu.make_async_copy(left_own, left_to, left_recv).start()
    for k in range(1, 4):
        send(left_own, left_to, left_send, left_recv, (dap, lax.rem(grp + k, 4)))
    right_second(2)
    right_third(0)
    right_second(3)
    right_third(1)
    for s2 in range(2):
        for part in range(2):
            tiles = units[part, pl.ds(256 * s2, 256), :].reshape(32, 8, 128)
            for s1 in range(2):
                revised_ref[:, s2, s1, :, 128 * part:128 * part + 128] = tiles[:, 4 * s1:4 * s1 + 4]
    pltpu.make_async_copy(revised_ref, revised_hbm, out_copy.at[4]).start()
    right_third(2)
    right_end(0)
    right_end(1)
    drain(left_all, left_recv)
    right_third(3)
    outer(0)
    finish(0)
    right_end(2)
    right_end(3)
    outer(1)
    finish(1)

    for i in range(4):
        four = pl.ds(4 * i, 4)
        pltpu.make_async_copy(out_ref.at[four], out_hbm.at[four], out_copy.at[i]).wait()
    pltpu.make_async_copy(revised_ref, revised_hbm, out_copy.at[4]).wait()
    for _ in range(31):
        drain(bias_ref, bias_send)
    drain(xs.at[0:31], x_send)
    drain(og.at[0:3], o_send)
    drain(finals.at[0:192], final_send)
    drain(left_all.at[0:384], left_send)
    for turn in range(4):
        right_sent(turn)


def emit_kernel(revised_in, pair_in, revised_out, pair_out, revised, pair, sems):
    copies = [(revised_in, revised, revised_out)]
    for i in range(4):
        four = pl.ds(4 * i, 4)
        copies.append((pair_in.at[four], pair.at[four], pair_out.at[four]))
    for i, (src, here, dst) in enumerate(copies):
        pltpu.make_async_copy(src, here, sems.at[0, i]).start()
    for i, (src, here, dst) in enumerate(copies):
        pltpu.make_async_copy(src, here, sems.at[0, i]).wait()
        pltpu.make_async_copy(here, dst, sems.at[1, i]).start()
    for i, (src, here, dst) in enumerate(copies):
        pltpu.make_async_copy(here, dst, sems.at[1, i]).wait()


VM = pl.BlockSpec(memory_space=pltpu.VMEM)
SM = pl.BlockSpec(memory_space=pltpu.SMEM)
ANY = pl.BlockSpec(memory_space=pl.ANY)
LIMIT = 58 * 1024 * 1024


def body(
    homolog_stack,
    couple_score_offset,
    strand_identity,
    strand_score_offset,
    homolog_presence,
    horizontal_matrix,
    horizontal_final_matrix,
    vertical_matrix,
    vertical_final_matrix,
    expand_matrix,
    shrink_matrix,
    tensor_matrix,
    couple_matrix,
):
    dma = pltpu.SemaphoreType.DMA
    regular = pltpu.SemaphoreType.REGULAR
    revised, pair = pl.pallas_call(
        kernel,
        out_shape=[
            jax.ShapeDtypeStruct((32, 2, 2, 4, 256), F32),
            jax.ShapeDtypeStruct((16, 128, 128), F32),
        ],
        in_specs=[ANY, VM, VM, SM] + [VM] * 4 + [ANY] * 5,
        out_specs=[ANY, ANY],
        scratch_shapes=[
            pltpu.VMEM((2, 4, 4, 2, 16, 512), F32),
            pltpu.VMEM((32, 2, 8, 256), F32),
            pltpu.VMEM((2, 32, 8, 256), F32),
            pltpu.VMEM((4, 2, 4, 4, 8, 128), F32),
            pltpu.VMEM((4, 2, 4, 4, 8, 128), F32),
            pltpu.VMEM((256, 256), F32),
            pltpu.VMEM((2, 512, 256), BF16),
            pltpu.VMEM((2, 512, 256), BF16),
            pltpu.VMEM((256, 768), BF16),
            pltpu.VMEM((256, 768), BF16),
            pltpu.VMEM((4, 2, 32, 16, 256), BF16),
            pltpu.VMEM((4, 512, 256), BF16),
            pltpu.VMEM((4, 1024, 256), BF16),
            pltpu.VMEM((4, 32, 16, 128), F32),
            pltpu.VMEM((32, 16, 128), F32),
            pltpu.VMEM((2, 128, 512), F32),
            pltpu.VMEM((2, 512, 128), F32),
            pltpu.VMEM((8, 512, 128), F32),
            pltpu.VMEM((2, 128, 128), F32),
            pltpu.VMEM((2, 512, 128), F32),
            pltpu.VMEM((128, 128), F32),
            pltpu.VMEM((4, 32, 128), F32),
            pltpu.VMEM((512, 128), F32),
            pltpu.VMEM((4, 2, 4, 4, 32, 128), F32),
            pltpu.VMEM((4, 1024, 256), BF16),
            pltpu.VMEM((4, 1024, 256), BF16),
            pltpu.VMEM((128, 1024), BF16),
            pltpu.VMEM((128, 1024), BF16),
            pltpu.VMEM((4, 256, 256), BF16),
            pltpu.VMEM((4, 256, 256), BF16),
            pltpu.VMEM((256, 256), BF16),
            pltpu.VMEM((256, 256), BF16),
            pltpu.VMEM((256, 1024), BF16),
            pltpu.VMEM((256, 1024), BF16),
            pltpu.VMEM((1024, 256), BF16),
            pltpu.VMEM((1024, 256), BF16),
            dma, dma((22,)), dma, dma, dma, dma((4,)), dma, dma,
            dma, dma, dma, dma((4, 10)), regular, regular, regular,
            pltpu.VMEM((4, 256, 256), F32),
            pltpu.VMEM((256, 256), F32),
            pltpu.VMEM((256, 1024), F32),
            pltpu.VMEM((1024, 256), F32),
            pltpu.VMEM((1024, 128), F32),
            dma((5,)),
            pltpu.VMEM((4, 32, 2, 8, 256), F32),
            dma((4,)),
            pltpu.VMEM((32, 2, 2, 4, 256), F32),
            pltpu.VMEM((16, 128, 128), F32),
            dma((5,)),
        ],
        compiler_params=pltpu.CompilerParams(
            collective_id=0, has_side_effects=True, vmem_limit_bytes=LIMIT
        ),
        name="msa_block",
    )(
        homolog_stack.reshape(4, 32, 2, 8, 256),
        couple_score_offset,
        strand_identity.reshape(1, 512),
        strand_score_offset,
        jnp.swapaxes(horizontal_matrix, 1, 2),
        horizontal_final_matrix,
        homolog_presence.reshape(1, 128),
        jnp.swapaxes(tensor_matrix, 1, 2),
        vertical_matrix,
        vertical_final_matrix,
        expand_matrix,
        shrink_matrix,
        couple_matrix,
    )
    revised, pair = pl.pallas_call(
        emit_kernel,
        out_shape=[
            jax.ShapeDtypeStruct((32, 2, 2, 4, 256), F32),
            jax.ShapeDtypeStruct((16, 128, 128), F32),
        ],
        in_specs=[ANY, ANY],
        out_specs=[ANY, ANY],
        scratch_shapes=[
            pltpu.VMEM((32, 2, 2, 4, 256), F32), pltpu.VMEM((16, 128, 128), F32), dma((2, 5)),
        ],
        name="emit",
    )(revised, pair)
    return revised.reshape(128, 4, 256), pair


def solution(mesh):
    return jax.shard_map(
        body,
        mesh=mesh,
        in_specs=(
            P("dap", None, None),
            P("grp", "dap", None),
            P(),
            P("grp"),
            P(),
            P(None, None, "grp"),
            P("grp", None),
            P(),
            P(),
            P(),
            P(),
            P(),
            P(),
        ),
        out_specs=(P(None, ("dap", "grp"), None), P("dap", "grp", None)),
        check_vma=False,
    )
```
